32 devices in a mesh: dp: 8 (over y, x, core), shard: 4 (over z).
Axes of the slice: x: 2, y: 2, z: 4, core: 2. Of those that a mesh axis runs over, the one named last changes fastest.
Arguments:
- partials: bfloat16 [8, 32, 256, 256], P('dp', 'shard'), may hold values from -4 to 4
- params: float32 [32, 256, 256], P('shard', 'dp'), may hold values from -0.75 to 0.75
- left_basis: float32 [8, 4, 1, 256, 256], P('dp', 'shard'), may hold values from -0.375 to 0.375
- right_basis: float32 [8, 4, 1, 256, 256], P('dp', 'shard'), may hold values from -0.375 to 0.375
- first_moment: float32 [8, 4, 1, 256, 256], P('dp', 'shard'), may hold values from -4 to 4
- second_moment: float32 [8, 4, 1, 256, 256], P('dp', 'shard'), may hold values from 0.1 to 10
- owner_list: int32 [32], replicated, may hold values from 0 to 31, as said below
Outputs:
- updated: float32 [32, 256, 256], P('shard')
- first_out: float32 [8, 4, 1, 256, 256], P('dp', 'shard')
- second_out: float32 [8, 4, 1, 256, 256], P('dp', 'shard')
The draws below stay inside these ranges and needn't reach their ends.
Inputs may be any that keep to these rules, and one draw needn't show every extreme that they name: `owner_list`: each owner device is named by at most 1 block, and some device by exactly 1.
All inputs are finite; a program needn't handle non-finite values.
Results may differ from the reference program's by a relative error of at most 0.0003.
Values sent between devices are 32-bit elements; how exact they have to be, the bound alone decides.
No kernel may reach another device: no remote copies, remote signals or barrier semaphores. Data moves between devices by JAX's collectives and lax.ppermute only.
A program may use at most 64 MiB of HBM per device.

```python
import math
import jax
import jax.numpy as jnp
from jax import lax

BLK = 256
CAP = 1
BLOCKS = 32
N_DP = 8
N_SHARD = 4


def draw_owner_list(key, part):
    order_key = jax.random.fold_in(key, 202)
    device_total = N_DP * N_SHARD
    return jax.random.permutation(order_key, device_total).astype(jnp.int32)[:BLOCKS]


def raised(values, stream_key, source, target, blocks, factor):
    def block_of(position):
        return (jnp.arange(values.shape[position]) // (values.shape[position] // blocks)).reshape((-1,) + (1,) * (values.ndim - 1 - position))

    first = jax.random.permutation(stream_key, blocks)[block_of(target)]
    far = (block_of(target) + blocks // 2) % blocks
    return jnp.where((block_of(source) == first) | (block_of(source) == far), factor * values, values)


def shard_levels(stream_key, dims, split, low, top_value):
    gain, own = 1.0, jax.random.fold_in(stream_key, 6)
    for dim, parts in split:
        steps = jnp.exp(jax.random.uniform(jax.random.fold_in(own, dim), (parts,), jnp.float32, low / len(split), top_value / len(split)))
        gain = gain * jnp.repeat(steps, dims[dim] // parts).reshape([-1 if axis == dim else 1 for axis in range(len(dims))])
    return gain


def normal_values(stream_key, shape, spread, reach, cuts=(), kind=jnp.bfloat16):
    array = spread * jax.random.normal(stream_key, shape, jnp.float32)
    if cuts:
        array = array * shard_levels(stream_key, shape, cuts, -0.22, 0.18)
    return jnp.clip(array, -reach, reach).astype(kind)


def noise_with(stream_key, shape, spread, bound, pieces, heavy, dtype=jnp.bfloat16):
    array = spread * jax.random.normal(stream_key, shape, jnp.float32)
    if pieces:
        array = array * shard_levels(stream_key, shape, pieces, -0.22, 0.18)
    return jnp.clip(raised(array, jax.random.fold_in(stream_key, 3), *heavy), -bound, bound).astype(dtype)


def setup_inputs(seed: int = 0) -> dict:
    key_list = jax.random.split(jax.random.key(seed), 8)
    partials = noise_with(key_list[0], (N_DP, BLOCKS, BLK, BLK), 0.2, 4.0, ((0, 8), (1, 4)), (0, 2, 8, 2.0))
    params = normal_values(key_list[1], (BLOCKS, BLK, BLK), 0.05, 0.75, ((0, 4), (1, 8)), jnp.float32)
    left_basis = normal_values(key_list[2], (N_DP, N_SHARD, CAP, BLK, BLK), BLK ** -0.5, 0.375, ((0, 8), (1, 4)), jnp.float32)
    right_basis = normal_values(key_list[3], (N_DP, N_SHARD, CAP, BLK, BLK), BLK ** -0.5, 0.375, ((0, 8), (1, 4)), jnp.float32)
    first_moment = normal_values(key_list[4], (N_DP, N_SHARD, CAP, BLK, BLK), 0.3, 4.0, ((0, 8), (1, 4)), jnp.float32)
    second_moment = jnp.clip(jnp.exp(math.log(10.0) - 4.6051702 * jax.random.uniform(key_list[5], (N_DP, N_SHARD, CAP, BLK, BLK), jnp.float32) ** shard_levels(key_list[5], (N_DP, N_SHARD, CAP, BLK, BLK), ((0, 8), (1, 4)), -0.2, 0.2)), 0.1, 10.0)
    owner_list = draw_owner_list(jax.random.fold_in(key_list[7], 71), 0)
    return {"partials": partials, "params": params, "left_basis": left_basis, "right_basis": right_basis, "first_moment": first_moment, "second_moment": second_moment, "owner_list": owner_list}


beta_one = 0.9
beta_two = 0.95
epsilon = 1e-08
learn_rate = 0.2
decay_rate = 0.1
step_count = 10

def reference(partials, params, left_basis, right_basis, first_moment, second_moment, owner_list):
    highest = lax.Precision.HIGHEST
    gradient = lax.optimization_barrier(jnp.sum(partials.astype(jnp.float32), axis=0))
    first_out = first_moment
    second_out = second_moment
    correct_one = 1.0 - beta_one ** step_count
    correct_two = 1.0 - beta_two ** step_count
    updated_list = []
    for block_index in range(BLOCKS):
        owner_idx = owner_list[block_index]
        owner_row = (owner_idx // N_SHARD).astype(jnp.int32)
        owner_col = (owner_idx % N_SHARD).astype(jnp.int32)
        left_mat = left_basis[owner_row, owner_col, 0]
        right_mat = right_basis[owner_row, owner_col, 0]
        first_old = first_moment[owner_row, owner_col, 0]
        second_old = second_moment[owner_row, owner_col, 0]
        partway = jnp.dot(left_mat.T, gradient[block_index], precision=highest, preferred_element_type=jnp.float32)
        rotated = jnp.dot(partway, right_mat, precision=highest, preferred_element_type=jnp.float32)
        first_new = beta_one * first_old + (1.0 - beta_one) * rotated
        second_new = beta_two * second_old + (1.0 - beta_two) * rotated * rotated
        scaled = first_new / correct_one / (jnp.sqrt(second_new / correct_two) + epsilon)
        back_rot = jnp.dot(scaled, right_mat.T, precision=highest, preferred_element_type=jnp.float32)
        change = jnp.dot(left_mat, back_rot, precision=highest, preferred_element_type=jnp.float32)
        updated_list.append(params[block_index] - learn_rate * (change + decay_rate * params[block_index]))
        first_out = first_out.at[owner_row, owner_col, 0].set(first_new)
        second_out = second_out.at[owner_row, owner_col, 0].set(second_new)
    return (jnp.stack(updated_list), first_out, second_out)
```

```python
import jax
import jax.numpy as jnp
from jax import lax
from jax.sharding import PartitionSpec as P

beta_one = 0.9
beta_two = 0.95
epsilon = 1e-08
learn_rate = 0.2
decay_rate = 0.1
step_count = 10


def swap(values, axis_size, bit):
    return lax.ppermute(values, "dp", [(i, i ^ (1 << bit)) for i in range(axis_size)])


def take(values, axis, index):
    return lax.dynamic_index_in_dim(values, index, axis, keepdims=False)


def halve(values, axes, bits, me, count):
    for bit in bits:
        axis = 1 + axes.index(bit)
        mine = (me >> bit) & 1
        away = take(values, axis, 1 - mine).astype(jnp.float32)
        here = take(values, axis, mine).astype(jnp.float32)
        values = here + swap(away, count, bit)
        axes = [a for a in axes if a != bit]
    return values


def spread(values, bits, me, count):
    axes = []
    for bit in bits:
        mine = (me >> bit) & 1
        other = swap(values, count, bit)
        low = jnp.where(mine == 0, values, other)
        high = jnp.where(mine == 0, other, values)
        place = sum(1 for a in axes if a > bit)
        values = jnp.stack([low, high], axis=1 + place)
        axes = sorted(axes + [bit], reverse=True)
    return values


def local(partials, params, left_basis, right_basis, first_moment, second_moment, owner_list):
    highest = lax.Precision.HIGHEST
    shard_here = lax.axis_index("shard")
    data_here = lax.axis_index("dp")
    shard_count = lax.axis_size("shard")
    data_count = lax.axis_size("dp")
    device_total = shard_count * data_count
    home_count, row_count, width = params.shape
    block_total = owner_list.shape[0]
    bit_count = data_count.bit_length() - 1
    high_low = list(range(bit_count))[::-1]
    middle = home_count // 2

    grid = partials[0].reshape((home_count,) + (2,) * bit_count + (row_count, width))
    low_first = halve(grid[:middle], high_low, list(range(bit_count)), data_here, data_count)
    high_first = halve(
        grid[middle:], high_low, [0] + list(range(1, bit_count))[::-1], data_here, data_count
    )
    summed = jnp.concatenate([low_first, high_first], axis=0)

    piece = row_count * width // shard_count
    cut = summed.reshape(home_count, shard_count, piece).swapaxes(0, 1)
    pieces = lax.all_to_all(cut, "shard", split_axis=0, concat_axis=0, tiled=True).reshape(
        block_total, piece
    )
    device_ids = jnp.arange(device_total, dtype=jnp.int32)
    picker = (owner_list[None, :] == device_ids[:, None]).astype(jnp.float32)
    leaving = jnp.einsum("eb,bn->en", picker, pieces, precision=highest)
    whole = lax.all_to_all(
        leaving, ("dp", "shard"), split_axis=0, concat_axis=0, tiled=True
    ).reshape(width, width)

    left_mat = left_basis[0, 0, 0]
    right_mat = right_basis[0, 0, 0]
    first_old = first_moment[0, 0, 0]
    second_old = second_moment[0, 0, 0]
    partway = jnp.einsum("ia,ij->aj", left_mat, whole, precision=highest)
    rotated = jnp.einsum("aj,jb->ab", partway, right_mat, precision=highest)
    first_new = beta_one * first_old + (1.0 - beta_one) * rotated
    second_new = beta_two * second_old + (1.0 - beta_two) * rotated * rotated
    correct_one = 1.0 - beta_one**step_count
    correct_two = 1.0 - beta_two**step_count
    scaled = first_new / correct_one / (jnp.sqrt(second_new / correct_two) + epsilon)
    back_rot = jnp.einsum("ab,jb->aj", scaled, right_mat, precision=highest)
    change = jnp.einsum("ia,aj->ij", left_mat, back_rot, precision=highest)

    coming = lax.all_to_all(
        change.reshape(device_total, piece), ("dp", "shard"), split_axis=0, concat_axis=0, tiled=True
    )
    back = jnp.einsum("eb,en->bn", picker, coming, precision=highest)
    returned = lax.all_to_all(
        back.reshape(shard_count, home_count, piece), "shard", split_axis=0, concat_axis=0, tiled=True
    )
    returned = returned.swapaxes(0, 1).reshape(home_count, row_count, width)
    new_home = params - learn_rate * (returned + decay_rate * params)
    updated = jnp.concatenate(
        [
            spread(new_home[:middle], high_low, data_here, data_count),
            spread(new_home[middle:], list(range(1, bit_count)) + [0], data_here, data_count),
        ],
        axis=0,
    ).reshape(home_count, width, width)

    my_id = data_here * shard_count + shard_here
    live = jnp.any(owner_list == my_id)
    first_keep = jnp.where(live, first_new, first_old)
    second_keep = jnp.where(live, second_new, second_old)
    return (updated, first_keep[None, None, None], second_keep[None, None, None])


def solution(mesh):
    return jax.shard_map(
        local,
        mesh=mesh,
        in_specs=(
            P("dp", "shard", None, None),
            P("shard", "dp", None),
            P("dp", "shard", None, None, None),
            P("dp", "shard", None, None, None),
            P("dp", "shard", None, None, None),
            P("dp", "shard", None, None, None),
            P(),
        ),
        out_specs=(
            P("shard", None, None),
            P("dp", "shard", None, None, None),
            P("dp", "shard", None, None, None),
        ),
        check_vma=False,
    )
```

```python
import jax
import jax.numpy as jnp
from jax import lax
from jax.sharding import PartitionSpec as P

beta_one = 0.9
beta_two = 0.95
epsilon = 1e-08
learn_rate = 0.2
decay_rate = 0.1
step_count = 10


def swap(values, name, mask, what="swap"):
    with jax.named_scope(what):
        return lax.ppermute(values, name, [(i, i ^ mask) for i in range(lax.axis_size(name))])


def take(values, axis, index):
    return lax.dynamic_index_in_dim(values, index, axis, keepdims=False)


def halve(values, axes, bits, me):
    for bit in bits:
        axis = 1 + axes.index(bit)
        mine = (me >> bit) & 1
        away = take(values, axis, 1 - mine).astype(jnp.float32)
        here = take(values, axis, mine).astype(jnp.float32)
        values = here + swap(away, "dp", 1 << bit)
        axes = [a for a in axes if a != bit]
    return values


def spread(values, bits, me):
    axes = []
    for bit in bits:
        mine = (me >> bit) & 1
        other = swap(values, "dp", 1 << bit)
        low = jnp.where(mine == 0, values, other)
        high = jnp.where(mine == 0, other, values)
        place = sum(1 for a in axes if a > bit)
        values = jnp.stack([low, high], axis=1 + place)
        axes = sorted(axes + [bit], reverse=True)
    return values


def unmix(values, index, axis=0):
    count = values.shape[axis]
    lead, tail = values.shape[:axis], values.shape[axis + 1 :]
    bits = count.bit_length() - 1
    values = values.reshape(lead + (2,) * bits + tail)
    for place in range(bits):
        bit = bits - 1 - place
        flipped = jnp.flip(values, axis + place)
        values = jnp.where((index >> bit) & 1 == 1, flipped, values)
    return values.reshape(lead + (count,) + tail)


def adam(left_mat, right_mat, first_old, second_old, whole, precision):
    partway = jnp.einsum("ia,ij->aj", left_mat, whole, precision=precision)
    rotated = jnp.einsum("aj,jb->ab", partway, right_mat, precision=precision)
    first_new = beta_one * first_old + (1.0 - beta_one) * rotated
    second_new = beta_two * second_old + (1.0 - beta_two) * rotated * rotated
    correct_one = 1.0 - beta_one**step_count
    correct_two = 1.0 - beta_two**step_count
    scaled = first_new / correct_one / (jnp.sqrt(second_new / correct_two) + epsilon)
    back_rot = jnp.einsum("ab,jb->aj", scaled, right_mat, precision=precision)
    change = jnp.einsum("ia,aj->ij", left_mat, back_rot, precision=precision)
    return first_new, second_new, change


def shard_exchange(parts):
    arrived = {k: swap(parts[k], "shard", k, f"shard_{k}") for k in (2, 3, 1)}
    return [parts[0]] + [arrived[k] for k in (1, 2, 3)]


def routed(partials, params, left_basis, right_basis, first_moment, second_moment, owner_list):
    high = lax.Precision.HIGH
    core, along_x, along_y, across = 1, 2, 4, 6
    shard_here = lax.axis_index("shard")
    data_here = lax.axis_index("dp")
    shard_count = lax.axis_size("shard")
    data_count = lax.axis_size("dp")
    device_total = shard_count * data_count
    home_count, row_count, width = params.shape
    half = home_count // 2
    piece = (row_count // shard_count, width)

    owners = unmix(owner_list.reshape(shard_count, home_count), shard_here).reshape(1, -1)
    device_ids = jnp.arange(device_total, dtype=jnp.int32)
    picker = (owners == device_ids[:, None]).astype(jnp.float32)

    chips = data_count // 2
    grid = partials[0].reshape((home_count, chips, 2, row_count, width))
    away_rows = take(grid, 2, 1 - (data_here & core))
    own_rows = take(grid, 2, data_here & core)
    away_rows, own_rows = lax.optimization_barrier((away_rows, own_rows))

    def rows_of(values, mask):
        return take(values, 1, (data_here ^ mask) // 2).astype(jnp.float32)

    part = {}
    for mask in (across, along_x, along_y, 0):
        total = rows_of(own_rows, mask) + swap(
            rows_of(away_rows, mask), "dp", core, f"sum_core_{mask}"
        )
        part[mask] = lax.optimization_barrier((total[:half], total[half:]))
        if mask == across:
            own_rows, part[mask] = lax.optimization_barrier((own_rows, part[mask]))
    near_y = part[along_y][0] + swap(part[across][0], "dp", along_x, "sum_far_low")
    near_x = part[along_x][1] + swap(part[across][1], "dp", along_y, "sum_far_top")
    low = part[0][0] + swap(part[along_x][0], "dp", along_x, "sum_x_low")
    top = part[0][1] + swap(part[along_y][1], "dp", along_y, "sum_y_top")
    low, top = lax.optimization_barrier((low, top))
    low = low + swap(near_y, "dp", along_y, "sum_relay_low")
    top = top + swap(near_x, "dp", along_x, "sum_relay_top")

    summed = jnp.concatenate([low, top], axis=0)
    summed = summed.reshape((home_count, shard_count) + piece)
    mixed = shard_exchange([take(summed, 1, shard_here ^ k) for k in range(shard_count)])
    pieces = jnp.concatenate(mixed, axis=0).reshape(device_total, -1)
    leaving = jnp.einsum("eb,bn->en", picker, pieces, precision=high)
    whole = lax.all_to_all(
        leaving.reshape((device_total,) + piece),
        ("dp", "shard"),
        split_axis=0,
        concat_axis=0,
        tiled=True,
    ).reshape(width, width)

    first_new, second_new, change = adam(
        left_basis[0, 0, 0],
        right_basis[0, 0, 0],
        first_moment[0, 0, 0],
        second_moment[0, 0, 0],
        whole,
        high,
    )

    coming = lax.all_to_all(
        change.reshape((device_total,) + piece),
        ("dp", "shard"),
        split_axis=0,
        concat_axis=0,
        tiled=True,
    ).reshape(device_total, -1)
    back = jnp.einsum("eb,en->bn", picker, coming, precision=high)
    back = back.reshape((shard_count, home_count) + piece)
    new_home = params
    returned = shard_exchange([back[k] for k in range(shard_count)])
    for k in (0, 3, 2, 1):
        start = (shard_here ^ k) * piece[0]
        home = lax.dynamic_slice_in_dim(params, start, piece[0], axis=1)
        home = home - learn_rate * (returned[k] + decay_rate * home)
        new_home = lax.dynamic_update_slice_in_dim(new_home, home, start, axis=1)

    low, top = new_home[:half], new_home[half:]
    x_top = swap(top, "dp", along_x, "rows_x_top")
    y_low = swap(low, "dp", along_y, "rows_y_low")
    other = swap(new_home, "dp", core, "rows_core_own")
    x_low = swap(low, "dp", along_x, "rows_x_low")
    y_top = swap(top, "dp", along_y, "rows_y_top")
    far_top = swap(x_top, "dp", along_y, "rows_relay_top")
    far_low = swap(y_low, "dp", along_x, "rows_relay_low")
    x_rows = jnp.concatenate([x_low, x_top], axis=0)
    y_rows = jnp.concatenate([y_top, y_low], axis=0)
    x_rows, y_rows, first_new, second_new = lax.optimization_barrier(
        (x_rows, y_rows, first_new, second_new)
    )
    far_rows = jnp.concatenate([far_low, far_top], axis=0)
    y_other = swap(y_rows, "dp", core, "rows_core_y")
    updated = jnp.zeros((home_count, width, width), jnp.float32)
    for mask, block, values in (
        (0, 0, new_home),
        (core, 0, other),
        (along_x, 0, x_rows),
        (along_y, half, y_rows[:half]),
        (along_y, 0, y_rows[half:]),
        (along_x ^ core, 0, swap(x_rows, "dp", core, "rows_core_x")),
        (along_y ^ core, half, y_other[:half]),
        (along_y ^ core, 0, y_other[half:]),
        (across, 0, far_rows),
        (across ^ core, 0, swap(far_rows, "dp", core, "rows_core_far")),
    ):
        start = (data_here ^ mask) * row_count
        updated = lax.dynamic_update_slice(updated, values, (block, start, 0))
    return updated, first_new[None, None, None], second_new[None, None, None]


def gathered(partials, params, left_basis, right_basis, first_moment, second_moment, owner_list):
    highest = lax.Precision.HIGHEST
    shard_here = lax.axis_index("shard")
    data_here = lax.axis_index("dp")
    shard_count = lax.axis_size("shard")
    data_count = lax.axis_size("dp")
    device_total = shard_count * data_count
    home_count, row_count, width = params.shape
    block_total = owner_list.shape[0]
    bit_count = data_count.bit_length() - 1
    high_low = list(range(bit_count))[::-1]
    middle = home_count // 2

    grid = partials[0].reshape((home_count,) + (2,) * bit_count + (row_count, width))
    low_first = halve(grid[:middle], high_low, list(range(bit_count)), data_here)
    high_first = halve(
        grid[middle:], high_low, [0] + list(range(1, bit_count))[::-1], data_here
    )
    summed = jnp.concatenate([low_first, high_first], axis=0)

    piece = row_count * width // shard_count
    cut = summed.reshape(home_count, shard_count, piece).swapaxes(0, 1)
    pieces = lax.all_to_all(cut, "shard", split_axis=0, concat_axis=0, tiled=True).reshape(
        block_total, piece
    )
    device_ids = jnp.arange(device_total, dtype=jnp.int32)
    picker = (owner_list[None, :] == device_ids[:, None]).astype(jnp.float32)
    leaving = jnp.einsum("eb,bn->en", picker, pieces, precision=highest)
    whole = lax.all_to_all(
        leaving, ("dp", "shard"), split_axis=0, concat_axis=0, tiled=True
    ).reshape(width, width)

    left_mat = left_basis[0, 0, 0]
    right_mat = right_basis[0, 0, 0]
    first_old = first_moment[0, 0, 0]
    second_old = second_moment[0, 0, 0]
    first_new, second_new, change = adam(
        left_mat, right_mat, first_old, second_old, whole, highest
    )

    coming = lax.all_to_all(
        change.reshape(device_total, piece), ("dp", "shard"), split_axis=0, concat_axis=0, tiled=True
    )
    back = jnp.einsum("eb,en->bn", picker, coming, precision=highest)
    returned = lax.all_to_all(
        back.reshape(shard_count, home_count, piece), "shard", split_axis=0, concat_axis=0, tiled=True
    )
    returned = returned.swapaxes(0, 1).reshape(home_count, row_count, width)
    new_home = params - learn_rate * (returned + decay_rate * params)
    updated = jnp.concatenate(
        [
            spread(new_home[:middle], high_low, data_here),
            spread(new_home[middle:], list(range(1, bit_count)) + [0], data_here),
        ],
        axis=0,
    ).reshape(home_count, width, width)

    my_id = data_here * shard_count + shard_here
    live = jnp.any(owner_list == my_id)
    first_keep = jnp.where(live, first_new, first_old)
    second_keep = jnp.where(live, second_new, second_old)
    return (updated, first_keep[None, None, None], second_keep[None, None, None])


def local(partials, params, left_basis, right_basis, first_moment, second_moment, owner_list):
    shard_count, data_count = lax.axis_size("shard"), lax.axis_size("dp")
    plain = (data_count, shard_count) != (8, 4) or params.shape[1] % (8 * shard_count) != 0
    plain = plain or owner_list.shape[0] != shard_count * data_count or params.shape[0] % 2 != 0
    form = gathered if plain else routed
    return form(
        partials, params, left_basis, right_basis, first_moment, second_moment, owner_list
    )


def solution(mesh):
    return jax.shard_map(
        local,
        mesh=mesh,
        in_specs=(
            P("dp", "shard", None, None),
            P("shard", "dp", None),
            P("dp", "shard", None, None, None),
            P("dp", "shard", None, None, None),
            P("dp", "shard", None, None, None),
            P("dp", "shard", None, None, None),
            P(),
        ),
        out_specs=(
            P("shard", None, None),
            P("dp", "shard", None, None, None),
            P("dp", "shard", None, None, None),
        ),
        check_vma=False,
    )
```

```python
import jax
import jax.numpy as jnp
from jax import lax
from jax.sharding import PartitionSpec as P

beta_one = 0.9
beta_two = 0.95
epsilon = 1e-08
learn_rate = 0.2
decay_rate = 0.1
step_count = 10


def swap(values, name, mask, what="swap"):
    with jax.named_scope(what):
        return lax.ppermute(values, name, [(i, i ^ mask) for i in range(lax.axis_size(name))])


def take(values, axis, index):
    return lax.dynamic_index_in_dim(values, index, axis, keepdims=False)


def halve(values, axes, bits, me):
    for bit in bits:
        axis = 1 + axes.index(bit)
        mine = (me >> bit) & 1
        away = take(values, axis, 1 - mine).astype(jnp.float32)
        here = take(values, axis, mine).astype(jnp.float32)
        values = here + swap(away, "dp", 1 << bit)
        axes = [a for a in axes if a != bit]
    return values


def spread(values, bits, me):
    axes = []
    for bit in bits:
        mine = (me >> bit) & 1
        other = swap(values, "dp", 1 << bit)
        low = jnp.where(mine == 0, values, other)
        high = jnp.where(mine == 0, other, values)
        place = sum(1 for a in axes if a > bit)
        values = jnp.stack([low, high], axis=1 + place)
        axes = sorted(axes + [bit], reverse=True)
    return values


def unmix(values, index, axis=0):
    count = values.shape[axis]
    lead, tail = values.shape[:axis], values.shape[axis + 1 :]
    bits = count.bit_length() - 1
    values = values.reshape(lead + (2,) * bits + tail)
    for place in range(bits):
        bit = bits - 1 - place
        flipped = jnp.flip(values, axis + place)
        values = jnp.where((index >> bit) & 1 == 1, flipped, values)
    return values.reshape(lead + (count,) + tail)


def adam(left_mat, right_mat, first_old, second_old, whole, precision):
    partway = jnp.einsum("ia,ij->aj", left_mat, whole, precision=precision)
    rotated = jnp.einsum("aj,jb->ab", partway, right_mat, precision=precision)
    first_new = beta_one * first_old + (1.0 - beta_one) * rotated
    second_new = beta_two * second_old + (1.0 - beta_two) * rotated * rotated
    correct_one = 1.0 - beta_one**step_count
    correct_two = 1.0 - beta_two**step_count
    scaled = first_new / correct_one / (jnp.sqrt(second_new / correct_two) + epsilon)
    back_rot = jnp.einsum("ab,jb->aj", scaled, right_mat, precision=precision)
    change = jnp.einsum("ia,aj->ij", left_mat, back_rot, precision=precision)
    return first_new, second_new, change


def shard_exchange(parts):
    arrived = {k: swap(parts[k], "shard", k, f"shard_{k}") for k in (2, 3, 1)}
    return [parts[0]] + [arrived[k] for k in (1, 2, 3)]


def routed(partials, params, left_basis, right_basis, first_moment, second_moment, owner_list):
    high = lax.Precision.HIGH
    core, along_x, along_y, across = 1, 2, 4, 6
    shard_here = lax.axis_index("shard")
    data_here = lax.axis_index("dp")
    shard_count = lax.axis_size("shard")
    data_count = lax.axis_size("dp")
    device_total = shard_count * data_count
    home_count, row_count, width = params.shape
    half = home_count // 2
    piece = (row_count // shard_count, width)

    owners = unmix(owner_list.reshape(shard_count, home_count), shard_here).reshape(1, -1)
    device_ids = jnp.arange(device_total, dtype=jnp.int32)
    picker = (owners == device_ids[:, None]).astype(jnp.float32)

    chips = data_count // 2
    grid = partials[0].reshape((home_count, chips, 2, row_count, width))
    away_rows = take(grid, 2, 1 - (data_here & core))
    own_rows = take(grid, 2, data_here & core)
    away_rows, own_rows = lax.optimization_barrier((away_rows, own_rows))

    def rows_of(values, mask):
        return take(values, 1, (data_here ^ mask) // 2).astype(jnp.float32)

    part = {}
    for mask in (across, along_x, along_y, 0):
        total = rows_of(own_rows, mask) + swap(
            rows_of(away_rows, mask), "dp", core, f"sum_core_{mask}"
        )
        part[mask] = lax.optimization_barrier((total[:half], total[half:]))
        if mask == across:
            own_rows, part[mask] = lax.optimization_barrier((own_rows, part[mask]))
    near_y = part[along_y][0] + swap(part[across][0], "dp", along_x, "sum_far_low")
    near_x = part[along_x][1] + swap(part[across][1], "dp", along_y, "sum_far_top")
    low = part[0][0] + swap(part[along_x][0], "dp", along_x, "sum_x_low")
    top = part[0][1] + swap(part[along_y][1], "dp", along_y, "sum_y_top")
    low, top = lax.optimization_barrier((low, top))
    low = low + swap(near_y, "dp", along_y, "sum_relay_low")
    top = top + swap(near_x, "dp", along_x, "sum_relay_top")

    summed = jnp.concatenate([low, top], axis=0)
    summed = summed.reshape((home_count, shard_count) + piece)
    mixed = shard_exchange([take(summed, 1, shard_here ^ k) for k in range(shard_count)])
    pieces = jnp.concatenate(mixed, axis=0).reshape(device_total, -1)
    leaving = jnp.einsum("eb,bn->en", picker, pieces, precision=high)
    whole = lax.all_to_all(
        leaving.reshape((device_total,) + piece),
        ("dp", "shard"),
        split_axis=0,
        concat_axis=0,
        tiled=True,
    ).reshape(width, width)

    first_new, second_new, change = adam(
        left_basis[0, 0, 0],
        right_basis[0, 0, 0],
        first_moment[0, 0, 0],
        second_moment[0, 0, 0],
        whole,
        high,
    )

    coming = lax.all_to_all(
        change.reshape((device_total,) + piece),
        ("dp", "shard"),
        split_axis=0,
        concat_axis=0,
        tiled=True,
    ).reshape(device_total, -1)
    back = jnp.einsum("eb,en->bn", picker, coming, precision=high)
    back = back.reshape((shard_count, home_count) + piece)
    new_home = params
    returned = shard_exchange([back[k] for k in range(shard_count)])
    for k in (0, 3, 2, 1):
        start = (shard_here ^ k) * piece[0]
        home = lax.dynamic_slice_in_dim(params, start, piece[0], axis=1)
        home = home - learn_rate * (returned[k] + decay_rate * home)
        new_home = lax.dynamic_update_slice_in_dim(new_home, home, start, axis=1)

    low, top = new_home[:half], new_home[half:]
    x_top = swap(top, "dp", along_x, "rows_x_top")
    y_low = swap(low, "dp", along_y, "rows_y_low")
    other = swap(new_home, "dp", core, "rows_core_own")
    x_low = swap(low, "dp", along_x, "rows_x_low")
    y_top = swap(top, "dp", along_y, "rows_y_top")
    far_top = swap(x_top, "dp", along_y, "rows_relay_top")
    far_low = swap(y_low, "dp", along_x, "rows_relay_low")
    x_rows = jnp.concatenate([x_low, x_top], axis=0)
    y_rows = jnp.concatenate([y_top, y_low], axis=0)
    x_rows, y_rows, far_top, first_new, second_new = lax.optimization_barrier(
        (x_rows, y_rows, far_top, first_new, second_new)
    )
    far_rows = jnp.concatenate([far_low, far_top], axis=0)
    y_other = swap(y_rows, "dp", core, "rows_core_y")
    updated = jnp.zeros((home_count, width, width), jnp.float32)
    for mask, block, values in (
        (0, 0, new_home),
        (core, 0, other),
        (along_x, 0, x_rows),
        (along_y, half, y_rows[:half]),
        (along_y, 0, y_rows[half:]),
        (along_x ^ core, 0, swap(x_rows, "dp", core, "rows_core_x")),
        (along_y ^ core, half, y_other[:half]),
        (along_y ^ core, 0, y_other[half:]),
        (across, 0, far_rows),
        (across ^ core, 0, swap(far_rows, "dp", core, "rows_core_far")),
    ):
        start = (data_here ^ mask) * row_count
        updated = lax.dynamic_update_slice(updated, values, (block, start, 0))
    return updated, first_new[None, None, None], second_new[None, None, None]


def gathered(partials, params, left_basis, right_basis, first_moment, second_moment, owner_list):
    highest = lax.Precision.HIGHEST
    shard_here = lax.axis_index("shard")
    data_here = lax.axis_index("dp")
    shard_count = lax.axis_size("shard")
    data_count = lax.axis_size("dp")
    device_total = shard_count * data_count
    home_count, row_count, width = params.shape
    block_total = owner_list.shape[0]
    bit_count = data_count.bit_length() - 1
    high_low = list(range(bit_count))[::-1]
    middle = home_count // 2

    grid = partials[0].reshape((home_count,) + (2,) * bit_count + (row_count, width))
    low_first = halve(grid[:middle], high_low, list(range(bit_count)), data_here)
    high_first = halve(
        grid[middle:], high_low, [0] + list(range(1, bit_count))[::-1], data_here
    )
    summed = jnp.concatenate([low_first, high_first], axis=0)

    piece = row_count * width // shard_count
    cut = summed.reshape(home_count, shard_count, piece).swapaxes(0, 1)
    pieces = lax.all_to_all(cut, "shard", split_axis=0, concat_axis=0, tiled=True).reshape(
        block_total, piece
    )
    device_ids = jnp.arange(device_total, dtype=jnp.int32)
    picker = (owner_list[None, :] == device_ids[:, None]).astype(jnp.float32)
    leaving = jnp.einsum("eb,bn->en", picker, pieces, precision=highest)
    whole = lax.all_to_all(
        leaving, ("dp", "shard"), split_axis=0, concat_axis=0, tiled=True
    ).reshape(width, width)

    left_mat = left_basis[0, 0, 0]
    right_mat = right_basis[0, 0, 0]
    first_old = first_moment[0, 0, 0]
    second_old = second_moment[0, 0, 0]
    first_new, second_new, change = adam(
        left_mat, right_mat, first_old, second_old, whole, highest
    )

    coming = lax.all_to_all(
        change.reshape(device_total, piece), ("dp", "shard"), split_axis=0, concat_axis=0, tiled=True
    )
    back = jnp.einsum("eb,en->bn", picker, coming, precision=highest)
    returned = lax.all_to_all(
        back.reshape(shard_count, home_count, piece), "shard", split_axis=0, concat_axis=0, tiled=True
    )
    returned = returned.swapaxes(0, 1).reshape(home_count, row_count, width)
    new_home = params - learn_rate * (returned + decay_rate * params)
    updated = jnp.concatenate(
        [
            spread(new_home[:middle], high_low, data_here),
            spread(new_home[middle:], list(range(1, bit_count)) + [0], data_here),
        ],
        axis=0,
    ).reshape(home_count, width, width)

    my_id = data_here * shard_count + shard_here
    live = jnp.any(owner_list == my_id)
    first_keep = jnp.where(live, first_new, first_old)
    second_keep = jnp.where(live, second_new, second_old)
    return (updated, first_keep[None, None, None], second_keep[None, None, None])


def local(partials, params, left_basis, right_basis, first_moment, second_moment, owner_list):
    shard_count, data_count = lax.axis_size("shard"), lax.axis_size("dp")
    plain = (data_count, shard_count) != (8, 4) or params.shape[1] % (8 * shard_count) != 0
    plain = plain or owner_list.shape[0] != shard_count * data_count or params.shape[0] % 2 != 0
    form = gathered if plain else routed
    return form(
        partials, params, left_basis, right_basis, first_moment, second_moment, owner_list
    )


def solution(mesh):
    return jax.shard_map(
        local,
        mesh=mesh,
        in_specs=(
            P("dp", "shard", None, None),
            P("shard", "dp", None),
            P("dp", "shard", None, None, None),
            P("dp", "shard", None, None, None),
            P("dp", "shard", None, None, None),
            P("dp", "shard", None, None, None),
            P(),
        ),
        out_specs=(
            P("shard", None, None),
            P("dp", "shard", None, None, None),
            P("dp", "shard", None, None, None),
        ),
        check_vma=False,
    )
```

```python
import jax
import jax.numpy as jnp
import numpy as np
from jax import lax
from jax.sharding import PartitionSpec as P

beta_one = 0.9
beta_two = 0.95
epsilon = 1e-08
learn_rate = 0.2
decay_rate = 0.1
step_count = 10


def swap(values, name, mask, what="swap"):
    with jax.named_scope(what):
        return lax.ppermute(values, name, [(i, i ^ mask) for i in range(lax.axis_size(name))])


def take(values, axis, index):
    return lax.dynamic_index_in_dim(values, index, axis, keepdims=False)


def halve(values, axes, bits, me):
    for bit in bits:
        axis = 1 + axes.index(bit)
        mine = (me >> bit) & 1
        away = take(values, axis, 1 - mine).astype(jnp.float32)
        here = take(values, axis, mine).astype(jnp.float32)
        values = here + swap(away, "dp", 1 << bit)
        axes = [a for a in axes if a != bit]
    return values


def spread(values, bits, me):
    axes = []
    for bit in bits:
        mine = (me >> bit) & 1
        other = swap(values, "dp", 1 << bit)
        low = jnp.where(mine == 0, values, other)
        high = jnp.where(mine == 0, other, values)
        place = sum(1 for a in axes if a > bit)
        values = jnp.stack([low, high], axis=1 + place)
        axes = sorted(axes + [bit], reverse=True)
    return values


def unmix(values, index, axis=0):
    count = values.shape[axis]
    lead, tail = values.shape[:axis], values.shape[axis + 1 :]
    bits = count.bit_length() - 1
    values = values.reshape(lead + (2,) * bits + tail)
    for place in range(bits):
        bit = bits - 1 - place
        flipped = jnp.flip(values, axis + place)
        values = jnp.where((index >> bit) & 1 == 1, flipped, values)
    return values.reshape(lead + (count,) + tail)


def adam(left_mat, right_mat, first_old, second_old, whole, precision):
    partway = jnp.einsum("ia,ij->aj", left_mat, whole, precision=precision)
    rotated = jnp.einsum("aj,jb->ab", partway, right_mat, precision=precision)
    first_new = beta_one * first_old + (1.0 - beta_one) * rotated
    second_new = beta_two * second_old + (1.0 - beta_two) * rotated * rotated
    correct_one = 1.0 - beta_one**step_count
    correct_two = 1.0 - beta_two**step_count
    scaled = first_new / correct_one / (jnp.sqrt(second_new / correct_two) + epsilon)
    back_rot = jnp.einsum("ab,jb->aj", scaled, right_mat, precision=precision)
    change = jnp.einsum("ia,aj->ij", left_mat, back_rot, precision=precision)
    return first_new, second_new, change


def shard_exchange(parts):
    arrived = {k: swap(parts[k], "shard", k, f"shard_{k}") for k in (2, 3, 1)}
    return [parts[0]] + [arrived[k] for k in (1, 2, 3)]


def routed(partials, params, left_basis, right_basis, first_moment, second_moment, owner_list):
    high = lax.Precision.HIGH
    core, along_x, along_y, across = 1, 2, 4, 6
    shard_here = lax.axis_index("shard")
    data_here = lax.axis_index("dp")
    shard_count = lax.axis_size("shard")
    data_count = lax.axis_size("dp")
    device_total = shard_count * data_count
    home_count, row_count, width = params.shape
    half = home_count // 2
    piece = (row_count // shard_count, width)

    chips = data_count // 2
    my_core = data_here & core

    groups = np.arange(device_total).reshape(chips, 2, shard_count).swapaxes(0, 1).reshape(2, -1).tolist()
    left_mat = left_basis[0, 0, 0].reshape((chips, 2, shard_count) + piece)
    left_mat = unmix(left_mat.swapaxes(1, 2), my_core, axis=2).reshape(width, width)

    def core_groups(values):
        return lax.all_to_all(
            values, ("dp", "shard"), split_axis=0, concat_axis=0, axis_index_groups=groups, tiled=True
        )

    grid = partials[0].reshape((home_count, chips, 2, row_count, width))
    away_rows = take(grid, 2, 1 - my_core)
    own_rows = take(grid, 2, my_core)
    away_rows, own_rows = lax.optimization_barrier((away_rows, own_rows))

    def rows_of(values, mask):
        return take(values, 1, (data_here ^ mask) // 2).astype(jnp.float32)

    part = {}
    for mask in (across, along_x, along_y, 0):
        away = rows_of(away_rows, mask)
        total = rows_of(own_rows, mask) + swap(away, "dp", core, f"sum_core_{mask}")
        part[mask] = lax.optimization_barrier((total[:half], total[half:]))
        if mask == across:
            own_rows, part[mask] = lax.optimization_barrier((own_rows, part[mask]))
    near_y = part[along_y][0] + swap(part[across][0], "dp", along_x, "sum_far_low")
    near_x = part[along_x][1] + swap(part[across][1], "dp", along_y, "sum_far_top")
    low = part[0][0] + swap(part[along_x][0], "dp", along_x, "sum_x_low")
    top = part[0][1] + swap(part[along_y][1], "dp", along_y, "sum_y_top")
    low, top = lax.optimization_barrier((low, top))
    low = low + swap(near_y, "dp", along_y, "sum_relay_low")
    top = top + swap(near_x, "dp", along_x, "sum_relay_top")

    summed = jnp.concatenate([low, top], axis=0)
    summed = summed.reshape((home_count, shard_count) + piece)
    summed, owner_list = lax.optimization_barrier((summed, owner_list))
    mixed = shard_exchange([take(summed, 1, shard_here ^ k) for k in range(shard_count)])
    owners = unmix(owner_list.reshape(shard_count, home_count), shard_here).reshape(1, -1)
    lane, column = owners // shard_count, owners % shard_count
    spot = (((lane & core) ^ my_core) * chips + lane // 2) * shard_count + column
    picker = (spot == jnp.arange(device_total, dtype=jnp.int32)[:, None]).astype(jnp.float32)
    pieces = jnp.concatenate(mixed, axis=0).reshape(device_total, -1)
    leaving = jnp.einsum("eb,bn->en", picker, pieces, precision=high)
    leaving = leaving.reshape((2, device_total // 2) + piece)
    leaving = [leaving[0], swap(leaving[1], "dp", core, "pieces_core")]
    whole = core_groups(jnp.stack(leaving, axis=1)).reshape(width, width)

    first_new, second_new, change = adam(
        left_mat, right_basis[0, 0, 0], first_moment[0, 0, 0], second_moment[0, 0, 0], whole, high
    )

    coming = core_groups(change.reshape((device_total // 2, 2) + piece))
    coming = [coming[:, 0], swap(coming[:, 1], "dp", core, "change_core")]
    coming = jnp.concatenate(coming, axis=0).reshape(device_total, -1)
    back = jnp.einsum("eb,en->bn", picker, coming, precision=high)
    back = back.reshape((shard_count, home_count) + piece)
    new_home = params
    returned = shard_exchange([back[k] for k in range(shard_count)])
    for k in (0, 3, 2, 1):
        start = (shard_here ^ k) * piece[0]
        home = lax.dynamic_slice_in_dim(params, start, piece[0], axis=1)
        home = home - learn_rate * (returned[k] + decay_rate * home)
        new_home = lax.dynamic_update_slice_in_dim(new_home, home, start, axis=1)

    low, top = new_home[:half], new_home[half:]
    x_top = swap(top, "dp", along_x, "rows_x_top")
    y_low = swap(low, "dp", along_y, "rows_y_low")
    other = swap(new_home, "dp", core, "rows_core_own")
    updated = jnp.zeros((home_count, width, width), jnp.float32)
    updated = lax.dynamic_update_slice_in_dim(updated, new_home, data_here * row_count, axis=1)
    low, top, updated = lax.optimization_barrier((low, top, updated))
    x_low = swap(low, "dp", along_x, "rows_x_low")
    y_top = swap(top, "dp", along_y, "rows_y_top")
    far_top = swap(x_top, "dp", along_y, "rows_relay_top")
    far_low = swap(y_low, "dp", along_x, "rows_relay_low")
    x_rows = jnp.concatenate([x_low, x_top], axis=0)
    y_rows = jnp.concatenate([y_top, y_low], axis=0)
    x_rows, y_rows, far_top, first_new, second_new = lax.optimization_barrier(
        (x_rows, y_rows, far_top, first_new, second_new)
    )
    far_rows = jnp.concatenate([far_low, far_top], axis=0)
    y_other = swap(y_rows, "dp", core, "rows_core_y")
    for mask, block, values in (
        (core, 0, other),
        (along_x, 0, x_rows),
        (along_y, half, y_rows[:half]),
        (along_y, 0, y_rows[half:]),
        (along_x ^ core, 0, swap(x_rows, "dp", core, "rows_core_x")),
        (along_y ^ core, half, y_other[:half]),
        (along_y ^ core, 0, y_other[half:]),
    ):
        start = (data_here ^ mask) * row_count
        updated = lax.dynamic_update_slice(updated, values, (block, start, 0))
    far_other = swap(far_rows, "dp", core, "rows_core_far")
    updated = updated.reshape(home_count, data_count, row_count, width)
    place = lax.broadcasted_iota(jnp.int32, updated.shape, 1) ^ data_here
    far_both = jnp.where(place == across, far_rows[:, None], far_other[:, None])
    updated = jnp.where(place < across, updated, far_both)
    updated = updated.reshape(home_count, width, width)
    return updated, first_new[None, None, None], second_new[None, None, None]


def gathered(partials, params, left_basis, right_basis, first_moment, second_moment, owner_list):
    highest = lax.Precision.HIGHEST
    shard_here = lax.axis_index("shard")
    data_here = lax.axis_index("dp")
    shard_count = lax.axis_size("shard")
    data_count = lax.axis_size("dp")
    device_total = shard_count * data_count
    home_count, row_count, width = params.shape
    block_total = owner_list.shape[0]
    bit_count = data_count.bit_length() - 1
    high_low = list(range(bit_count))[::-1]
    middle = home_count // 2

    grid = partials[0].reshape((home_count,) + (2,) * bit_count + (row_count, width))
    low_first = halve(grid[:middle], high_low, list(range(bit_count)), data_here)
    high_first = halve(
        grid[middle:], high_low, [0] + list(range(1, bit_count))[::-1], data_here
    )
    summed = jnp.concatenate([low_first, high_first], axis=0)

    piece = row_count * width // shard_count
    cut = summed.reshape(home_count, shard_count, piece).swapaxes(0, 1)
    pieces = lax.all_to_all(cut, "shard", split_axis=0, concat_axis=0, tiled=True).reshape(
        block_total, piece
    )
    device_ids = jnp.arange(device_total, dtype=jnp.int32)
    picker = (owner_list[None, :] == device_ids[:, None]).astype(jnp.float32)
    leaving = jnp.einsum("eb,bn->en", picker, pieces, precision=highest)
    whole = lax.all_to_all(
        leaving, ("dp", "shard"), split_axis=0, concat_axis=0, tiled=True
    ).reshape(width, width)

    left_mat = left_basis[0, 0, 0]
    right_mat = right_basis[0, 0, 0]
    first_old = first_moment[0, 0, 0]
    second_old = second_moment[0, 0, 0]
    first_new, second_new, change = adam(
        left_mat, right_mat, first_old, second_old, whole, highest
    )

    coming = lax.all_to_all(
        change.reshape(device_total, piece), ("dp", "shard"), split_axis=0, concat_axis=0, tiled=True
    )
    back = jnp.einsum("eb,en->bn", picker, coming, precision=highest)
    returned = lax.all_to_all(
        back.reshape(shard_count, home_count, piece), "shard", split_axis=0, concat_axis=0, tiled=True
    )
    returned = returned.swapaxes(0, 1).reshape(home_count, row_count, width)
    new_home = params - learn_rate * (returned + decay_rate * params)
    updated = jnp.concatenate(
        [
            spread(new_home[:middle], high_low, data_here),
            spread(new_home[middle:], list(range(1, bit_count)) + [0], data_here),
        ],
        axis=0,
    ).reshape(home_count, width, width)

    my_id = data_here * shard_count + shard_here
    live = jnp.any(owner_list == my_id)
    first_keep = jnp.where(live, first_new, first_old)
    second_keep = jnp.where(live, second_new, second_old)
    return (updated, first_keep[None, None, None], second_keep[None, None, None])


def local(partials, params, left_basis, right_basis, first_moment, second_moment, owner_list):
    shard_count, data_count = lax.axis_size("shard"), lax.axis_size("dp")
    plain = (data_count, shard_count) != (8, 4) or params.shape[1] % (8 * shard_count) != 0
    plain = plain or owner_list.shape[0] != shard_count * data_count or params.shape[0] % 2 != 0
    form = gathered if plain else routed
    return form(
        partials, params, left_basis, right_basis, first_moment, second_moment, owner_list
    )


def solution(mesh):
    return jax.shard_map(
        local,
        mesh=mesh,
        in_specs=(
            P("dp", "shard", None, None),
            P("shard", "dp", None),
            P("dp", "shard", None, None, None),
            P("dp", "shard", None, None, None),
            P("dp", "shard", None, None, None),
            P("dp", "shard", None, None, None),
            P(),
        ),
        out_specs=(
            P("shard", None, None),
            P("dp", "shard", None, None, None),
            P("dp", "shard", None, None, None),
        ),
        check_vma=False,
    )
```

```python
import jax
import jax.numpy as jnp
from jax import lax
from jax.sharding import PartitionSpec as P

beta_one = 0.9
beta_two = 0.95
epsilon = 1e-08
learn_rate = 0.2
decay_rate = 0.1
step_count = 10


def swap(values, name, mask, what="swap"):
    with jax.named_scope(what):
        return lax.ppermute(values, name, [(i, i ^ mask) for i in range(lax.axis_size(name))])


def take(values, axis, index):
    return lax.dynamic_index_in_dim(values, index, axis, keepdims=False)


def halve(values, axes, bits, me):
    for bit in bits:
        axis = 1 + axes.index(bit)
        mine = (me >> bit) & 1
        away = take(values, axis, 1 - mine).astype(jnp.float32)
        here = take(values, axis, mine).astype(jnp.float32)
        values = here + swap(away, "dp", 1 << bit)
        axes = [a for a in axes if a != bit]
    return values


def spread(values, bits, me):
    axes = []
    for bit in bits:
        mine = (me >> bit) & 1
        other = swap(values, "dp", 1 << bit)
        low = jnp.where(mine == 0, values, other)
        high = jnp.where(mine == 0, other, values)
        place = sum(1 for a in axes if a > bit)
        values = jnp.stack([low, high], axis=1 + place)
        axes = sorted(axes + [bit], reverse=True)
    return values


def unmix(values, index, axis=0):
    count = values.shape[axis]
    lead, tail = values.shape[:axis], values.shape[axis + 1 :]
    bits = count.bit_length() - 1
    values = values.reshape(lead + (2,) * bits + tail)
    for place in range(bits):
        bit = bits - 1 - place
        flipped = jnp.flip(values, axis + place)
        values = jnp.where((index >> bit) & 1 == 1, flipped, values)
    return values.reshape(lead + (count,) + tail)


def adam(left_mat, right_mat, first_old, second_old, whole, precision):
    partway = jnp.einsum("ia,ij->aj", left_mat, whole, precision=precision)
    rotated = jnp.einsum("aj,jb->ab", partway, right_mat, precision=precision)
    first_new = beta_one * first_old + (1.0 - beta_one) * rotated
    second_new = beta_two * second_old + (1.0 - beta_two) * rotated * rotated
    correct_one = 1.0 - beta_one**step_count
    correct_two = 1.0 - beta_two**step_count
    scaled = first_new / correct_one / (jnp.sqrt(second_new / correct_two) + epsilon)
    back_rot = jnp.einsum("ab,jb->aj", scaled, right_mat, precision=precision)
    change = jnp.einsum("ia,aj->ij", left_mat, back_rot, precision=precision)
    return first_new, second_new, change


def shard_exchange(parts):
    arrived = {k: swap(parts[k], "shard", k, f"shard_{k}") for k in (2, 3, 1)}
    return [parts[0]] + [arrived[k] for k in (1, 2, 3)]


def routed(partials, params, left_basis, right_basis, first_moment, second_moment, owner_list):
    high = lax.Precision.HIGH
    core, along_x, along_y, across = 1, 2, 4, 6
    shard_here = lax.axis_index("shard")
    data_here = lax.axis_index("dp")
    shard_count = lax.axis_size("shard")
    data_count = lax.axis_size("dp")
    device_total = shard_count * data_count
    home_count, row_count, width = params.shape
    half = home_count // 2
    piece = (row_count // shard_count, width)
    chips = data_count // 2
    my_core = data_here & core
    shard_half, shard_low = shard_here >> 1, shard_here & 1

    def set_of(values, index):
        split = values.reshape((home_count, 2, values.shape[1] // 2, width))
        return take(split, 1, index)

    grid = partials[0].reshape((home_count, chips, 2, row_count, width))
    away_rows = take(grid, 2, 1 - my_core)
    own_rows = take(grid, 2, my_core)
    away_rows, own_rows = lax.optimization_barrier((away_rows, own_rows))

    def rows_of(values, mask):
        return take(values, 1, (data_here ^ mask) // 2).astype(jnp.float32)

    near, far = {}, {}
    for mask in (across, along_x, along_y, 0):
        total = rows_of(own_rows, mask) + swap(
            rows_of(away_rows, mask), "dp", core, f"sum_core_{mask}"
        )
        near[mask], far[mask] = lax.optimization_barrier(
            (set_of(total, shard_half), set_of(total, 1 - shard_half))
        )
        if mask == across:
            own_rows, near[mask], far[mask] = lax.optimization_barrier(
                (own_rows, near[mask], far[mask])
            )
    far_relay = far[along_y] + swap(far[across], "dp", along_x, "sum_across_far")
    near_relay = near[along_x] + swap(near[across], "dp", along_y, "sum_across_near")
    far_sum = far[0] + swap(far[along_x], "dp", along_x, "sum_x_far")
    far_sum = lax.optimization_barrier(far_sum)
    far_sum = far_sum + swap(far_relay, "dp", along_y, "sum_relay_far")
    near_sum = near[0] + swap(near_relay, "dp", along_x, "sum_relay_near")
    near_sum = lax.optimization_barrier(near_sum)
    near_sum = near_sum + swap(near[along_y], "dp", along_y, "sum_y_near")

    mixed = shard_exchange(
        [
            set_of(near_sum, shard_low),
            set_of(near_sum, 1 - shard_low),
            set_of(far_sum, shard_low),
            set_of(far_sum, 1 - shard_low),
        ]
    )
    owners = unmix(owner_list.reshape(shard_count, home_count), shard_here).reshape(1, -1)
    device_ids = jnp.arange(device_total, dtype=jnp.int32)
    picker = (owners == device_ids[:, None]).astype(jnp.float32)
    pieces = jnp.concatenate(mixed, axis=0).reshape(device_total, -1)
    leaving = jnp.einsum("eb,bn->en", picker, pieces, precision=high)
    whole = lax.all_to_all(
        leaving.reshape((device_total,) + piece),
        ("dp", "shard"),
        split_axis=0,
        concat_axis=0,
        tiled=True,
    ).reshape(width, width)

    first_new, second_new, change = adam(
        left_basis[0, 0, 0],
        right_basis[0, 0, 0],
        first_moment[0, 0, 0],
        second_moment[0, 0, 0],
        whole,
        high,
    )

    coming = lax.all_to_all(
        change.reshape((device_total,) + piece),
        ("dp", "shard"),
        split_axis=0,
        concat_axis=0,
        tiled=True,
    ).reshape(device_total, -1)
    back = jnp.einsum("eb,en->bn", picker, coming, precision=high)
    back = back.reshape((shard_count, home_count) + piece)
    returned = shard_exchange([back[k] for k in range(shard_count)])

    new_home = params
    for k in (0, 3, 2, 1):
        start = (shard_here ^ k) * piece[0]
        home = lax.dynamic_slice_in_dim(params, start, piece[0], axis=1)
        home = home - learn_rate * (returned[k] + decay_rate * home)
        new_home = lax.dynamic_update_slice_in_dim(new_home, home, start, axis=1)

    low, top = new_home[:half], new_home[half:]
    x_top = swap(top, "dp", along_x, "rows_x_top")
    y_low = swap(low, "dp", along_y, "rows_y_low")
    other = swap(new_home, "dp", core, "rows_core_own")
    x_low = swap(low, "dp", along_x, "rows_x_low")
    y_top = swap(top, "dp", along_y, "rows_y_top")
    far_top = swap(x_top, "dp", along_y, "rows_relay_top")
    far_low = swap(y_low, "dp", along_x, "rows_relay_low")
    x_rows = jnp.concatenate([x_low, x_top], axis=0)
    y_rows = jnp.concatenate([y_top, y_low], axis=0)
    x_rows, y_rows, far_top, first_new, second_new = lax.optimization_barrier(
        (x_rows, y_rows, far_top, first_new, second_new)
    )
    far_rows = jnp.concatenate([far_low, far_top], axis=0)
    y_other = swap(y_rows, "dp", core, "rows_core_y")
    updated = jnp.zeros((home_count, width, width), jnp.float32)
    for mask, block, values in (
        (0, 0, new_home),
        (core, 0, other),
        (along_x, 0, x_rows),
        (along_y, half, y_rows[:half]),
        (along_y, 0, y_rows[half:]),
        (along_x ^ core, 0, swap(x_rows, "dp", core, "rows_core_x")),
        (along_y ^ core, half, y_other[:half]),
        (along_y ^ core, 0, y_other[half:]),
        (across, 0, far_rows),
        (across ^ core, 0, swap(far_rows, "dp", core, "rows_core_far")),
    ):
        start = (data_here ^ mask) * row_count
        updated = lax.dynamic_update_slice(updated, values, (block, start, 0))
    return updated, first_new[None, None, None], second_new[None, None, None]


def gathered(partials, params, left_basis, right_basis, first_moment, second_moment, owner_list):
    highest = lax.Precision.HIGHEST
    shard_here = lax.axis_index("shard")
    data_here = lax.axis_index("dp")
    shard_count = lax.axis_size("shard")
    data_count = lax.axis_size("dp")
    device_total = shard_count * data_count
    home_count, row_count, width = params.shape
    block_total = owner_list.shape[0]
    bit_count = data_count.bit_length() - 1
    high_low = list(range(bit_count))[::-1]
    middle = home_count // 2

    grid = partials[0].reshape((home_count,) + (2,) * bit_count + (row_count, width))
    low_first = halve(grid[:middle], high_low, list(range(bit_count)), data_here)
    high_first = halve(
        grid[middle:], high_low, [0] + list(range(1, bit_count))[::-1], data_here
    )
    summed = jnp.concatenate([low_first, high_first], axis=0)

    piece = row_count * width // shard_count
    cut = summed.reshape(home_count, shard_count, piece).swapaxes(0, 1)
    pieces = lax.all_to_all(cut, "shard", split_axis=0, concat_axis=0, tiled=True).reshape(
        block_total, piece
    )
    device_ids = jnp.arange(device_total, dtype=jnp.int32)
    picker = (owner_list[None, :] == device_ids[:, None]).astype(jnp.float32)
    leaving = jnp.einsum("eb,bn->en", picker, pieces, precision=highest)
    whole = lax.all_to_all(
        leaving, ("dp", "shard"), split_axis=0, concat_axis=0, tiled=True
    ).reshape(width, width)

    left_mat = left_basis[0, 0, 0]
    right_mat = right_basis[0, 0, 0]
    first_old = first_moment[0, 0, 0]
    second_old = second_moment[0, 0, 0]
    first_new, second_new, change = adam(
        left_mat, right_mat, first_old, second_old, whole, highest
    )

    coming = lax.all_to_all(
        change.reshape(device_total, piece), ("dp", "shard"), split_axis=0, concat_axis=0, tiled=True
    )
    back = jnp.einsum("eb,en->bn", picker, coming, precision=highest)
    returned = lax.all_to_all(
        back.reshape(shard_count, home_count, piece), "shard", split_axis=0, concat_axis=0, tiled=True
    )
    returned = returned.swapaxes(0, 1).reshape(home_count, row_count, width)
    new_home = params - learn_rate * (returned + decay_rate * params)
    updated = jnp.concatenate(
        [
            spread(new_home[:middle], high_low, data_here),
            spread(new_home[middle:], list(range(1, bit_count)) + [0], data_here),
        ],
        axis=0,
    ).reshape(home_count, width, width)

    my_id = data_here * shard_count + shard_here
    live = jnp.any(owner_list == my_id)
    first_keep = jnp.where(live, first_new, first_old)
    second_keep = jnp.where(live, second_new, second_old)
    return (updated, first_keep[None, None, None], second_keep[None, None, None])


def local(partials, params, left_basis, right_basis, first_moment, second_moment, owner_list):
    shard_count, data_count = lax.axis_size("shard"), lax.axis_size("dp")
    plain = (data_count, shard_count) != (8, 4) or params.shape[1] % (8 * shard_count) != 0
    plain = plain or owner_list.shape[0] != shard_count * data_count or params.shape[0] % 2 != 0
    form = gathered if plain else routed
    return form(
        partials, params, left_basis, right_basis, first_moment, second_moment, owner_list
    )


def solution(mesh):
    return jax.shard_map(
        local,
        mesh=mesh,
        in_specs=(
            P("dp", "shard", None, None),
            P("shard", "dp", None),
            P("dp", "shard", None, None, None),
            P("dp", "shard", None, None, None),
            P("dp", "shard", None, None, None),
            P("dp", "shard", None, None, None),
            P(),
        ),
        out_specs=(
            P("shard", None, None),
            P("dp", "shard", None, None, None),
            P("dp", "shard", None, None, None),
        ),
        check_vma=False,
    )
```

```python
import jax
import jax.numpy as jnp
from jax import lax
from jax.sharding import PartitionSpec as P

beta_one = 0.9
beta_two = 0.95
epsilon = 1e-08
learn_rate = 0.2
decay_rate = 0.1
step_count = 10


def swap(values, name, mask, what="swap"):
    masks = mask if isinstance(mask, tuple) else (mask, mask)
    pairs = [(i, i ^ masks[i & 1]) for i in range(lax.axis_size(name))]
    with jax.named_scope(what):
        return lax.ppermute(values, name, pairs)


def take(values, axis, index):
    return lax.dynamic_index_in_dim(values, index, axis, keepdims=False)


def halve(values, axes, bits, me):
    for bit in bits:
        axis = 1 + axes.index(bit)
        mine = (me >> bit) & 1
        away = take(values, axis, 1 - mine).astype(jnp.float32)
        here = take(values, axis, mine).astype(jnp.float32)
        values = here + swap(away, "dp", 1 << bit)
        axes = [a for a in axes if a != bit]
    return values


def spread(values, bits, me):
    axes = []
    for bit in bits:
        mine = (me >> bit) & 1
        other = swap(values, "dp", 1 << bit)
        low = jnp.where(mine == 0, values, other)
        high = jnp.where(mine == 0, other, values)
        place = sum(1 for a in axes if a > bit)
        values = jnp.stack([low, high], axis=1 + place)
        axes = sorted(axes + [bit], reverse=True)
    return values


def unmix(values, index, axis=0):
    count = values.shape[axis]
    lead, tail = values.shape[:axis], values.shape[axis + 1 :]
    bits = count.bit_length() - 1
    values = values.reshape(lead + (2,) * bits + tail)
    for place in range(bits):
        bit = bits - 1 - place
        flipped = jnp.flip(values, axis + place)
        values = jnp.where((index >> bit) & 1 == 1, flipped, values)
    return values.reshape(lead + (count,) + tail)


def adam(left_mat, right_mat, first_old, second_old, whole, precision):
    partway = jnp.einsum("ia,ij->aj", left_mat, whole, precision=precision)
    rotated = jnp.einsum("aj,jb->ab", partway, right_mat, precision=precision)
    first_new = beta_one * first_old + (1.0 - beta_one) * rotated
    second_new = beta_two * second_old + (1.0 - beta_two) * rotated * rotated
    correct_one = 1.0 - beta_one**step_count
    correct_two = 1.0 - beta_two**step_count
    scaled = first_new / correct_one / (jnp.sqrt(second_new / correct_two) + epsilon)
    back_rot = jnp.einsum("ab,jb->aj", scaled, right_mat, precision=precision)
    change = jnp.einsum("ia,aj->ij", left_mat, back_rot, precision=precision)
    return first_new, second_new, change


def shard_exchange(parts):
    arrived = {k: swap(parts[k], "shard", k, f"shard_{k}") for k in (2, 3, 1)}
    return [parts[0]] + [arrived[k] for k in (1, 2, 3)]


def routed(partials, params, left_basis, right_basis, first_moment, second_moment, owner_list):
    high = lax.Precision.HIGH
    core, across = 1, 6
    first_link, second_link = (2, 4), (4, 2)
    shard_here = lax.axis_index("shard")
    data_here = lax.axis_index("dp")
    shard_count = lax.axis_size("shard")
    data_count = lax.axis_size("dp")
    device_total = shard_count * data_count
    home_count, row_count, width = params.shape
    half = home_count // 2
    piece = (row_count // shard_count, width)
    chips = data_count // 2
    my_core = data_here & core
    first_chip = jnp.where(my_core == 0, *first_link)
    second_chip = across - first_chip
    shard_half, shard_low = shard_here >> 1, shard_here & 1

    def set_of(values, index):
        split = values.reshape((home_count, 2, values.shape[1] // 2, width))
        return take(split, 1, index)

    grid = partials[0].reshape((home_count, chips, 2, row_count, width))
    away_rows = take(grid, 2, 1 - my_core)
    own_rows = take(grid, 2, my_core)
    away_rows, own_rows = lax.optimization_barrier((away_rows, own_rows))

    def rows_of(values, mask):
        return take(values, 1, (data_here ^ mask) // 2).astype(jnp.float32)

    near, far = {}, {}
    for name, mask, other_mask in (
        ("across", across, across),
        ("first", first_chip, second_chip),
        ("second", second_chip, first_chip),
        ("own", 0, 0),
    ):
        total = rows_of(own_rows, mask) + swap(
            rows_of(away_rows, other_mask), "dp", core, f"sum_core_{name}"
        )
        near[name], far[name] = lax.optimization_barrier(
            (set_of(total, shard_half), set_of(total, 1 - shard_half))
        )
        if name == "across":
            own_rows, near[name], far[name] = lax.optimization_barrier(
                (own_rows, near[name], far[name])
            )
    far_relay = far["second"] + swap(far["across"], "dp", first_link, "sum_across_far")
    near_relay = near["first"] + swap(near["across"], "dp", second_link, "sum_across_near")
    far_relay, near_relay = lax.optimization_barrier((far_relay, near_relay))
    far_sum = far["own"] + swap(far["first"], "dp", first_link, "sum_first_far")
    near_sum = near["own"] + swap(near["second"], "dp", second_link, "sum_second_near")
    far_sum, near_sum = lax.optimization_barrier((far_sum, near_sum))
    far_sum = far_sum + swap(far_relay, "dp", second_link, "sum_relay_far")
    near_sum = near_sum + swap(near_relay, "dp", first_link, "sum_relay_near")

    mixed = shard_exchange(
        [
            set_of(near_sum, shard_low),
            set_of(near_sum, 1 - shard_low),
            set_of(far_sum, shard_low),
            set_of(far_sum, 1 - shard_low),
        ]
    )
    owners = unmix(owner_list.reshape(shard_count, home_count), shard_here).reshape(1, -1)
    device_ids = jnp.arange(device_total, dtype=jnp.int32)
    picker = (owners == device_ids[:, None]).astype(jnp.float32)
    pieces = jnp.concatenate(mixed, axis=0).reshape(device_total, -1)
    leaving = jnp.einsum("eb,bn->en", picker, pieces, precision=high)
    whole = lax.all_to_all(
        leaving.reshape((device_total,) + piece),
        ("dp", "shard"),
        split_axis=0,
        concat_axis=0,
        tiled=True,
    ).reshape(width, width)

    first_new, second_new, change = adam(
        left_basis[0, 0, 0],
        right_basis[0, 0, 0],
        first_moment[0, 0, 0],
        second_moment[0, 0, 0],
        whole,
        high,
    )

    coming = lax.all_to_all(
        change.reshape((device_total,) + piece),
        ("dp", "shard"),
        split_axis=0,
        concat_axis=0,
        tiled=True,
    ).reshape(device_total, -1)
    back = jnp.einsum("eb,en->bn", picker, coming, precision=high)
    back = back.reshape((shard_count, home_count) + piece)
    returned = shard_exchange([back[k] for k in range(shard_count)])

    new_home = params
    for k in (0, 3, 2, 1):
        start = (shard_here ^ k) * piece[0]
        home = lax.dynamic_slice_in_dim(params, start, piece[0], axis=1)
        home = home - learn_rate * (returned[k] + decay_rate * home)
        new_home = lax.dynamic_update_slice_in_dim(new_home, home, start, axis=1)

    low, top = new_home[:half], new_home[half:]
    first_top = swap(top, "dp", first_link, "rows_first_top")
    second_low = swap(low, "dp", second_link, "rows_second_low")
    other = swap(new_home, "dp", core, "rows_core_own")
    first_low = swap(low, "dp", first_link, "rows_first_low")
    second_top = swap(top, "dp", second_link, "rows_second_top")
    far_top = swap(first_top, "dp", second_link, "rows_relay_top")
    far_low = swap(second_low, "dp", first_link, "rows_relay_low")
    first_rows = jnp.concatenate([first_low, first_top], axis=0)
    second_rows = jnp.concatenate([second_top, second_low], axis=0)
    first_rows, second_rows, far_top, first_new, second_new = lax.optimization_barrier(
        (first_rows, second_rows, far_top, first_new, second_new)
    )
    far_rows = jnp.concatenate([far_low, far_top], axis=0)
    second_other = swap(second_rows, "dp", core, "rows_core_second")
    updated = jnp.zeros((home_count, width, width), jnp.float32)
    for mask, block, values in (
        (0, 0, new_home),
        (core, 0, other),
        (first_chip, 0, first_rows),
        (second_chip, half, second_rows[:half]),
        (second_chip, 0, second_rows[half:]),
        (second_chip ^ core, 0, swap(first_rows, "dp", core, "rows_core_first")),
        (first_chip ^ core, half, second_other[:half]),
        (first_chip ^ core, 0, second_other[half:]),
        (across, 0, far_rows),
        (across ^ core, 0, swap(far_rows, "dp", core, "rows_core_far")),
    ):
        start = (data_here ^ mask) * row_count
        updated = lax.dynamic_update_slice(updated, values, (block, start, 0))
    return updated, first_new[None, None, None], second_new[None, None, None]


def gathered(partials, params, left_basis, right_basis, first_moment, second_moment, owner_list):
    highest = lax.Precision.HIGHEST
    shard_here = lax.axis_index("shard")
    data_here = lax.axis_index("dp")
    shard_count = lax.axis_size("shard")
    data_count = lax.axis_size("dp")
    device_total = shard_count * data_count
    home_count, row_count, width = params.shape
    block_total = owner_list.shape[0]
    bit_count = data_count.bit_length() - 1
    high_low = list(range(bit_count))[::-1]
    middle = home_count // 2

    grid = partials[0].reshape((home_count,) + (2,) * bit_count + (row_count, width))
    low_first = halve(grid[:middle], high_low, list(range(bit_count)), data_here)
    high_first = halve(
        grid[middle:], high_low, [0] + list(range(1, bit_count))[::-1], data_here
    )
    summed = jnp.concatenate([low_first, high_first], axis=0)

    piece = row_count * width // shard_count
    cut = summed.reshape(home_count, shard_count, piece).swapaxes(0, 1)
    pieces = lax.all_to_all(cut, "shard", split_axis=0, concat_axis=0, tiled=True).reshape(
        block_total, piece
    )
    device_ids = jnp.arange(device_total, dtype=jnp.int32)
    picker = (owner_list[None, :] == device_ids[:, None]).astype(jnp.float32)
    leaving = jnp.einsum("eb,bn->en", picker, pieces, precision=highest)
    whole = lax.all_to_all(
        leaving, ("dp", "shard"), split_axis=0, concat_axis=0, tiled=True
    ).reshape(width, width)

    left_mat = left_basis[0, 0, 0]
    right_mat = right_basis[0, 0, 0]
    first_old = first_moment[0, 0, 0]
    second_old = second_moment[0, 0, 0]
    first_new, second_new, change = adam(
        left_mat, right_mat, first_old, second_old, whole, highest
    )

    coming = lax.all_to_all(
        change.reshape(device_total, piece), ("dp", "shard"), split_axis=0, concat_axis=0, tiled=True
    )
    back = jnp.einsum("eb,en->bn", picker, coming, precision=highest)
    returned = lax.all_to_all(
        back.reshape(shard_count, home_count, piece), "shard", split_axis=0, concat_axis=0, tiled=True
    )
    returned = returned.swapaxes(0, 1).reshape(home_count, row_count, width)
    new_home = params - learn_rate * (returned + decay_rate * params)
    updated = jnp.concatenate(
        [
            spread(new_home[:middle], high_low, data_here),
            spread(new_home[middle:], list(range(1, bit_count)) + [0], data_here),
        ],
        axis=0,
    ).reshape(home_count, width, width)

    my_id = data_here * shard_count + shard_here
    live = jnp.any(owner_list == my_id)
    first_keep = jnp.where(live, first_new, first_old)
    second_keep = jnp.where(live, second_new, second_old)
    return (updated, first_keep[None, None, None], second_keep[None, None, None])


def local(partials, params, left_basis, right_basis, first_moment, second_moment, owner_list):
    shard_count, data_count = lax.axis_size("shard"), lax.axis_size("dp")
    plain = (data_count, shard_count) != (8, 4) or params.shape[1] % (8 * shard_count) != 0
    plain = plain or owner_list.shape[0] != shard_count * data_count or params.shape[0] % 2 != 0
    form = gathered if plain else routed
    return form(
        partials, params, left_basis, right_basis, first_moment, second_moment, owner_list
    )


def solution(mesh):
    return jax.shard_map(
        local,
        mesh=mesh,
        in_specs=(
            P("dp", "shard", None, None),
            P("shard", "dp", None),
            P("dp", "shard", None, None, None),
            P("dp", "shard", None, None, None),
            P("dp", "shard", None, None, None),
            P("dp", "shard", None, None, None),
            P(),
        ),
        out_specs=(
            P("shard", None, None),
            P("dp", "shard", None, None, None),
            P("dp", "shard", None, None, None),
        ),
        check_vma=False,
    )
```

```python
import jax
import jax.numpy as jnp
from jax import lax
from jax.sharding import PartitionSpec as P

beta_one = 0.9
beta_two = 0.95
epsilon = 1e-08
learn_rate = 0.2
decay_rate = 0.1
step_count = 10


def swap(values, name, mask, what="swap"):
    masks = mask if isinstance(mask, tuple) else (mask, mask)
    pairs = [(i, i ^ masks[i & 1]) for i in range(lax.axis_size(name))]
    with jax.named_scope(what):
        return lax.ppermute(values, name, pairs)


def take(values, axis, index):
    return lax.dynamic_index_in_dim(values, index, axis, keepdims=False)


def halve(values, axes, bits, me):
    for bit in bits:
        axis = 1 + axes.index(bit)
        mine = (me >> bit) & 1
        away = take(values, axis, 1 - mine).astype(jnp.float32)
        here = take(values, axis, mine).astype(jnp.float32)
        values = here + swap(away, "dp", 1 << bit)
        axes = [a for a in axes if a != bit]
    return values


def spread(values, bits, me):
    axes = []
    for bit in bits:
        mine = (me >> bit) & 1
        other = swap(values, "dp", 1 << bit)
        low = jnp.where(mine == 0, values, other)
        high = jnp.where(mine == 0, other, values)
        place = sum(1 for a in axes if a > bit)
        values = jnp.stack([low, high], axis=1 + place)
        axes = sorted(axes + [bit], reverse=True)
    return values


def unmix(values, index, axis=0):
    count = values.shape[axis]
    lead, tail = values.shape[:axis], values.shape[axis + 1 :]
    bits = count.bit_length() - 1
    values = values.reshape(lead + (2,) * bits + tail)
    for place in range(bits):
        bit = bits - 1 - place
        flipped = jnp.flip(values, axis + place)
        values = jnp.where((index >> bit) & 1 == 1, flipped, values)
    return values.reshape(lead + (count,) + tail)


def adam(left_mat, right_mat, first_old, second_old, whole, precision):
    partway = jnp.einsum("ia,ij->aj", left_mat, whole, precision=precision)
    rotated = jnp.einsum("aj,jb->ab", partway, right_mat, precision=precision)
    first_new = beta_one * first_old + (1.0 - beta_one) * rotated
    second_new = beta_two * second_old + (1.0 - beta_two) * rotated * rotated
    correct_one = 1.0 - beta_one**step_count
    correct_two = 1.0 - beta_two**step_count
    scaled = first_new / correct_one / (jnp.sqrt(second_new / correct_two) + epsilon)
    back_rot = jnp.einsum("ab,jb->aj", scaled, right_mat, precision=precision)
    change = jnp.einsum("ia,aj->ij", left_mat, back_rot, precision=precision)
    return first_new, second_new, change


def shard_exchange(parts):
    arrived = {k: swap(parts[k], "shard", k, f"shard_{k}") for k in (2, 3, 1)}
    return [parts[0]] + [arrived[k] for k in (1, 2, 3)]


def routed(partials, params, left_basis, right_basis, first_moment, second_moment, owner_list):
    high = lax.Precision.HIGH
    core, across = 1, 6
    first_link, second_link = (2, 4), (4, 2)
    near_order = (0, 1, 3, 2)
    shard_here = lax.axis_index("shard")
    data_here = lax.axis_index("dp")
    shard_count = lax.axis_size("shard")
    data_count = lax.axis_size("dp")
    device_total = shard_count * data_count
    home_count, row_count, width = params.shape
    half = home_count // 2
    piece = (row_count // shard_count, width)
    chips = data_count // 2
    my_core = data_here & core
    first_chip = jnp.where(my_core == 0, *first_link)
    second_chip = across - first_chip
    shard_half, shard_low = shard_here >> 1, shard_here & 1

    def set_of(values, index):
        split = values.reshape((home_count, 2, values.shape[1] // 2, width))
        return take(split, 1, index)

    grid = partials[0].reshape((home_count, chips, 2, row_count, width))
    away_rows = take(grid, 2, 1 - my_core)
    own_rows = take(grid, 2, my_core)
    away_rows, own_rows = lax.optimization_barrier((away_rows, own_rows))

    def rows_of(values, mask):
        return take(values, 1, (data_here ^ mask) // 2).astype(jnp.float32)

    along_x, along_y = (2, 2), (4, 4)
    near, far = {}, {}
    for mask in (across, 2, 4, 0):
        total = rows_of(own_rows, mask) + swap(
            rows_of(away_rows, mask), "dp", core, f"sum_core_{mask}"
        )
        near[mask], far[mask] = lax.optimization_barrier(
            (set_of(total, shard_half), set_of(total, 1 - shard_half))
        )
        if mask == across:
            own_rows, near[mask], far[mask] = lax.optimization_barrier(
                (own_rows, near[mask], far[mask])
            )
    far_relay = far[4] + swap(far[across], "dp", along_x, "sum_across_far")
    near_relay = near[2] + swap(near[across], "dp", along_y, "sum_across_near")
    far_sum = far[0] + swap(far[2], "dp", along_x, "sum_x_far")
    far_sum = lax.optimization_barrier(far_sum)
    far_sum = far_sum + swap(far_relay, "dp", along_y, "sum_relay_far")
    near_sum = near[0] + swap(near_relay, "dp", along_x, "sum_relay_near")
    near_sum = lax.optimization_barrier(near_sum)
    near_sum = near_sum + swap(near[4], "dp", along_y, "sum_y_near")

    near_sum, owner_list = lax.optimization_barrier((near_sum, owner_list))

    mixed = shard_exchange(
        [
            set_of(near_sum, shard_low),
            set_of(near_sum, 1 - shard_low),
            set_of(far_sum, shard_low),
            set_of(far_sum, 1 - shard_low),
        ]
    )
    owners = unmix(owner_list.reshape(shard_count, home_count), shard_here)
    owners = jnp.concatenate([owners[k] for k in near_order])[None, :]
    device_ids = jnp.arange(device_total, dtype=jnp.int32)
    picker = (owners == device_ids[:, None]).astype(jnp.float32)
    pieces = jnp.concatenate([mixed[k] for k in near_order], axis=0).reshape(device_total, -1)
    leaving = jnp.einsum("eb,bn->en", picker, pieces, precision=high)
    whole = lax.all_to_all(
        leaving.reshape((device_total,) + piece),
        ("dp", "shard"),
        split_axis=0,
        concat_axis=0,
        tiled=True,
    ).reshape(width, width)

    first_new, second_new, change = adam(
        left_basis[0, 0, 0],
        right_basis[0, 0, 0],
        first_moment[0, 0, 0],
        second_moment[0, 0, 0],
        whole,
        high,
    )

    coming = lax.all_to_all(
        change.reshape((device_total,) + piece),
        ("dp", "shard"),
        split_axis=0,
        concat_axis=0,
        tiled=True,
    ).reshape(device_total, -1)
    back = jnp.einsum("eb,en->bn", picker, coming, precision=high)
    back = back.reshape((shard_count, home_count) + piece)
    returned = shard_exchange([back[near_order.index(k)] for k in range(shard_count)])

    new_home = params
    for k in (0, 3, 2, 1):
        start = (shard_here ^ k) * piece[0]
        home = lax.dynamic_slice_in_dim(params, start, piece[0], axis=1)
        home = home - learn_rate * (returned[k] + decay_rate * home)
        new_home = lax.dynamic_update_slice_in_dim(new_home, home, start, axis=1)

    low, top = new_home[:half], new_home[half:]
    first_top = swap(top, "dp", first_link, "rows_first_top")
    second_low = swap(low, "dp", second_link, "rows_second_low")
    other = swap(new_home, "dp", core, "rows_core_own")
    first_low = swap(low, "dp", first_link, "rows_first_low")
    second_top = swap(top, "dp", second_link, "rows_second_top")
    far_top = swap(first_top, "dp", second_link, "rows_relay_top")
    far_low = swap(second_low, "dp", first_link, "rows_relay_low")
    first_rows = jnp.concatenate([first_low, first_top], axis=0)
    second_rows = jnp.concatenate([second_top, second_low], axis=0)
    first_rows, second_rows, far_top, first_new, second_new = lax.optimization_barrier(
        (first_rows, second_rows, far_top, first_new, second_new)
    )
    far_rows = jnp.concatenate([far_low, far_top], axis=0)
    second_other = swap(second_rows, "dp", core, "rows_core_second")
    updated = jnp.zeros((home_count, width, width), jnp.float32)
    for mask, block, values in (
        (0, 0, new_home),
        (core, 0, other),
        (first_chip, 0, first_rows),
        (second_chip, half, second_rows[:half]),
        (second_chip, 0, second_rows[half:]),
        (second_chip ^ core, 0, swap(first_rows, "dp", core, "rows_core_first")),
        (first_chip ^ core, half, second_other[:half]),
        (first_chip ^ core, 0, second_other[half:]),
        (across, 0, far_rows),
        (across ^ core, 0, swap(far_rows, "dp", core, "rows_core_far")),
    ):
        start = (data_here ^ mask) * row_count
        updated = lax.dynamic_update_slice(updated, values, (block, start, 0))
    return updated, first_new[None, None, None], second_new[None, None, None]


def gathered(partials, params, left_basis, right_basis, first_moment, second_moment, owner_list):
    highest = lax.Precision.HIGHEST
    shard_here = lax.axis_index("shard")
    data_here = lax.axis_index("dp")
    shard_count = lax.axis_size("shard")
    data_count = lax.axis_size("dp")
    device_total = shard_count * data_count
    home_count, row_count, width = params.shape
    block_total = owner_list.shape[0]
    bit_count = data_count.bit_length() - 1
    high_low = list(range(bit_count))[::-1]
    middle = home_count // 2

    grid = partials[0].reshape((home_count,) + (2,) * bit_count + (row_count, width))
    low_first = halve(grid[:middle], high_low, list(range(bit_count)), data_here)
    high_first = halve(
        grid[middle:], high_low, [0] + list(range(1, bit_count))[::-1], data_here
    )
    summed = jnp.concatenate([low_first, high_first], axis=0)

    piece = row_count * width // shard_count
    cut = summed.reshape(home_count, shard_count, piece).swapaxes(0, 1)
    pieces = lax.all_to_all(cut, "shard", split_axis=0, concat_axis=0, tiled=True).reshape(
        block_total, piece
    )
    device_ids = jnp.arange(device_total, dtype=jnp.int32)
    picker = (owner_list[None, :] == device_ids[:, None]).astype(jnp.float32)
    leaving = jnp.einsum("eb,bn->en", picker, pieces, precision=highest)
    whole = lax.all_to_all(
        leaving, ("dp", "shard"), split_axis=0, concat_axis=0, tiled=True
    ).reshape(width, width)

    left_mat = left_basis[0, 0, 0]
    right_mat = right_basis[0, 0, 0]
    first_old = first_moment[0, 0, 0]
    second_old = second_moment[0, 0, 0]
    first_new, second_new, change = adam(
        left_mat, right_mat, first_old, second_old, whole, highest
    )

    coming = lax.all_to_all(
        change.reshape(device_total, piece), ("dp", "shard"), split_axis=0, concat_axis=0, tiled=True
    )
    back = jnp.einsum("eb,en->bn", picker, coming, precision=highest)
    returned = lax.all_to_all(
        back.reshape(shard_count, home_count, piece), "shard", split_axis=0, concat_axis=0, tiled=True
    )
    returned = returned.swapaxes(0, 1).reshape(home_count, row_count, width)
    new_home = params - learn_rate * (returned + decay_rate * params)
    updated = jnp.concatenate(
        [
            spread(new_home[:middle], high_low, data_here),
            spread(new_home[middle:], list(range(1, bit_count)) + [0], data_here),
        ],
        axis=0,
    ).reshape(home_count, width, width)

    my_id = data_here * shard_count + shard_here
    live = jnp.any(owner_list == my_id)
    first_keep = jnp.where(live, first_new, first_old)
    second_keep = jnp.where(live, second_new, second_old)
    return (updated, first_keep[None, None, None], second_keep[None, None, None])


def local(partials, params, left_basis, right_basis, first_moment, second_moment, owner_list):
    shard_count, data_count = lax.axis_size("shard"), lax.axis_size("dp")
    plain = (data_count, shard_count) != (8, 4) or params.shape[1] % (8 * shard_count) != 0
    plain = plain or owner_list.shape[0] != shard_count * data_count or params.shape[0] % 2 != 0
    form = gathered if plain else routed
    return form(
        partials, params, left_basis, right_basis, first_moment, second_moment, owner_list
    )


def solution(mesh):
    return jax.shard_map(
        local,
        mesh=mesh,
        in_specs=(
            P("dp", "shard", None, None),
            P("shard", "dp", None),
            P("dp", "shard", None, None, None),
            P("dp", "shard", None, None, None),
            P("dp", "shard", None, None, None),
            P("dp", "shard", None, None, None),
            P(),
        ),
        out_specs=(
            P("shard", None, None),
            P("dp", "shard", None, None, None),
            P("dp", "shard", None, None, None),
        ),
        check_vma=False,
    )
```

```python
import jax
import jax.numpy as jnp
from jax import lax
from jax.sharding import PartitionSpec as P

beta_one = 0.9
beta_two = 0.95
epsilon = 1e-08
learn_rate = 0.2
decay_rate = 0.1
step_count = 10


def swap(values, name, mask, what="swap"):
    masks = mask if isinstance(mask, tuple) else (mask, mask)
    pairs = [(i, i ^ masks[i & 1]) for i in range(lax.axis_size(name))]
    with jax.named_scope(what):
        return lax.ppermute(values, name, pairs)


def take(values, axis, index):
    return lax.dynamic_index_in_dim(values, index, axis, keepdims=False)


def halve(values, axes, bits, me):
    for bit in bits:
        axis = 1 + axes.index(bit)
        mine = (me >> bit) & 1
        away = take(values, axis, 1 - mine).astype(jnp.float32)
        here = take(values, axis, mine).astype(jnp.float32)
        values = here + swap(away, "dp", 1 << bit)
        axes = [a for a in axes if a != bit]
    return values


def spread(values, bits, me):
    axes = []
    for bit in bits:
        mine = (me >> bit) & 1
        other = swap(values, "dp", 1 << bit)
        low = jnp.where(mine == 0, values, other)
        high = jnp.where(mine == 0, other, values)
        place = sum(1 for a in axes if a > bit)
        values = jnp.stack([low, high], axis=1 + place)
        axes = sorted(axes + [bit], reverse=True)
    return values


def unmix(values, index, axis=0):
    count = values.shape[axis]
    lead, tail = values.shape[:axis], values.shape[axis + 1 :]
    bits = count.bit_length() - 1
    values = values.reshape(lead + (2,) * bits + tail)
    for place in range(bits):
        bit = bits - 1 - place
        flipped = jnp.flip(values, axis + place)
        values = jnp.where((index >> bit) & 1 == 1, flipped, values)
    return values.reshape(lead + (count,) + tail)


def adam(left_mat, right_mat, first_old, second_old, whole, precision):
    partway = jnp.einsum("ia,ij->aj", left_mat, whole, precision=precision)
    rotated = jnp.einsum("aj,jb->ab", partway, right_mat, precision=precision)
    first_new = beta_one * first_old + (1.0 - beta_one) * rotated
    second_new = beta_two * second_old + (1.0 - beta_two) * rotated * rotated
    correct_one = 1.0 - beta_one**step_count
    correct_two = 1.0 - beta_two**step_count
    scaled = first_new / correct_one / (jnp.sqrt(second_new / correct_two) + epsilon)
    back_rot = jnp.einsum("ab,jb->aj", scaled, right_mat, precision=precision)
    change = jnp.einsum("ia,aj->ij", left_mat, back_rot, precision=precision)
    return first_new, second_new, change


def shard_exchange(parts):
    arrived = {k: swap(parts[k], "shard", k, f"shard_{k}") for k in (2, 3, 1)}
    return [parts[0]] + [arrived[k] for k in (1, 2, 3)]


def routed(partials, params, left_basis, right_basis, first_moment, second_moment, owner_list):
    high = lax.Precision.HIGH
    core, across = 1, 6
    first_link, second_link = (2, 4), (4, 2)
    near_order = (0, 1, 3, 2)
    shard_here = lax.axis_index("shard")
    data_here = lax.axis_index("dp")
    shard_count = lax.axis_size("shard")
    data_count = lax.axis_size("dp")
    device_total = shard_count * data_count
    home_count, row_count, width = params.shape
    half = home_count // 2
    piece = (row_count // shard_count, width)
    chips = data_count // 2
    my_core = data_here & core
    first_chip = jnp.where(my_core == 0, *first_link)
    second_chip = across - first_chip
    shard_half, shard_low = shard_here >> 1, shard_here & 1

    def set_of(values, index):
        split = values.reshape((home_count, 2, values.shape[1] // 2, width))
        return take(split, 1, index)

    grid = partials[0].reshape((home_count, chips, 2, row_count, width))

    def rows_of(values, mask):
        return take(values, 1, (data_here ^ mask) // 2).astype(jnp.float32)

    away = {"across": rows_of(take(grid, 2, 1 - my_core), across)}
    grid, away["across"] = lax.optimization_barrier((grid, away["across"]))
    away_rows = take(grid, 2, 1 - my_core)
    own_rows = take(grid, 2, my_core)
    away_rows, own_rows = lax.optimization_barrier((away_rows, own_rows))

    near, far = {}, {}
    for name, mask, other_mask in (
        ("across", across, across),
        ("first", first_chip, second_chip),
        ("second", second_chip, first_chip),
        ("own", 0, 0),
    ):
        if name != "across":
            away[name] = rows_of(away_rows, other_mask)
        total = rows_of(own_rows, mask) + swap(away[name], "dp", core, f"sum_core_{name}")
        near[name], far[name] = lax.optimization_barrier(
            (set_of(total, shard_half), set_of(total, 1 - shard_half))
        )
        if name == "across":
            own_rows, near[name], far[name] = lax.optimization_barrier(
                (own_rows, near[name], far[name])
            )

    def sends(rows, what):
        relay = rows["second"] + swap(rows["across"], "dp", first_link, f"sum_across_{what}")
        direct = swap(rows["first"], "dp", first_link, f"sum_first_{what}")
        return direct, swap(relay, "dp", second_link, f"sum_relay_{what}")

    direct, relayed = sends(far, "far")
    far_sum = lax.optimization_barrier(far["own"] + direct) + relayed
    direct, relayed = sends(near, "near")
    near_sum = lax.optimization_barrier(near["own"] + relayed) + direct
    near_sum, owner_list = lax.optimization_barrier((near_sum, owner_list))

    mixed = shard_exchange(
        [
            set_of(near_sum, shard_low),
            set_of(near_sum, 1 - shard_low),
            set_of(far_sum, shard_low),
            set_of(far_sum, 1 - shard_low),
        ]
    )
    owners = unmix(owner_list.reshape(shard_count, home_count), shard_here)
    owners = jnp.concatenate([owners[k] for k in near_order])[None, :]
    device_ids = jnp.arange(device_total, dtype=jnp.int32)
    picker = (owners == device_ids[:, None]).astype(jnp.float32)
    pieces = jnp.concatenate([mixed[k] for k in near_order], axis=0).reshape(device_total, -1)
    leaving = jnp.einsum("eb,bn->en", picker, pieces, precision=high)
    whole = lax.all_to_all(
        leaving.reshape((device_total,) + piece),
        ("dp", "shard"),
        split_axis=0,
        concat_axis=0,
        tiled=True,
    ).reshape(width, width)

    first_new, second_new, change = adam(
        left_basis[0, 0, 0],
        right_basis[0, 0, 0],
        first_moment[0, 0, 0],
        second_moment[0, 0, 0],
        whole,
        high,
    )

    coming = lax.all_to_all(
        change.reshape((device_total,) + piece),
        ("dp", "shard"),
        split_axis=0,
        concat_axis=0,
        tiled=True,
    ).reshape(device_total, -1)
    coming, data_here, shard_here, params = lax.optimization_barrier(
        (coming, data_here, shard_here, params)
    )
    first_chip = jnp.where((data_here & core) == 0, *first_link)
    second_chip = across - first_chip
    back = jnp.einsum("eb,en->bn", picker, coming, precision=high)
    back = back.reshape((shard_count, home_count) + piece)
    returned = shard_exchange([back[near_order.index(k)] for k in range(shard_count)])

    new_home = params
    for k in (0, 3, 2, 1):
        start = (shard_here ^ k) * piece[0]
        home = lax.dynamic_slice_in_dim(params, start, piece[0], axis=1)
        home = home - learn_rate * (returned[k] + decay_rate * home)
        new_home = lax.dynamic_update_slice_in_dim(new_home, home, start, axis=1)

    low, top = new_home[:half], new_home[half:]
    first_top = swap(top, "dp", first_link, "rows_first_top")
    second_low = swap(low, "dp", second_link, "rows_second_low")
    other = swap(new_home, "dp", core, "rows_core_own")
    first_low = swap(low, "dp", first_link, "rows_first_low")
    second_top = swap(top, "dp", second_link, "rows_second_top")
    far_top = swap(first_top, "dp", second_link, "rows_relay_top")
    far_low = swap(second_low, "dp", first_link, "rows_relay_low")
    first_rows = jnp.concatenate([first_low, first_top], axis=0)
    second_rows = jnp.concatenate([second_top, second_low], axis=0)
    first_rows, second_rows, far_top, first_new, second_new = lax.optimization_barrier(
        (first_rows, second_rows, far_top, first_new, second_new)
    )
    far_rows = jnp.concatenate([far_low, far_top], axis=0)
    second_other = swap(second_rows, "dp", core, "rows_core_second")
    updated = jnp.zeros((home_count, width, width), jnp.float32)
    for mask, block, values in (
        (0, 0, new_home),
        (core, 0, other),
        (first_chip, 0, first_rows),
        (second_chip, half, second_rows[:half]),
        (second_chip, 0, second_rows[half:]),
        (second_chip ^ core, 0, swap(first_rows, "dp", core, "rows_core_first")),
        (first_chip ^ core, half, second_other[:half]),
        (first_chip ^ core, 0, second_other[half:]),
        (across, 0, far_rows),
        (across ^ core, 0, swap(far_rows, "dp", core, "rows_core_far")),
    ):
        start = (data_here ^ mask) * row_count
        updated = lax.dynamic_update_slice(updated, values, (block, start, 0))
    return updated, first_new[None, None, None], second_new[None, None, None]


def gathered(partials, params, left_basis, right_basis, first_moment, second_moment, owner_list):
    highest = lax.Precision.HIGHEST
    shard_here = lax.axis_index("shard")
    data_here = lax.axis_index("dp")
    shard_count = lax.axis_size("shard")
    data_count = lax.axis_size("dp")
    device_total = shard_count * data_count
    home_count, row_count, width = params.shape
    block_total = owner_list.shape[0]
    bit_count = data_count.bit_length() - 1
    high_low = list(range(bit_count))[::-1]
    middle = home_count // 2

    grid = partials[0].reshape((home_count,) + (2,) * bit_count + (row_count, width))
    low_first = halve(grid[:middle], high_low, list(range(bit_count)), data_here)
    high_first = halve(
        grid[middle:], high_low, [0] + list(range(1, bit_count))[::-1], data_here
    )
    summed = jnp.concatenate([low_first, high_first], axis=0)

    piece = row_count * width // shard_count
    cut = summed.reshape(home_count, shard_count, piece).swapaxes(0, 1)
    pieces = lax.all_to_all(cut, "shard", split_axis=0, concat_axis=0, tiled=True).reshape(
        block_total, piece
    )
    device_ids = jnp.arange(device_total, dtype=jnp.int32)
    picker = (owner_list[None, :] == device_ids[:, None]).astype(jnp.float32)
    leaving = jnp.einsum("eb,bn->en", picker, pieces, precision=highest)
    whole = lax.all_to_all(
        leaving, ("dp", "shard"), split_axis=0, concat_axis=0, tiled=True
    ).reshape(width, width)

    left_mat = left_basis[0, 0, 0]
    right_mat = right_basis[0, 0, 0]
    first_old = first_moment[0, 0, 0]
    second_old = second_moment[0, 0, 0]
    first_new, second_new, change = adam(
        left_mat, right_mat, first_old, second_old, whole, highest
    )

    coming = lax.all_to_all(
        change.reshape(device_total, piece), ("dp", "shard"), split_axis=0, concat_axis=0, tiled=True
    )
    back = jnp.einsum("eb,en->bn", picker, coming, precision=highest)
    returned = lax.all_to_all(
        back.reshape(shard_count, home_count, piece), "shard", split_axis=0, concat_axis=0, tiled=True
    )
    returned = returned.swapaxes(0, 1).reshape(home_count, row_count, width)
    new_home = params - learn_rate * (returned + decay_rate * params)
    updated = jnp.concatenate(
        [
            spread(new_home[:middle], high_low, data_here),
            spread(new_home[middle:], list(range(1, bit_count)) + [0], data_here),
        ],
        axis=0,
    ).reshape(home_count, width, width)

    my_id = data_here * shard_count + shard_here
    live = jnp.any(owner_list == my_id)
    first_keep = jnp.where(live, first_new, first_old)
    second_keep = jnp.where(live, second_new, second_old)
    return (updated, first_keep[None, None, None], second_keep[None, None, None])


def local(partials, params, left_basis, right_basis, first_moment, second_moment, owner_list):
    shard_count, data_count = lax.axis_size("shard"), lax.axis_size("dp")
    plain = (data_count, shard_count) != (8, 4) or params.shape[1] % (8 * shard_count) != 0
    plain = plain or owner_list.shape[0] != shard_count * data_count or params.shape[0] % 2 != 0
    form = gathered if plain else routed
    return form(
        partials, params, left_basis, right_basis, first_moment, second_moment, owner_list
    )


def solution(mesh):
    return jax.shard_map(
        local,
        mesh=mesh,
        in_specs=(
            P("dp", "shard", None, None),
            P("shard", "dp", None),
            P("dp", "shard", None, None, None),
            P("dp", "shard", None, None, None),
            P("dp", "shard", None, None, None),
            P("dp", "shard", None, None, None),
            P(),
        ),
        out_specs=(
            P("shard", None, None),
            P("dp", "shard", None, None, None),
            P("dp", "shard", None, None, None),
        ),
        check_vma=False,
    )
```

```python
import jax
import jax.numpy as jnp
from jax import lax
from jax.sharding import PartitionSpec as P

beta_one = 0.9
beta_two = 0.95
epsilon = 1e-08
learn_rate = 0.2
decay_rate = 0.1
step_count = 10


def swap(values, name, mask, what="swap"):
    masks = mask if isinstance(mask, tuple) else (mask, mask)
    pairs = [(i, i ^ masks[i & 1]) for i in range(lax.axis_size(name))]
    with jax.named_scope(what):
        return lax.ppermute(values, name, pairs)


def take(values, axis, index):
    return lax.dynamic_index_in_dim(values, index, axis, keepdims=False)


def halve(values, axes, bits, me):
    for bit in bits:
        axis = 1 + axes.index(bit)
        mine = (me >> bit) & 1
        away = take(values, axis, 1 - mine).astype(jnp.float32)
        here = take(values, axis, mine).astype(jnp.float32)
        values = here + swap(away, "dp", 1 << bit)
        axes = [a for a in axes if a != bit]
    return values


def spread(values, bits, me):
    axes = []
    for bit in bits:
        mine = (me >> bit) & 1
        other = swap(values, "dp", 1 << bit)
        low = jnp.where(mine == 0, values, other)
        high = jnp.where(mine == 0, other, values)
        place = sum(1 for a in axes if a > bit)
        values = jnp.stack([low, high], axis=1 + place)
        axes = sorted(axes + [bit], reverse=True)
    return values


def unmix(values, index, axis=0):
    count = values.shape[axis]
    lead, tail = values.shape[:axis], values.shape[axis + 1 :]
    bits = count.bit_length() - 1
    values = values.reshape(lead + (2,) * bits + tail)
    for place in range(bits):
        bit = bits - 1 - place
        flipped = jnp.flip(values, axis + place)
        values = jnp.where((index >> bit) & 1 == 1, flipped, values)
    return values.reshape(lead + (count,) + tail)


def adam(left_mat, right_mat, first_old, second_old, whole, precision):
    partway = jnp.einsum("ia,ij->aj", left_mat, whole, precision=precision)
    rotated = jnp.einsum("aj,jb->ab", partway, right_mat, precision=precision)
    first_new = beta_one * first_old + (1.0 - beta_one) * rotated
    second_new = beta_two * second_old + (1.0 - beta_two) * rotated * rotated
    correct_one = 1.0 - beta_one**step_count
    correct_two = 1.0 - beta_two**step_count
    scaled = first_new / correct_one / (jnp.sqrt(second_new / correct_two) + epsilon)
    back_rot = jnp.einsum("ab,jb->aj", scaled, right_mat, precision=precision)
    change = jnp.einsum("ia,aj->ij", left_mat, back_rot, precision=precision)
    return first_new, second_new, change


def shard_exchange(parts):
    arrived = {k: swap(parts[k], "shard", k, f"shard_{k}") for k in (2, 3, 1)}
    return [parts[0]] + [arrived[k] for k in (1, 2, 3)]


def routed(partials, params, left_basis, right_basis, first_moment, second_moment, owner_list):
    high = lax.Precision.HIGH
    core, across = 1, 6
    first_link, second_link = (2, 4), (4, 2)
    near_order = (0, 1, 3, 2)
    shard_here = lax.axis_index("shard")
    data_here = lax.axis_index("dp")
    shard_count = lax.axis_size("shard")
    data_count = lax.axis_size("dp")
    device_total = shard_count * data_count
    home_count, row_count, width = params.shape
    half = home_count // 2
    piece = (row_count // shard_count, width)
    chips = data_count // 2
    my_core = data_here & core
    first_chip = jnp.where(my_core == 0, *first_link)
    second_chip = across - first_chip
    shard_half, shard_low = shard_here >> 1, shard_here & 1

    def set_of(values, index):
        split = values.reshape((home_count, 2, values.shape[1] // 2, width))
        return take(split, 1, index)

    grid = partials[0].reshape((home_count, chips, 2, row_count, width))
    away_rows = take(grid, 2, 1 - my_core)
    own_rows = take(grid, 2, my_core)
    away_rows, own_rows = lax.optimization_barrier((away_rows, own_rows))

    def rows_of(values, mask):
        return take(values, 1, (data_here ^ mask) // 2).astype(jnp.float32)

    near, far = {}, {}
    for name, mask, other_mask in (
        ("across", across, across),
        ("first", first_chip, second_chip),
        ("second", second_chip, first_chip),
        ("own", 0, 0),
    ):
        total = rows_of(own_rows, mask) + swap(
            rows_of(away_rows, other_mask), "dp", core, f"sum_core_{name}"
        )
        near[name], far[name] = lax.optimization_barrier(
            (set_of(total, shard_half), set_of(total, 1 - shard_half))
        )
        if name == "across":
            own_rows, near[name], far[name] = lax.optimization_barrier(
                (own_rows, near[name], far[name])
            )

    def sends(rows, what):
        relay = rows["second"] + swap(rows["across"], "dp", first_link, f"sum_across_{what}")
        direct = swap(rows["first"], "dp", first_link, f"sum_first_{what}")
        return direct, swap(relay, "dp", second_link, f"sum_relay_{what}")

    direct, relayed = sends(far, "far")
    far_sum = lax.optimization_barrier(far["own"] + direct) + relayed
    direct, relayed = sends(near, "near")
    near_sum = lax.optimization_barrier(near["own"] + relayed) + direct
    near_sum, owner_list = lax.optimization_barrier((near_sum, owner_list))

    mixed = shard_exchange(
        [
            set_of(near_sum, shard_low),
            set_of(near_sum, 1 - shard_low),
            set_of(far_sum, shard_low),
            set_of(far_sum, 1 - shard_low),
        ]
    )
    owners = unmix(owner_list.reshape(shard_count, home_count), shard_here)
    owners = jnp.concatenate([owners[k] for k in near_order])[None, :]
    device_ids = jnp.arange(device_total, dtype=jnp.int32)
    picker = (owners == device_ids[:, None]).astype(jnp.float32)
    pieces = jnp.concatenate([mixed[k] for k in near_order], axis=0).reshape(device_total, -1)
    leaving = jnp.einsum("eb,bn->en", picker, pieces, precision=high)
    whole = lax.all_to_all(
        leaving.reshape((device_total,) + piece),
        ("dp", "shard"),
        split_axis=0,
        concat_axis=0,
        tiled=True,
    ).reshape(width, width)

    first_new, second_new, change = adam(
        left_basis[0, 0, 0],
        right_basis[0, 0, 0],
        first_moment[0, 0, 0],
        second_moment[0, 0, 0],
        whole,
        high,
    )

    coming = lax.all_to_all(
        change.reshape((device_total,) + piece),
        ("dp", "shard"),
        split_axis=0,
        concat_axis=0,
        tiled=True,
    ).reshape(device_total, -1)
    coming, data_here, shard_here, params = lax.optimization_barrier(
        (coming, data_here, shard_here, params)
    )
    first_chip = jnp.where((data_here & core) == 0, *first_link)
    second_chip = across - first_chip
    back = jnp.einsum("eb,en->bn", picker, coming, precision=high)
    back = back.reshape((shard_count, home_count) + piece)
    returned = shard_exchange([back[near_order.index(k)] for k in range(shard_count)])

    new_home = params
    for k in (0, 3, 2, 1):
        start = (shard_here ^ k) * piece[0]
        home = lax.dynamic_slice_in_dim(params, start, piece[0], axis=1)
        home = home - learn_rate * (returned[k] + decay_rate * home)
        new_home = lax.dynamic_update_slice_in_dim(new_home, home, start, axis=1)

    low, top = new_home[:half], new_home[half:]
    first_top = swap(top, "dp", first_link, "rows_first_top")
    second_low = swap(low, "dp", second_link, "rows_second_low")
    other = swap(new_home, "dp", core, "rows_core_own")
    first_low = swap(low, "dp", first_link, "rows_first_low")
    second_top = swap(top, "dp", second_link, "rows_second_top")
    far_top = swap(first_top, "dp", second_link, "rows_relay_top")
    far_low = swap(second_low, "dp", first_link, "rows_relay_low")
    first_rows = jnp.concatenate([first_low, first_top], axis=0)
    second_rows = jnp.concatenate([second_top, second_low], axis=0)
    first_rows, second_rows, far_top, first_new, second_new = lax.optimization_barrier(
        (first_rows, second_rows, far_top, first_new, second_new)
    )
    far_rows = jnp.concatenate([far_low, far_top], axis=0)
    second_other = swap(second_rows, "dp", core, "rows_core_second")
    updated = jnp.zeros((home_count, width, width), jnp.float32)
    for mask, block, values in (
        (0, 0, new_home),
        (core, 0, other),
        (first_chip, 0, first_rows),
        (second_chip, half, second_rows[:half]),
        (second_chip, 0, second_rows[half:]),
        (second_chip ^ core, 0, swap(first_rows, "dp", core, "rows_core_first")),
        (first_chip ^ core, half, second_other[:half]),
        (first_chip ^ core, 0, second_other[half:]),
        (across, 0, far_rows),
        (across ^ core, 0, swap(far_rows, "dp", core, "rows_core_far")),
    ):
        start = (data_here ^ mask) * row_count
        updated = lax.dynamic_update_slice(updated, values, (block, start, 0))
    return updated, first_new[None, None, None], second_new[None, None, None]


def gathered(partials, params, left_basis, right_basis, first_moment, second_moment, owner_list):
    highest = lax.Precision.HIGHEST
    shard_here = lax.axis_index("shard")
    data_here = lax.axis_index("dp")
    shard_count = lax.axis_size("shard")
    data_count = lax.axis_size("dp")
    device_total = shard_count * data_count
    home_count, row_count, width = params.shape
    block_total = owner_list.shape[0]
    bit_count = data_count.bit_length() - 1
    high_low = list(range(bit_count))[::-1]
    middle = home_count // 2

    grid = partials[0].reshape((home_count,) + (2,) * bit_count + (row_count, width))
    low_first = halve(grid[:middle], high_low, list(range(bit_count)), data_here)
    high_first = halve(
        grid[middle:], high_low, [0] + list(range(1, bit_count))[::-1], data_here
    )
    summed = jnp.concatenate([low_first, high_first], axis=0)

    piece = row_count * width // shard_count
    cut = summed.reshape(home_count, shard_count, piece).swapaxes(0, 1)
    pieces = lax.all_to_all(cut, "shard", split_axis=0, concat_axis=0, tiled=True).reshape(
        block_total, piece
    )
    device_ids = jnp.arange(device_total, dtype=jnp.int32)
    picker = (owner_list[None, :] == device_ids[:, None]).astype(jnp.float32)
    leaving = jnp.einsum("eb,bn->en", picker, pieces, precision=highest)
    whole = lax.all_to_all(
        leaving, ("dp", "shard"), split_axis=0, concat_axis=0, tiled=True
    ).reshape(width, width)

    left_mat = left_basis[0, 0, 0]
    right_mat = right_basis[0, 0, 0]
    first_old = first_moment[0, 0, 0]
    second_old = second_moment[0, 0, 0]
    first_new, second_new, change = adam(
        left_mat, right_mat, first_old, second_old, whole, highest
    )

    coming = lax.all_to_all(
        change.reshape(device_total, piece), ("dp", "shard"), split_axis=0, concat_axis=0, tiled=True
    )
    back = jnp.einsum("eb,en->bn", picker, coming, precision=highest)
    returned = lax.all_to_all(
        back.reshape(shard_count, home_count, piece), "shard", split_axis=0, concat_axis=0, tiled=True
    )
    returned = returned.swapaxes(0, 1).reshape(home_count, row_count, width)
    new_home = params - learn_rate * (returned + decay_rate * params)
    updated = jnp.concatenate(
        [
            spread(new_home[:middle], high_low, data_here),
            spread(new_home[middle:], list(range(1, bit_count)) + [0], data_here),
        ],
        axis=0,
    ).reshape(home_count, width, width)

    my_id = data_here * shard_count + shard_here
    live = jnp.any(owner_list == my_id)
    first_keep = jnp.where(live, first_new, first_old)
    second_keep = jnp.where(live, second_new, second_old)
    return (updated, first_keep[None, None, None], second_keep[None, None, None])


def local(partials, params, left_basis, right_basis, first_moment, second_moment, owner_list):
    shard_count, data_count = lax.axis_size("shard"), lax.axis_size("dp")
    plain = (data_count, shard_count) != (8, 4) or params.shape[1] % (8 * shard_count) != 0
    plain = plain or owner_list.shape[0] != shard_count * data_count or params.shape[0] % 2 != 0
    form = gathered if plain else routed
    return form(
        partials, params, left_basis, right_basis, first_moment, second_moment, owner_list
    )


def solution(mesh):
    return jax.shard_map(
        local,
        mesh=mesh,
        in_specs=(
            P("dp", "shard", None, None),
            P("shard", "dp", None),
            P("dp", "shard", None, None, None),
            P("dp", "shard", None, None, None),
            P("dp", "shard", None, None, None),
            P("dp", "shard", None, None, None),
            P(),
        ),
        out_specs=(
            P("shard", None, None),
            P("dp", "shard", None, None, None),
            P("dp", "shard", None, None, None),
        ),
        check_vma=False,
    )
```

```python
import jax
import jax.numpy as jnp
from jax import lax
from jax.sharding import PartitionSpec as P

beta_one = 0.9
beta_two = 0.95
epsilon = 1e-08
learn_rate = 0.2
decay_rate = 0.1
step_count = 10


def swap(values, name, mask, what="swap"):
    masks = mask if isinstance(mask, tuple) else (mask, mask)
    pairs = [(i, i ^ masks[i & 1]) for i in range(lax.axis_size(name))]
    with jax.named_scope(what):
        return lax.ppermute(values, name, pairs)


def take(values, axis, index):
    return lax.dynamic_index_in_dim(values, index, axis, keepdims=False)


def halve(values, axes, bits, me):
    for bit in bits:
        axis = 1 + axes.index(bit)
        mine = (me >> bit) & 1
        away = take(values, axis, 1 - mine).astype(jnp.float32)
        here = take(values, axis, mine).astype(jnp.float32)
        values = here + swap(away, "dp", 1 << bit)
        axes = [a for a in axes if a != bit]
    return values


def spread(values, bits, me):
    axes = []
    for bit in bits:
        mine = (me >> bit) & 1
        other = swap(values, "dp", 1 << bit)
        low = jnp.where(mine == 0, values, other)
        high = jnp.where(mine == 0, other, values)
        place = sum(1 for a in axes if a > bit)
        values = jnp.stack([low, high], axis=1 + place)
        axes = sorted(axes + [bit], reverse=True)
    return values


def unmix(values, index, axis=0):
    count = values.shape[axis]
    lead, tail = values.shape[:axis], values.shape[axis + 1 :]
    bits = count.bit_length() - 1
    values = values.reshape(lead + (2,) * bits + tail)
    for place in range(bits):
        bit = bits - 1 - place
        flipped = jnp.flip(values, axis + place)
        values = jnp.where((index >> bit) & 1 == 1, flipped, values)
    return values.reshape(lead + (count,) + tail)


def adam(left_mat, right_mat, first_old, second_old, whole, precision):
    partway = jnp.einsum("ia,ij->aj", left_mat, whole, precision=precision)
    rotated = jnp.einsum("aj,jb->ab", partway, right_mat, precision=precision)
    first_new = beta_one * first_old + (1.0 - beta_one) * rotated
    second_new = beta_two * second_old + (1.0 - beta_two) * rotated * rotated
    correct_one = 1.0 - beta_one**step_count
    correct_two = 1.0 - beta_two**step_count
    scaled = first_new / correct_one / (jnp.sqrt(second_new / correct_two) + epsilon)
    back_rot = jnp.einsum("ab,jb->aj", scaled, right_mat, precision=precision)
    change = jnp.einsum("ia,aj->ij", left_mat, back_rot, precision=precision)
    return first_new, second_new, change


def shard_exchange(parts):
    arrived = {k: swap(parts[k], "shard", k, f"shard_{k}") for k in (2, 3, 1)}
    return [parts[0]] + [arrived[k] for k in (1, 2, 3)]


def routed(partials, params, left_basis, right_basis, first_moment, second_moment, owner_list):
    high = lax.Precision.HIGH
    core, across = 1, 6
    first_link, second_link = (2, 4), (4, 2)
    near_order = (0, 1, 3, 2)
    shard_here = lax.axis_index("shard")
    data_here = lax.axis_index("dp")
    shard_count = lax.axis_size("shard")
    data_count = lax.axis_size("dp")
    device_total = shard_count * data_count
    home_count, row_count, width = params.shape
    piece = (row_count // shard_count, width)
    chips = data_count // 2
    my_core = data_here & core
    first_chip = jnp.where(my_core == 0, *first_link)
    second_chip = across - first_chip
    shard_half, shard_low = shard_here >> 1, shard_here & 1

    def set_of(values, index):
        split = values.reshape((home_count, 2, values.shape[1] // 2, width))
        return take(split, 1, index)

    grid = partials[0].reshape((home_count, chips, 2, row_count, width))
    away_rows = take(grid, 2, 1 - my_core)
    own_rows = take(grid, 2, my_core)
    away_rows, own_rows = lax.optimization_barrier((away_rows, own_rows))

    def rows_of(values, mask):
        return take(values, 1, (data_here ^ mask) // 2).astype(jnp.float32)

    near, far = {}, {}
    for name, mask, other_mask in (
        ("across", across, across),
        ("first", first_chip, second_chip),
        ("second", second_chip, first_chip),
        ("own", 0, 0),
    ):
        total = rows_of(own_rows, mask) + swap(
            rows_of(away_rows, other_mask), "dp", core, f"sum_core_{name}"
        )
        near[name], far[name] = lax.optimization_barrier(
            (set_of(total, shard_half), set_of(total, 1 - shard_half))
        )
        if name == "across":
            own_rows, near[name], far[name] = lax.optimization_barrier(
                (own_rows, near[name], far[name])
            )

    def sends(rows, what):
        relay = rows["second"] + swap(rows["across"], "dp", first_link, f"sum_across_{what}")
        direct = swap(rows["first"], "dp", first_link, f"sum_first_{what}")
        return direct, swap(relay, "dp", second_link, f"sum_relay_{what}")

    direct, relayed = sends(far, "far")
    far_sum = lax.optimization_barrier(far["own"] + direct) + relayed
    direct, relayed = sends(near, "near")
    near_sum = lax.optimization_barrier(near["own"] + relayed) + direct
    near_sum, owner_list = lax.optimization_barrier((near_sum, owner_list))

    mixed = shard_exchange(
        [
            set_of(near_sum, shard_low),
            set_of(near_sum, 1 - shard_low),
            set_of(far_sum, shard_low),
            set_of(far_sum, 1 - shard_low),
        ]
    )
    owners = unmix(owner_list.reshape(shard_count, home_count), shard_here)
    owners = jnp.concatenate([owners[k] for k in near_order])[None, :]
    device_ids = jnp.arange(device_total, dtype=jnp.int32)
    picker = (owners == device_ids[:, None]).astype(jnp.float32)
    pieces = jnp.concatenate([mixed[k] for k in near_order], axis=0).reshape(device_total, -1)
    leaving = jnp.einsum("eb,bn->en", picker, pieces, precision=high)
    whole = lax.all_to_all(
        leaving.reshape((device_total,) + piece),
        ("dp", "shard"),
        split_axis=0,
        concat_axis=0,
        tiled=True,
    ).reshape(width, width)

    first_new, second_new, change = adam(
        left_basis[0, 0, 0],
        right_basis[0, 0, 0],
        first_moment[0, 0, 0],
        second_moment[0, 0, 0],
        whole,
        high,
    )

    coming = lax.all_to_all(
        change.reshape((device_total,) + piece),
        ("dp", "shard"),
        split_axis=0,
        concat_axis=0,
        tiled=True,
    ).reshape(device_total, -1)
    coming, data_here, shard_here, params = lax.optimization_barrier(
        (coming, data_here, shard_here, params)
    )
    first_chip = jnp.where((data_here & core) == 0, *first_link)
    second_chip = across - first_chip
    back = jnp.einsum("eb,en->bn", picker, coming, precision=high)
    back = back.reshape((shard_count, home_count) + piece)
    returned = shard_exchange([back[near_order.index(k)] for k in range(shard_count)])


    def both(first, second, flip):
        return jnp.where(
            flip == 0,
            jnp.concatenate([first, second], axis=1),
            jnp.concatenate([second, first], axis=1),
        )

    def stepped(change_rows, home):
        return home - learn_rate * (change_rows + decay_rate * home)

    near_own = stepped(both(returned[0], returned[1], shard_low), set_of(params, shard_half))
    params, near_own = lax.optimization_barrier((params, near_own))
    near_second = swap(near_own, "dp", second_link, "rows_second_near")
    near_first = swap(near_own, "dp", first_link, "rows_first_near")
    far_own = stepped(both(returned[2], returned[3], shard_low), set_of(params, 1 - shard_half))
    far_second = swap(far_own, "dp", second_link, "rows_second_far")
    far_first = swap(far_own, "dp", first_link, "rows_first_far")
    near_second, near_first, _ = lax.optimization_barrier((near_second, near_first, far_own))
    near_across = swap(near_second, "dp", first_link, "rows_relay_near")
    far_across = swap(far_second, "dp", first_link, "rows_relay_far")
    near_rows = jnp.stack([near_own, near_first, near_second, near_across])
    near_rows, _, first_new, second_new = lax.optimization_barrier(
        (near_rows, far_second, first_new, second_new)
    )
    far_rows = jnp.stack([far_own, far_first, far_second, far_across])

    updated = jnp.zeros((home_count, width, width), jnp.float32)
    for what, place, rows in (
        ("near", shard_half, near_rows),
        ("far", 1 - shard_half, far_rows),
    ):
        other = swap(rows, "dp", core, f"rows_core_{what}")
        for mask, values in (
            (0, rows[0]),
            (first_chip, rows[1]),
            (second_chip, rows[2]),
            (across, rows[3]),
            (core, other[0]),
            (second_chip ^ core, other[1]),
            (first_chip ^ core, other[2]),
            (across ^ core, other[3]),
        ):
            start = ((data_here ^ mask) * 2 + place) * (row_count // 2)
            updated = lax.dynamic_update_slice_in_dim(updated, values, start, axis=1)
    return updated, first_new[None, None, None], second_new[None, None, None]


def gathered(partials, params, left_basis, right_basis, first_moment, second_moment, owner_list):
    highest = lax.Precision.HIGHEST
    shard_here = lax.axis_index("shard")
    data_here = lax.axis_index("dp")
    shard_count = lax.axis_size("shard")
    data_count = lax.axis_size("dp")
    device_total = shard_count * data_count
    home_count, row_count, width = params.shape
    block_total = owner_list.shape[0]
    bit_count = data_count.bit_length() - 1
    high_low = list(range(bit_count))[::-1]
    middle = home_count // 2

    grid = partials[0].reshape((home_count,) + (2,) * bit_count + (row_count, width))
    low_first = halve(grid[:middle], high_low, list(range(bit_count)), data_here)
    high_first = halve(
        grid[middle:], high_low, [0] + list(range(1, bit_count))[::-1], data_here
    )
    summed = jnp.concatenate([low_first, high_first], axis=0)

    piece = row_count * width // shard_count
    cut = summed.reshape(home_count, shard_count, piece).swapaxes(0, 1)
    pieces = lax.all_to_all(cut, "shard", split_axis=0, concat_axis=0, tiled=True).reshape(
        block_total, piece
    )
    device_ids = jnp.arange(device_total, dtype=jnp.int32)
    picker = (owner_list[None, :] == device_ids[:, None]).astype(jnp.float32)
    leaving = jnp.einsum("eb,bn->en", picker, pieces, precision=highest)
    whole = lax.all_to_all(
        leaving, ("dp", "shard"), split_axis=0, concat_axis=0, tiled=True
    ).reshape(width, width)

    left_mat = left_basis[0, 0, 0]
    right_mat = right_basis[0, 0, 0]
    first_old = first_moment[0, 0, 0]
    second_old = second_moment[0, 0, 0]
    first_new, second_new, change = adam(
        left_mat, right_mat, first_old, second_old, whole, highest
    )

    coming = lax.all_to_all(
        change.reshape(device_total, piece), ("dp", "shard"), split_axis=0, concat_axis=0, tiled=True
    )
    back = jnp.einsum("eb,en->bn", picker, coming, precision=highest)
    returned = lax.all_to_all(
        back.reshape(shard_count, home_count, piece), "shard", split_axis=0, concat_axis=0, tiled=True
    )
    returned = returned.swapaxes(0, 1).reshape(home_count, row_count, width)
    new_home = params - learn_rate * (returned + decay_rate * params)
    updated = jnp.concatenate(
        [
            spread(new_home[:middle], high_low, data_here),
            spread(new_home[middle:], list(range(1, bit_count)) + [0], data_here),
        ],
        axis=0,
    ).reshape(home_count, width, width)

    my_id = data_here * shard_count + shard_here
    live = jnp.any(owner_list == my_id)
    first_keep = jnp.where(live, first_new, first_old)
    second_keep = jnp.where(live, second_new, second_old)
    return (updated, first_keep[None, None, None], second_keep[None, None, None])


def local(partials, params, left_basis, right_basis, first_moment, second_moment, owner_list):
    shard_count, data_count = lax.axis_size("shard"), lax.axis_size("dp")
    plain = (data_count, shard_count) != (8, 4) or params.shape[1] % (8 * shard_count) != 0
    plain = plain or owner_list.shape[0] != shard_count * data_count or params.shape[0] % 2 != 0
    form = gathered if plain else routed
    return form(
        partials, params, left_basis, right_basis, first_moment, second_moment, owner_list
    )


def solution(mesh):
    return jax.shard_map(
        local,
        mesh=mesh,
        in_specs=(
            P("dp", "shard", None, None),
            P("shard", "dp", None),
            P("dp", "shard", None, None, None),
            P("dp", "shard", None, None, None),
            P("dp", "shard", None, None, None),
            P("dp", "shard", None, None, None),
            P(),
        ),
        out_specs=(
            P("shard", None, None),
            P("dp", "shard", None, None, None),
            P("dp", "shard", None, None, None),
        ),
        check_vma=False,
    )
```

```python
import jax
import jax.numpy as jnp
from jax import lax
from jax.sharding import PartitionSpec as P

beta_one = 0.9
beta_two = 0.95
epsilon = 1e-08
learn_rate = 0.2
decay_rate = 0.1
step_count = 10


def swap(values, name, mask, what="swap"):
    masks = mask if isinstance(mask, tuple) else (mask, mask)
    pairs = [(i, i ^ masks[i & 1]) for i in range(lax.axis_size(name))]
    with jax.named_scope(what):
        return lax.ppermute(values, name, pairs)


def take(values, axis, index):
    return lax.dynamic_index_in_dim(values, index, axis, keepdims=False)


def halve(values, axes, bits, me):
    for bit in bits:
        axis = 1 + axes.index(bit)
        mine = (me >> bit) & 1
        away = take(values, axis, 1 - mine).astype(jnp.float32)
        here = take(values, axis, mine).astype(jnp.float32)
        values = here + swap(away, "dp", 1 << bit)
        axes = [a for a in axes if a != bit]
    return values


def spread(values, bits, me):
    axes = []
    for bit in bits:
        mine = (me >> bit) & 1
        other = swap(values, "dp", 1 << bit)
        low = jnp.where(mine == 0, values, other)
        high = jnp.where(mine == 0, other, values)
        place = sum(1 for a in axes if a > bit)
        values = jnp.stack([low, high], axis=1 + place)
        axes = sorted(axes + [bit], reverse=True)
    return values


def unmix(values, index, axis=0):
    count = values.shape[axis]
    lead, tail = values.shape[:axis], values.shape[axis + 1 :]
    bits = count.bit_length() - 1
    values = values.reshape(lead + (2,) * bits + tail)
    for place in range(bits):
        bit = bits - 1 - place
        flipped = jnp.flip(values, axis + place)
        values = jnp.where((index >> bit) & 1 == 1, flipped, values)
    return values.reshape(lead + (count,) + tail)


def adam(left_mat, right_mat, first_old, second_old, whole, precision):
    partway = jnp.einsum("ia,ij->aj", left_mat, whole, precision=precision)
    rotated = jnp.einsum("aj,jb->ab", partway, right_mat, precision=precision)
    first_new = beta_one * first_old + (1.0 - beta_one) * rotated
    second_new = beta_two * second_old + (1.0 - beta_two) * rotated * rotated
    correct_one = 1.0 - beta_one**step_count
    correct_two = 1.0 - beta_two**step_count
    scaled = first_new / correct_one / (jnp.sqrt(second_new / correct_two) + epsilon)
    back_rot = jnp.einsum("ab,jb->aj", scaled, right_mat, precision=precision)
    change = jnp.einsum("ia,aj->ij", left_mat, back_rot, precision=precision)
    return first_new, second_new, change


def shard_exchange(parts):
    arrived = {k: swap(parts[k], "shard", k, f"shard_{k}") for k in (2, 3, 1)}
    return [parts[0]] + [arrived[k] for k in (1, 2, 3)]


def routed(partials, params, left_basis, right_basis, first_moment, second_moment, owner_list):
    high = lax.Precision.HIGH
    core, across = 1, 6
    first_link, second_link = (2, 4), (4, 2)
    near_order = (0, 1, 3, 2)
    shard_here = lax.axis_index("shard")
    data_here = lax.axis_index("dp")
    shard_count = lax.axis_size("shard")
    data_count = lax.axis_size("dp")
    device_total = shard_count * data_count
    home_count, row_count, width = params.shape
    piece = (row_count // shard_count, width)
    chips = data_count // 2
    my_core = data_here & core
    first_chip = jnp.where(my_core == 0, *first_link)
    second_chip = across - first_chip
    shard_half, shard_low = shard_here >> 1, shard_here & 1

    def set_of(values, index):
        split = values.reshape((home_count, 2, values.shape[1] // 2, width))
        return take(split, 1, index)

    grid = partials[0].reshape((home_count, chips, 2, row_count, width))
    away_rows = take(grid, 2, 1 - my_core)
    own_rows = take(grid, 2, my_core)
    away_rows, own_rows = lax.optimization_barrier((away_rows, own_rows))

    def rows_of(values, mask):
        return take(values, 1, (data_here ^ mask) // 2).astype(jnp.float32)

    near, far = {}, {}
    for name, mask, other_mask in (
        ("across", across, across),
        ("first", first_chip, second_chip),
        ("second", second_chip, first_chip),
        ("own", 0, 0),
    ):
        total = rows_of(own_rows, mask) + swap(
            rows_of(away_rows, other_mask), "dp", core, f"sum_core_{name}"
        )
        near[name], far[name] = lax.optimization_barrier(
            (set_of(total, shard_half), set_of(total, 1 - shard_half))
        )
        if name == "across":
            own_rows, near[name], far[name] = lax.optimization_barrier(
                (own_rows, near[name], far[name])
            )

    def sends(rows, what):
        relay = rows["second"] + swap(rows["across"], "dp", first_link, f"sum_across_{what}")
        direct = swap(rows["first"], "dp", first_link, f"sum_first_{what}")
        return direct, swap(relay, "dp", second_link, f"sum_relay_{what}")

    direct, relayed = sends(far, "far")
    far_sum = lax.optimization_barrier(far["own"] + direct) + relayed
    direct, relayed = sends(near, "near")
    near_sum = lax.optimization_barrier(near["own"] + relayed) + direct
    near_sum, owner_list = lax.optimization_barrier((near_sum, owner_list))

    mixed = shard_exchange(
        [
            set_of(near_sum, shard_low),
            set_of(near_sum, 1 - shard_low),
            set_of(far_sum, shard_low),
            set_of(far_sum, 1 - shard_low),
        ]
    )
    owners = unmix(owner_list.reshape(shard_count, home_count), shard_here)
    owners = jnp.concatenate([owners[k] for k in near_order])[None, :]
    device_ids = jnp.arange(device_total, dtype=jnp.int32)
    picker = (owners == device_ids[:, None]).astype(jnp.float32)
    pieces = jnp.concatenate([mixed[k] for k in near_order], axis=0).reshape(device_total, -1)
    leaving = jnp.einsum("eb,bn->en", picker, pieces, precision=high)
    whole = lax.all_to_all(
        leaving.reshape((device_total,) + piece),
        ("dp", "shard"),
        split_axis=0,
        concat_axis=0,
        tiled=True,
    ).reshape(width, width)

    first_new, second_new, change = adam(
        left_basis[0, 0, 0],
        right_basis[0, 0, 0],
        first_moment[0, 0, 0],
        second_moment[0, 0, 0],
        whole,
        high,
    )

    coming = lax.all_to_all(
        change.reshape((device_total,) + piece),
        ("dp", "shard"),
        split_axis=0,
        concat_axis=0,
        tiled=True,
    ).reshape(device_total, -1)
    coming, data_here, shard_here, params = lax.optimization_barrier(
        (coming, data_here, shard_here, params)
    )
    first_chip = jnp.where((data_here & core) == 0, *first_link)
    second_chip = across - first_chip
    back = jnp.einsum("eb,en->bn", picker, coming, precision=high)
    back = back.reshape((shard_count, home_count) + piece)
    returned = shard_exchange([back[near_order.index(k)] for k in range(shard_count)])


    def both(first, second, flip):
        return jnp.where(
            flip == 0,
            jnp.concatenate([first, second], axis=1),
            jnp.concatenate([second, first], axis=1),
        )

    def stepped(change_rows, home):
        return home - learn_rate * (change_rows + decay_rate * home)

    near_own = stepped(both(returned[0], returned[1], shard_low), set_of(params, shard_half))
    params, near_own = lax.optimization_barrier((params, near_own))
    near_second = swap(near_own, "dp", second_link, "rows_second_near")
    near_first = swap(near_own, "dp", first_link, "rows_first_near")
    far_own = stepped(both(returned[2], returned[3], shard_low), set_of(params, 1 - shard_half))
    far_second = swap(far_own, "dp", second_link, "rows_second_far")
    far_first = swap(far_own, "dp", first_link, "rows_first_far")
    near_second, near_first, _ = lax.optimization_barrier((near_second, near_first, far_own))
    near_across = swap(near_second, "dp", first_link, "rows_relay_near")
    far_across = swap(far_second, "dp", first_link, "rows_relay_far")
    other = {}
    rows_first = jnp.stack([near_own, near_first, near_second])
    copied = swap(rows_first, "dp", core, "rows_core_first")
    other.update(zip((0, 1, 2), copied))
    rows_second = jnp.stack([near_across, far_own, far_second])
    copied = swap(rows_second, "dp", core, "rows_core_second")
    copied, first_new, second_new = lax.optimization_barrier((copied, first_new, second_new))
    other.update(zip((3, 4, 6), copied))
    rows_last = jnp.stack([far_first, far_across])
    copied = swap(rows_last, "dp", core, "rows_core_last")
    other.update(zip((5, 7), copied))

    rows = [near_own, near_first, near_second, near_across, far_own, far_first, far_second, far_across]
    masks = (0, first_chip, second_chip, across)
    other_masks = (core, second_chip ^ core, first_chip ^ core, across ^ core)
    updated = jnp.zeros((home_count, width, width), jnp.float32)
    for part in (0, 1, 2, 3, 4, 6, 5, 7):
        place = shard_half if part < 4 else 1 - shard_half
        for mask, values in ((masks[part % 4], rows[part]), (other_masks[part % 4], other[part])):
            start = ((data_here ^ mask) * 2 + place) * (row_count // 2)
            updated = lax.dynamic_update_slice_in_dim(updated, values, start, axis=1)
    return updated, first_new[None, None, None], second_new[None, None, None]


def gathered(partials, params, left_basis, right_basis, first_moment, second_moment, owner_list):
    highest = lax.Precision.HIGHEST
    shard_here = lax.axis_index("shard")
    data_here = lax.axis_index("dp")
    shard_count = lax.axis_size("shard")
    data_count = lax.axis_size("dp")
    device_total = shard_count * data_count
    home_count, row_count, width = params.shape
    block_total = owner_list.shape[0]
    bit_count = data_count.bit_length() - 1
    high_low = list(range(bit_count))[::-1]
    middle = home_count // 2

    grid = partials[0].reshape((home_count,) + (2,) * bit_count + (row_count, width))
    low_first = halve(grid[:middle], high_low, list(range(bit_count)), data_here)
    high_first = halve(
        grid[middle:], high_low, [0] + list(range(1, bit_count))[::-1], data_here
    )
    summed = jnp.concatenate([low_first, high_first], axis=0)

    piece = row_count * width // shard_count
    cut = summed.reshape(home_count, shard_count, piece).swapaxes(0, 1)
    pieces = lax.all_to_all(cut, "shard", split_axis=0, concat_axis=0, tiled=True).reshape(
        block_total, piece
    )
    device_ids = jnp.arange(device_total, dtype=jnp.int32)
    picker = (owner_list[None, :] == device_ids[:, None]).astype(jnp.float32)
    leaving = jnp.einsum("eb,bn->en", picker, pieces, precision=highest)
    whole = lax.all_to_all(
        leaving, ("dp", "shard"), split_axis=0, concat_axis=0, tiled=True
    ).reshape(width, width)

    left_mat = left_basis[0, 0, 0]
    right_mat = right_basis[0, 0, 0]
    first_old = first_moment[0, 0, 0]
    second_old = second_moment[0, 0, 0]
    first_new, second_new, change = adam(
        left_mat, right_mat, first_old, second_old, whole, highest
    )

    coming = lax.all_to_all(
        change.reshape(device_total, piece), ("dp", "shard"), split_axis=0, concat_axis=0, tiled=True
    )
    back = jnp.einsum("eb,en->bn", picker, coming, precision=highest)
    returned = lax.all_to_all(
        back.reshape(shard_count, home_count, piece), "shard", split_axis=0, concat_axis=0, tiled=True
    )
    returned = returned.swapaxes(0, 1).reshape(home_count, row_count, width)
    new_home = params - learn_rate * (returned + decay_rate * params)
    updated = jnp.concatenate(
        [
            spread(new_home[:middle], high_low, data_here),
            spread(new_home[middle:], list(range(1, bit_count)) + [0], data_here),
        ],
        axis=0,
    ).reshape(home_count, width, width)

    my_id = data_here * shard_count + shard_here
    live = jnp.any(owner_list == my_id)
    first_keep = jnp.where(live, first_new, first_old)
    second_keep = jnp.where(live, second_new, second_old)
    return (updated, first_keep[None, None, None], second_keep[None, None, None])


def local(partials, params, left_basis, right_basis, first_moment, second_moment, owner_list):
    shard_count, data_count = lax.axis_size("shard"), lax.axis_size("dp")
    plain = (data_count, shard_count) != (8, 4) or params.shape[1] % (8 * shard_count) != 0
    plain = plain or owner_list.shape[0] != shard_count * data_count or params.shape[0] % 2 != 0
    form = gathered if plain else routed
    return form(
        partials, params, left_basis, right_basis, first_moment, second_moment, owner_list
    )


def solution(mesh):
    return jax.shard_map(
        local,
        mesh=mesh,
        in_specs=(
            P("dp", "shard", None, None),
            P("shard", "dp", None),
            P("dp", "shard", None, None, None),
            P("dp", "shard", None, None, None),
            P("dp", "shard", None, None, None),
            P("dp", "shard", None, None, None),
            P(),
        ),
        out_specs=(
            P("shard", None, None),
            P("dp", "shard", None, None, None),
            P("dp", "shard", None, None, None),
        ),
        check_vma=False,
    )
```

```python
import jax
import jax.numpy as jnp
from jax import lax
from jax.sharding import PartitionSpec as P

beta_one = 0.9
beta_two = 0.95
epsilon = 1e-08
learn_rate = 0.2
decay_rate = 0.1
step_count = 10


def swap(values, name, mask, what="swap"):
    masks = mask if isinstance(mask, tuple) else (mask, mask)
    pairs = [(i, i ^ masks[i & 1]) for i in range(lax.axis_size(name))]
    with jax.named_scope(what):
        return lax.ppermute(values, name, pairs)


def take(values, axis, index):
    return lax.dynamic_index_in_dim(values, index, axis, keepdims=False)


def halve(values, axes, bits, me):
    for bit in bits:
        axis = 1 + axes.index(bit)
        mine = (me >> bit) & 1
        away = take(values, axis, 1 - mine).astype(jnp.float32)
        here = take(values, axis, mine).astype(jnp.float32)
        values = here + swap(away, "dp", 1 << bit)
        axes = [a for a in axes if a != bit]
    return values


def spread(values, bits, me):
    axes = []
    for bit in bits:
        mine = (me >> bit) & 1
        other = swap(values, "dp", 1 << bit)
        low = jnp.where(mine == 0, values, other)
        high = jnp.where(mine == 0, other, values)
        place = sum(1 for a in axes if a > bit)
        values = jnp.stack([low, high], axis=1 + place)
        axes = sorted(axes + [bit], reverse=True)
    return values


def unmix(values, index, axis=0):
    count = values.shape[axis]
    lead, tail = values.shape[:axis], values.shape[axis + 1 :]
    bits = count.bit_length() - 1
    values = values.reshape(lead + (2,) * bits + tail)
    for place in range(bits):
        bit = bits - 1 - place
        flipped = jnp.flip(values, axis + place)
        values = jnp.where((index >> bit) & 1 == 1, flipped, values)
    return values.reshape(lead + (count,) + tail)


def adam(left_mat, right_mat, first_old, second_old, whole, precision):
    partway = jnp.einsum("ia,ij->aj", left_mat, whole, precision=precision)
    rotated = jnp.einsum("aj,jb->ab", partway, right_mat, precision=precision)
    first_new = beta_one * first_old + (1.0 - beta_one) * rotated
    second_new = beta_two * second_old + (1.0 - beta_two) * rotated * rotated
    correct_one = 1.0 - beta_one**step_count
    correct_two = 1.0 - beta_two**step_count
    scaled = first_new / correct_one / (jnp.sqrt(second_new / correct_two) + epsilon)
    back_rot = jnp.einsum("ab,jb->aj", scaled, right_mat, precision=precision)
    change = jnp.einsum("ia,aj->ij", left_mat, back_rot, precision=precision)
    return first_new, second_new, change


def shard_exchange(parts):
    arrived = {k: swap(parts[k], "shard", k, f"shard_{k}") for k in (2, 3, 1)}
    return [parts[0]] + [arrived[k] for k in (1, 2, 3)]


def routed(partials, params, left_basis, right_basis, first_moment, second_moment, owner_list):
    high = lax.Precision.HIGH
    core, across = 1, 6
    first_link, second_link = (2, 4), (4, 2)
    near_order = (0, 1, 3, 2)
    shard_here = lax.axis_index("shard")
    data_here = lax.axis_index("dp")
    shard_count = lax.axis_size("shard")
    data_count = lax.axis_size("dp")
    device_total = shard_count * data_count
    home_count, row_count, width = params.shape
    piece = (row_count // shard_count, width)
    chips = data_count // 2
    my_core = data_here & core
    first_chip = jnp.where(my_core == 0, *first_link)
    second_chip = across - first_chip
    shard_half, shard_low = shard_here >> 1, shard_here & 1

    def set_of(values, index):
        split = values.reshape((home_count, 2, values.shape[1] // 2, width))
        return take(split, 1, index)

    grid = partials[0].reshape((home_count, chips, 2, row_count, width))
    away_rows = take(grid, 2, 1 - my_core)
    own_rows = take(grid, 2, my_core)
    away_rows, own_rows = lax.optimization_barrier((away_rows, own_rows))

    def rows_of(values, mask):
        return take(values, 1, (data_here ^ mask) // 2).astype(jnp.float32)

    near, far = {}, {}
    for name, mask, other_mask in (
        ("across", across, across),
        ("first", first_chip, second_chip),
        ("second", second_chip, first_chip),
        ("own", 0, 0),
    ):
        total = rows_of(own_rows, mask) + swap(
            rows_of(away_rows, other_mask), "dp", core, f"sum_core_{name}"
        )
        near[name], far[name] = lax.optimization_barrier(
            (set_of(total, shard_half), set_of(total, 1 - shard_half))
        )
        if name == "across":
            own_rows, near[name], far[name] = lax.optimization_barrier(
                (own_rows, near[name], far[name])
            )

    def sends(rows, what):
        relay = rows["second"] + swap(rows["across"], "dp", first_link, f"sum_across_{what}")
        direct = swap(rows["first"], "dp", first_link, f"sum_first_{what}")
        return direct, swap(relay, "dp", second_link, f"sum_relay_{what}")

    direct, relayed = sends(far, "far")
    far_sum = lax.optimization_barrier(far["own"] + direct) + relayed
    direct, relayed = sends(near, "near")
    near_sum = lax.optimization_barrier(near["own"] + relayed) + direct
    near_sum, owner_list = lax.optimization_barrier((near_sum, owner_list))

    mixed = shard_exchange(
        [
            set_of(near_sum, shard_low),
            set_of(near_sum, 1 - shard_low),
            set_of(far_sum, shard_low),
            set_of(far_sum, 1 - shard_low),
        ]
    )
    owners = unmix(owner_list.reshape(shard_count, home_count), shard_here)
    owners = jnp.concatenate([owners[k] for k in near_order])[None, :]
    device_ids = jnp.arange(device_total, dtype=jnp.int32)
    picker = (owners == device_ids[:, None]).astype(jnp.float32)
    pieces = jnp.concatenate([mixed[k] for k in near_order], axis=0).reshape(device_total, -1)
    leaving = jnp.einsum("eb,bn->en", picker, pieces, precision=high)
    whole = lax.all_to_all(
        leaving.reshape((device_total,) + piece),
        ("dp", "shard"),
        split_axis=0,
        concat_axis=0,
        tiled=True,
    ).reshape(width, width)

    first_new, second_new, change = adam(
        left_basis[0, 0, 0],
        right_basis[0, 0, 0],
        first_moment[0, 0, 0],
        second_moment[0, 0, 0],
        whole,
        high,
    )

    coming = lax.all_to_all(
        change.reshape((device_total,) + piece),
        ("dp", "shard"),
        split_axis=0,
        concat_axis=0,
        tiled=True,
    ).reshape(device_total, -1)
    coming, data_here, shard_here, params = lax.optimization_barrier(
        (coming, data_here, shard_here, params)
    )
    first_chip = jnp.where((data_here & core) == 0, *first_link)
    second_chip = across - first_chip
    back = jnp.einsum("eb,en->bn", picker, coming, precision=high)
    back = back.reshape((shard_count, home_count) + piece)
    returned = shard_exchange([back[near_order.index(k)] for k in range(shard_count)])


    def both(first, second, flip):
        return jnp.where(
            flip == 0,
            jnp.concatenate([first, second], axis=1),
            jnp.concatenate([second, first], axis=1),
        )

    def stepped(change_rows, home):
        return home - learn_rate * (change_rows + decay_rate * home)

    near_own = stepped(both(returned[0], returned[1], shard_low), set_of(params, shard_half))
    params, near_own = lax.optimization_barrier((params, near_own))
    near_second = swap(near_own, "dp", second_link, "rows_second_near")
    near_first = swap(near_own, "dp", first_link, "rows_first_near")
    far_own = stepped(both(returned[2], returned[3], shard_low), set_of(params, 1 - shard_half))
    far_second = swap(far_own, "dp", second_link, "rows_second_far")
    near_second, near_first, _ = lax.optimization_barrier((near_second, near_first, far_own))
    near_across = swap(near_second, "dp", first_link, "rows_relay_near")
    far_across = swap(far_second, "dp", first_link, "rows_relay_far")
    far_last, _ = lax.optimization_barrier((far_own, near_across))
    far_first = swap(far_last, "dp", first_link, "rows_first_far")
    other = {}
    rows_first = jnp.stack([near_own, near_first, near_second])
    copied = swap(rows_first, "dp", core, "rows_core_first")
    other.update(zip((0, 1, 2), copied))
    rows_second = jnp.stack([near_across, far_own, far_second])
    copied = swap(rows_second, "dp", core, "rows_core_second")
    copied, first_new, second_new = lax.optimization_barrier((copied, first_new, second_new))
    other.update(zip((3, 4, 6), copied))
    rows_last = jnp.stack([far_first, far_across])
    copied = swap(rows_last, "dp", core, "rows_core_last")
    other.update(zip((5, 7), copied))

    rows = [near_own, near_first, near_second, near_across, far_own, far_first, far_second, far_across]
    masks = (0, first_chip, second_chip, across)
    other_masks = (core, second_chip ^ core, first_chip ^ core, across ^ core)
    updated = jnp.zeros((home_count, width, width), jnp.float32)
    for part in (0, 1, 2, 3, 4, 6, 5, 7):
        place = shard_half if part < 4 else 1 - shard_half
        for mask, values in ((masks[part % 4], rows[part]), (other_masks[part % 4], other[part])):
            start = ((data_here ^ mask) * 2 + place) * (row_count // 2)
            updated = lax.dynamic_update_slice_in_dim(updated, values, start, axis=1)
    return updated, first_new[None, None, None], second_new[None, None, None]


def gathered(partials, params, left_basis, right_basis, first_moment, second_moment, owner_list):
    highest = lax.Precision.HIGHEST
    shard_here = lax.axis_index("shard")
    data_here = lax.axis_index("dp")
    shard_count = lax.axis_size("shard")
    data_count = lax.axis_size("dp")
    device_total = shard_count * data_count
    home_count, row_count, width = params.shape
    block_total = owner_list.shape[0]
    bit_count = data_count.bit_length() - 1
    high_low = list(range(bit_count))[::-1]
    middle = home_count // 2

    grid = partials[0].reshape((home_count,) + (2,) * bit_count + (row_count, width))
    low_first = halve(grid[:middle], high_low, list(range(bit_count)), data_here)
    high_first = halve(
        grid[middle:], high_low, [0] + list(range(1, bit_count))[::-1], data_here
    )
    summed = jnp.concatenate([low_first, high_first], axis=0)

    piece = row_count * width // shard_count
    cut = summed.reshape(home_count, shard_count, piece).swapaxes(0, 1)
    pieces = lax.all_to_all(cut, "shard", split_axis=0, concat_axis=0, tiled=True).reshape(
        block_total, piece
    )
    device_ids = jnp.arange(device_total, dtype=jnp.int32)
    picker = (owner_list[None, :] == device_ids[:, None]).astype(jnp.float32)
    leaving = jnp.einsum("eb,bn->en", picker, pieces, precision=highest)
    whole = lax.all_to_all(
        leaving, ("dp", "shard"), split_axis=0, concat_axis=0, tiled=True
    ).reshape(width, width)

    left_mat = left_basis[0, 0, 0]
    right_mat = right_basis[0, 0, 0]
    first_old = first_moment[0, 0, 0]
    second_old = second_moment[0, 0, 0]
    first_new, second_new, change = adam(
        left_mat, right_mat, first_old, second_old, whole, highest
    )

    coming = lax.all_to_all(
        change.reshape(device_total, piece), ("dp", "shard"), split_axis=0, concat_axis=0, tiled=True
    )
    back = jnp.einsum("eb,en->bn", picker, coming, precision=highest)
    returned = lax.all_to_all(
        back.reshape(shard_count, home_count, piece), "shard", split_axis=0, concat_axis=0, tiled=True
    )
    returned = returned.swapaxes(0, 1).reshape(home_count, row_count, width)
    new_home = params - learn_rate * (returned + decay_rate * params)
    updated = jnp.concatenate(
        [
            spread(new_home[:middle], high_low, data_here),
            spread(new_home[middle:], list(range(1, bit_count)) + [0], data_here),
        ],
        axis=0,
    ).reshape(home_count, width, width)

    my_id = data_here * shard_count + shard_here
    live = jnp.any(owner_list == my_id)
    first_keep = jnp.where(live, first_new, first_old)
    second_keep = jnp.where(live, second_new, second_old)
    return (updated, first_keep[None, None, None], second_keep[None, None, None])


def local(partials, params, left_basis, right_basis, first_moment, second_moment, owner_list):
    shard_count, data_count = lax.axis_size("shard"), lax.axis_size("dp")
    plain = (data_count, shard_count) != (8, 4) or params.shape[1] % (8 * shard_count) != 0
    plain = plain or owner_list.shape[0] != shard_count * data_count or params.shape[0] % 2 != 0
    form = gathered if plain else routed
    return form(
        partials, params, left_basis, right_basis, first_moment, second_moment, owner_list
    )


def solution(mesh):
    return jax.shard_map(
        local,
        mesh=mesh,
        in_specs=(
            P("dp", "shard", None, None),
            P("shard", "dp", None),
            P("dp", "shard", None, None, None),
            P("dp", "shard", None, None, None),
            P("dp", "shard", None, None, None),
            P("dp", "shard", None, None, None),
            P(),
        ),
        out_specs=(
            P("shard", None, None),
            P("dp", "shard", None, None, None),
            P("dp", "shard", None, None, None),
        ),
        check_vma=False,
    )
```

```python
import jax
import jax.numpy as jnp
from jax import lax
from jax.sharding import PartitionSpec as P

beta_one = 0.9
beta_two = 0.95
epsilon = 1e-08
learn_rate = 0.2
decay_rate = 0.1
step_count = 10


def swap(values, name, mask, what="swap"):
    masks = mask if isinstance(mask, tuple) else (mask, mask)
    pairs = [(i, i ^ masks[i & 1]) for i in range(lax.axis_size(name))]
    with jax.named_scope(what):
        return lax.ppermute(values, name, pairs)


def take(values, axis, index):
    return lax.dynamic_index_in_dim(values, index, axis, keepdims=False)


def halve(values, axes, bits, me):
    for bit in bits:
        axis = 1 + axes.index(bit)
        mine = (me >> bit) & 1
        away = take(values, axis, 1 - mine).astype(jnp.float32)
        here = take(values, axis, mine).astype(jnp.float32)
        values = here + swap(away, "dp", 1 << bit)
        axes = [a for a in axes if a != bit]
    return values


def spread(values, bits, me):
    axes = []
    for bit in bits:
        mine = (me >> bit) & 1
        other = swap(values, "dp", 1 << bit)
        low = jnp.where(mine == 0, values, other)
        high = jnp.where(mine == 0, other, values)
        place = sum(1 for a in axes if a > bit)
        values = jnp.stack([low, high], axis=1 + place)
        axes = sorted(axes + [bit], reverse=True)
    return values


def unmix(values, index, axis=0):
    count = values.shape[axis]
    lead, tail = values.shape[:axis], values.shape[axis + 1 :]
    bits = count.bit_length() - 1
    values = values.reshape(lead + (2,) * bits + tail)
    for place in range(bits):
        bit = bits - 1 - place
        flipped = jnp.flip(values, axis + place)
        values = jnp.where((index >> bit) & 1 == 1, flipped, values)
    return values.reshape(lead + (count,) + tail)


def adam(left_mat, right_mat, first_old, second_old, whole, precision):
    partway = jnp.einsum("ia,ij->aj", left_mat, whole, precision=precision)
    rotated = jnp.einsum("aj,jb->ab", partway, right_mat, precision=precision)
    first_new = beta_one * first_old + (1.0 - beta_one) * rotated
    second_new = beta_two * second_old + (1.0 - beta_two) * rotated * rotated
    correct_one = 1.0 - beta_one**step_count
    correct_two = 1.0 - beta_two**step_count
    scaled = first_new / correct_one / (jnp.sqrt(second_new / correct_two) + epsilon)
    back_rot = jnp.einsum("ab,jb->aj", scaled, right_mat, precision=precision)
    change = jnp.einsum("ia,aj->ij", left_mat, back_rot, precision=precision)
    return first_new, second_new, change


def shard_exchange(parts):
    arrived = {k: swap(parts[k], "shard", k, f"shard_{k}") for k in (2, 3, 1)}
    return [parts[0]] + [arrived[k] for k in (1, 2, 3)]


def routed(partials, params, left_basis, right_basis, first_moment, second_moment, owner_list):
    high = lax.Precision.HIGH
    core, across = 1, 6
    first_link, second_link = (2, 4), (4, 2)
    near_order = (0, 1, 3, 2)
    shard_here = lax.axis_index("shard")
    data_here = lax.axis_index("dp")
    shard_count = lax.axis_size("shard")
    data_count = lax.axis_size("dp")
    device_total = shard_count * data_count
    home_count, row_count, width = params.shape
    half = home_count // 2
    piece = (row_count // shard_count, width)
    chips = data_count // 2
    my_core = data_here & core
    first_chip = jnp.where(my_core == 0, *first_link)
    second_chip = across - first_chip
    shard_half, shard_low = shard_here >> 1, shard_here & 1

    def set_of(values, index):
        split = values.reshape((home_count, 2, values.shape[1] // 2, width))
        return take(split, 1, index)

    grid = partials[0].reshape((home_count, chips, 2, row_count, width))
    away_rows = take(grid, 2, 1 - my_core)
    own_rows = take(grid, 2, my_core)
    away_rows, own_rows = lax.optimization_barrier((away_rows, own_rows))

    def rows_of(values, mask):
        return take(values, 1, (data_here ^ mask) // 2).astype(jnp.float32)

    near, far = {}, {}
    for name, mask, other_mask in (
        ("across", across, across),
        ("first", first_chip, second_chip),
        ("second", second_chip, first_chip),
        ("own", 0, 0),
    ):
        total = rows_of(own_rows, mask) + swap(
            rows_of(away_rows, other_mask), "dp", core, f"sum_core_{name}"
        )
        near[name], far[name] = lax.optimization_barrier(
            (set_of(total, shard_half), set_of(total, 1 - shard_half))
        )
        if name == "across":
            own_rows, near[name], far[name] = lax.optimization_barrier(
                (own_rows, near[name], far[name])
            )

    def sends(rows, what):
        relay = rows["second"] + swap(rows["across"], "dp", first_link, f"sum_across_{what}")
        direct = swap(rows["first"], "dp", first_link, f"sum_first_{what}")
        return direct, swap(relay, "dp", second_link, f"sum_relay_{what}")

    direct, relayed = sends(far, "far")
    far_sum = lax.optimization_barrier(far["own"] + direct) + relayed
    direct, relayed = sends(near, "near")
    near_sum = lax.optimization_barrier(near["own"] + relayed) + direct
    near_sum, owner_list = lax.optimization_barrier((near_sum, owner_list))

    mixed = shard_exchange(
        [
            set_of(near_sum, shard_low),
            set_of(near_sum, 1 - shard_low),
            set_of(far_sum, shard_low),
            set_of(far_sum, 1 - shard_low),
        ]
    )
    owners = unmix(owner_list.reshape(shard_count, home_count), shard_here)
    owners = jnp.concatenate([owners[k] for k in near_order])[None, :]
    device_ids = jnp.arange(device_total, dtype=jnp.int32)
    picker = (owners == device_ids[:, None]).astype(jnp.float32)
    pieces = jnp.concatenate([mixed[k] for k in near_order], axis=0).reshape(device_total, -1)
    leaving = jnp.einsum("eb,bn->en", picker, pieces, precision=high)
    whole = lax.all_to_all(
        leaving.reshape((device_total,) + piece),
        ("dp", "shard"),
        split_axis=0,
        concat_axis=0,
        tiled=True,
    ).reshape(width, width)

    first_new, second_new, change = adam(
        left_basis[0, 0, 0],
        right_basis[0, 0, 0],
        first_moment[0, 0, 0],
        second_moment[0, 0, 0],
        whole,
        high,
    )

    coming = lax.all_to_all(
        change.reshape((device_total,) + piece),
        ("dp", "shard"),
        split_axis=0,
        concat_axis=0,
        tiled=True,
    ).reshape(device_total, -1)
    coming, data_here, shard_here, params = lax.optimization_barrier(
        (coming, data_here, shard_here, params)
    )
    first_chip = jnp.where((data_here & core) == 0, *first_link)
    second_chip = across - first_chip
    back = jnp.einsum("eb,en->bn", picker, coming, precision=high)
    back = back.reshape((shard_count, home_count) + piece)
    returned = shard_exchange([back[near_order.index(k)] for k in range(shard_count)])

    new_home = params
    for k in (0, 3, 2, 1):
        start = (shard_here ^ k) * piece[0]
        home = lax.dynamic_slice_in_dim(params, start, piece[0], axis=1)
        home = home - learn_rate * (returned[k] + decay_rate * home)
        new_home = lax.dynamic_update_slice_in_dim(new_home, home, start, axis=1)

    low, top = new_home[:half], new_home[half:]
    first_top = swap(top, "dp", first_link, "rows_first_top")
    second_low = swap(low, "dp", second_link, "rows_second_low")
    first_low = swap(low, "dp", first_link, "rows_first_low")
    second_top = swap(top, "dp", second_link, "rows_second_top")
    far_top = swap(first_top, "dp", second_link, "rows_relay_top")
    far_low = swap(second_low, "dp", first_link, "rows_relay_low")
    own_home, _ = lax.optimization_barrier((new_home, first_top))
    other = swap(own_home, "dp", core, "rows_core_own")
    first_rows = jnp.concatenate([first_low, first_top], axis=0)
    second_rows = jnp.concatenate([second_top, second_low], axis=0)
    first_rows, second_rows, far_top, first_new, second_new = lax.optimization_barrier(
        (first_rows, second_rows, far_top, first_new, second_new)
    )
    far_rows = jnp.concatenate([far_low, far_top], axis=0)
    second_other = swap(second_rows, "dp", core, "rows_core_second")
    updated = jnp.zeros((home_count, width, width), jnp.float32)
    for mask, block, values in (
        (0, 0, new_home),
        (core, 0, other),
        (first_chip, 0, first_rows),
        (second_chip, half, second_rows[:half]),
        (second_chip, 0, second_rows[half:]),
        (second_chip ^ core, 0, swap(first_rows, "dp", core, "rows_core_first")),
        (first_chip ^ core, half, second_other[:half]),
        (first_chip ^ core, 0, second_other[half:]),
        (across, 0, far_rows),
        (across ^ core, 0, swap(far_rows, "dp", core, "rows_core_far")),
    ):
        start = (data_here ^ mask) * row_count
        updated = lax.dynamic_update_slice(updated, values, (block, start, 0))
    return updated, first_new[None, None, None], second_new[None, None, None]


def gathered(partials, params, left_basis, right_basis, first_moment, second_moment, owner_list):
    highest = lax.Precision.HIGHEST
    shard_here = lax.axis_index("shard")
    data_here = lax.axis_index("dp")
    shard_count = lax.axis_size("shard")
    data_count = lax.axis_size("dp")
    device_total = shard_count * data_count
    home_count, row_count, width = params.shape
    block_total = owner_list.shape[0]
    bit_count = data_count.bit_length() - 1
    high_low = list(range(bit_count))[::-1]
    middle = home_count // 2

    grid = partials[0].reshape((home_count,) + (2,) * bit_count + (row_count, width))
    low_first = halve(grid[:middle], high_low, list(range(bit_count)), data_here)
    high_first = halve(
        grid[middle:], high_low, [0] + list(range(1, bit_count))[::-1], data_here
    )
    summed = jnp.concatenate([low_first, high_first], axis=0)

    piece = row_count * width // shard_count
    cut = summed.reshape(home_count, shard_count, piece).swapaxes(0, 1)
    pieces = lax.all_to_all(cut, "shard", split_axis=0, concat_axis=0, tiled=True).reshape(
        block_total, piece
    )
    device_ids = jnp.arange(device_total, dtype=jnp.int32)
    picker = (owner_list[None, :] == device_ids[:, None]).astype(jnp.float32)
    leaving = jnp.einsum("eb,bn->en", picker, pieces, precision=highest)
    whole = lax.all_to_all(
        leaving, ("dp", "shard"), split_axis=0, concat_axis=0, tiled=True
    ).reshape(width, width)

    left_mat = left_basis[0, 0, 0]
    right_mat = right_basis[0, 0, 0]
    first_old = first_moment[0, 0, 0]
    second_old = second_moment[0, 0, 0]
    first_new, second_new, change = adam(
        left_mat, right_mat, first_old, second_old, whole, highest
    )

    coming = lax.all_to_all(
        change.reshape(device_total, piece), ("dp", "shard"), split_axis=0, concat_axis=0, tiled=True
    )
    back = jnp.einsum("eb,en->bn", picker, coming, precision=highest)
    returned = lax.all_to_all(
        back.reshape(shard_count, home_count, piece), "shard", split_axis=0, concat_axis=0, tiled=True
    )
    returned = returned.swapaxes(0, 1).reshape(home_count, row_count, width)
    new_home = params - learn_rate * (returned + decay_rate * params)
    updated = jnp.concatenate(
        [
            spread(new_home[:middle], high_low, data_here),
            spread(new_home[middle:], list(range(1, bit_count)) + [0], data_here),
        ],
        axis=0,
    ).reshape(home_count, width, width)

    my_id = data_here * shard_count + shard_here
    live = jnp.any(owner_list == my_id)
    first_keep = jnp.where(live, first_new, first_old)
    second_keep = jnp.where(live, second_new, second_old)
    return (updated, first_keep[None, None, None], second_keep[None, None, None])


def local(partials, params, left_basis, right_basis, first_moment, second_moment, owner_list):
    shard_count, data_count = lax.axis_size("shard"), lax.axis_size("dp")
    plain = (data_count, shard_count) != (8, 4) or params.shape[1] % (8 * shard_count) != 0
    plain = plain or owner_list.shape[0] != shard_count * data_count or params.shape[0] % 2 != 0
    form = gathered if plain else routed
    return form(
        partials, params, left_basis, right_basis, first_moment, second_moment, owner_list
    )


def solution(mesh):
    return jax.shard_map(
        local,
        mesh=mesh,
        in_specs=(
            P("dp", "shard", None, None),
            P("shard", "dp", None),
            P("dp", "shard", None, None, None),
            P("dp", "shard", None, None, None),
            P("dp", "shard", None, None, None),
            P("dp", "shard", None, None, None),
            P(),
        ),
        out_specs=(
            P("shard", None, None),
            P("dp", "shard", None, None, None),
            P("dp", "shard", None, None, None),
        ),
        check_vma=False,
    )
```

```python
import jax
import jax.numpy as jnp
from jax import lax
from jax.sharding import PartitionSpec as P

beta_one = 0.9
beta_two = 0.95
epsilon = 1e-08
learn_rate = 0.2
decay_rate = 0.1
step_count = 10


def swap(values, name, mask, what="swap"):
    masks = mask if isinstance(mask, tuple) else (mask, mask)
    pairs = [(i, i ^ masks[i & 1]) for i in range(lax.axis_size(name))]
    with jax.named_scope(what):
        return lax.ppermute(values, name, pairs)


def take(values, axis, index):
    return lax.dynamic_index_in_dim(values, index, axis, keepdims=False)


def halve(values, axes, bits, me):
    for bit in bits:
        axis = 1 + axes.index(bit)
        mine = (me >> bit) & 1
        away = take(values, axis, 1 - mine).astype(jnp.float32)
        here = take(values, axis, mine).astype(jnp.float32)
        values = here + swap(away, "dp", 1 << bit)
        axes = [a for a in axes if a != bit]
    return values


def spread(values, bits, me):
    axes = []
    for bit in bits:
        mine = (me >> bit) & 1
        other = swap(values, "dp", 1 << bit)
        low = jnp.where(mine == 0, values, other)
        high = jnp.where(mine == 0, other, values)
        place = sum(1 for a in axes if a > bit)
        values = jnp.stack([low, high], axis=1 + place)
        axes = sorted(axes + [bit], reverse=True)
    return values


def unmix(values, index, axis=0):
    count = values.shape[axis]
    lead, tail = values.shape[:axis], values.shape[axis + 1 :]
    bits = count.bit_length() - 1
    values = values.reshape(lead + (2,) * bits + tail)
    for place in range(bits):
        bit = bits - 1 - place
        flipped = jnp.flip(values, axis + place)
        values = jnp.where((index >> bit) & 1 == 1, flipped, values)
    return values.reshape(lead + (count,) + tail)


def adam(left_mat, right_mat, first_old, second_old, whole, precision):
    partway = jnp.einsum("ia,ij->aj", left_mat, whole, precision=precision)
    rotated = jnp.einsum("aj,jb->ab", partway, right_mat, precision=precision)
    first_new = beta_one * first_old + (1.0 - beta_one) * rotated
    second_new = beta_two * second_old + (1.0 - beta_two) * rotated * rotated
    correct_one = 1.0 - beta_one**step_count
    correct_two = 1.0 - beta_two**step_count
    scaled = first_new / correct_one / (jnp.sqrt(second_new / correct_two) + epsilon)
    back_rot = jnp.einsum("ab,jb->aj", scaled, right_mat, precision=precision)
    change = jnp.einsum("ia,aj->ij", left_mat, back_rot, precision=precision)
    return first_new, second_new, change


def shard_exchange(parts):
    arrived = {k: swap(parts[k], "shard", k, f"shard_{k}") for k in (2, 3, 1)}
    return [parts[0]] + [arrived[k] for k in (1, 2, 3)]


def routed(partials, params, left_basis, right_basis, first_moment, second_moment, owner_list):
    high = lax.Precision.HIGH
    core, across = 1, 6
    first_link, second_link = (4, 2), (2, 4)
    near_order = (0, 1, 3, 2)
    shard_here = lax.axis_index("shard")
    data_here = lax.axis_index("dp")
    shard_count = lax.axis_size("shard")
    data_count = lax.axis_size("dp")
    device_total = shard_count * data_count
    home_count, row_count, width = params.shape
    half = home_count // 2
    piece = (row_count // shard_count, width)
    chips = data_count // 2
    my_core = data_here & core
    first_chip = jnp.where(my_core == 0, *first_link)
    second_chip = across - first_chip
    shard_half, shard_low = shard_here >> 1, shard_here & 1

    def set_of(values, index):
        split = values.reshape((home_count, 2, values.shape[1] // 2, width))
        return take(split, 1, index)

    grid = partials[0].reshape((home_count, chips, 2, row_count, width))
    away_rows = take(grid, 2, 1 - my_core)
    own_rows = take(grid, 2, my_core)
    away_rows, own_rows = lax.optimization_barrier((away_rows, own_rows))

    def rows_of(values, mask):
        return take(values, 1, (data_here ^ mask) // 2).astype(jnp.float32)

    near, far = {}, {}
    for name, mask, other_mask in (
        ("across", across, across),
        ("first", first_chip, second_chip),
        ("second", second_chip, first_chip),
        ("own", 0, 0),
    ):
        total = rows_of(own_rows, mask) + swap(
            rows_of(away_rows, other_mask), "dp", core, f"sum_core_{name}"
        )
        near[name], far[name] = lax.optimization_barrier(
            (set_of(total, shard_half), set_of(total, 1 - shard_half))
        )
        if name == "across":
            own_rows, near[name], far[name] = lax.optimization_barrier(
                (own_rows, near[name], far[name])
            )

    def sends(rows, what):
        relay = rows["second"] + swap(rows["across"], "dp", first_link, f"sum_across_{what}")
        direct = swap(rows["first"], "dp", first_link, f"sum_first_{what}")
        return direct, swap(relay, "dp", second_link, f"sum_relay_{what}")

    direct, relayed = sends(far, "far")
    far_sum = lax.optimization_barrier(far["own"] + direct) + relayed
    direct, relayed = sends(near, "near")
    near_sum = lax.optimization_barrier(near["own"] + relayed) + direct
    near_sum, owner_list = lax.optimization_barrier((near_sum, owner_list))

    mixed = shard_exchange(
        [
            set_of(near_sum, shard_low),
            set_of(near_sum, 1 - shard_low),
            set_of(far_sum, shard_low),
            set_of(far_sum, 1 - shard_low),
        ]
    )
    owners = unmix(owner_list.reshape(shard_count, home_count), shard_here)
    owners = jnp.concatenate([owners[k] for k in near_order])[None, :]
    device_ids = jnp.arange(device_total, dtype=jnp.int32)
    picker = (owners == device_ids[:, None]).astype(jnp.float32)
    pieces = jnp.concatenate([mixed[k] for k in near_order], axis=0).reshape(device_total, -1)
    leaving = jnp.einsum("eb,bn->en", picker, pieces, precision=high)
    whole = lax.all_to_all(
        leaving.reshape((device_total,) + piece),
        ("dp", "shard"),
        split_axis=0,
        concat_axis=0,
        tiled=True,
    ).reshape(width, width)

    first_new, second_new, change = adam(
        left_basis[0, 0, 0],
        right_basis[0, 0, 0],
        first_moment[0, 0, 0],
        second_moment[0, 0, 0],
        whole,
        high,
    )

    coming = lax.all_to_all(
        change.reshape((device_total,) + piece),
        ("dp", "shard"),
        split_axis=0,
        concat_axis=0,
        tiled=True,
    ).reshape(device_total, -1)
    coming, data_here, shard_here, params = lax.optimization_barrier(
        (coming, data_here, shard_here, params)
    )
    first_chip = jnp.where((data_here & core) == 0, *first_link)
    second_chip = across - first_chip
    back = jnp.einsum("eb,en->bn", picker, coming, precision=high)
    back = back.reshape((shard_count, home_count) + piece)
    returned = shard_exchange([back[near_order.index(k)] for k in range(shard_count)])

    new_home = params
    for k in (0, 3, 2, 1):
        start = (shard_here ^ k) * piece[0]
        home = lax.dynamic_slice_in_dim(params, start, piece[0], axis=1)
        home = home - learn_rate * (returned[k] + decay_rate * home)
        new_home = lax.dynamic_update_slice_in_dim(new_home, home, start, axis=1)

    low, top = new_home[:half], new_home[half:]
    first_top = swap(top, "dp", first_link, "rows_first_top")
    second_low = swap(low, "dp", second_link, "rows_second_low")
    other = swap(new_home, "dp", core, "rows_core_own")
    first_low = swap(low, "dp", first_link, "rows_first_low")
    second_top = swap(top, "dp", second_link, "rows_second_top")
    far_top = swap(first_top, "dp", second_link, "rows_relay_top")
    far_low = swap(second_low, "dp", first_link, "rows_relay_low")
    first_rows = jnp.concatenate([first_low, first_top], axis=0)
    second_rows = jnp.concatenate([second_top, second_low], axis=0)
    first_rows, second_rows, far_top, first_new, second_new = lax.optimization_barrier(
        (first_rows, second_rows, far_top, first_new, second_new)
    )
    far_rows = jnp.concatenate([far_low, far_top], axis=0)
    second_other = swap(second_rows, "dp", core, "rows_core_second")
    updated = jnp.zeros((home_count, width, width), jnp.float32)
    for mask, block, values in (
        (0, 0, new_home),
        (core, 0, other),
        (first_chip, 0, first_rows),
        (second_chip, half, second_rows[:half]),
        (second_chip, 0, second_rows[half:]),
        (second_chip ^ core, 0, swap(first_rows, "dp", core, "rows_core_first")),
        (first_chip ^ core, half, second_other[:half]),
        (first_chip ^ core, 0, second_other[half:]),
        (across, 0, far_rows),
        (across ^ core, 0, swap(far_rows, "dp", core, "rows_core_far")),
    ):
        start = (data_here ^ mask) * row_count
        updated = lax.dynamic_update_slice(updated, values, (block, start, 0))
    return updated, first_new[None, None, None], second_new[None, None, None]


def gathered(partials, params, left_basis, right_basis, first_moment, second_moment, owner_list):
    highest = lax.Precision.HIGHEST
    shard_here = lax.axis_index("shard")
    data_here = lax.axis_index("dp")
    shard_count = lax.axis_size("shard")
    data_count = lax.axis_size("dp")
    device_total = shard_count * data_count
    home_count, row_count, width = params.shape
    block_total = owner_list.shape[0]
    bit_count = data_count.bit_length() - 1
    high_low = list(range(bit_count))[::-1]
    middle = home_count // 2

    grid = partials[0].reshape((home_count,) + (2,) * bit_count + (row_count, width))
    low_first = halve(grid[:middle], high_low, list(range(bit_count)), data_here)
    high_first = halve(
        grid[middle:], high_low, [0] + list(range(1, bit_count))[::-1], data_here
    )
    summed = jnp.concatenate([low_first, high_first], axis=0)

    piece = row_count * width // shard_count
    cut = summed.reshape(home_count, shard_count, piece).swapaxes(0, 1)
    pieces = lax.all_to_all(cut, "shard", split_axis=0, concat_axis=0, tiled=True).reshape(
        block_total, piece
    )
    device_ids = jnp.arange(device_total, dtype=jnp.int32)
    picker = (owner_list[None, :] == device_ids[:, None]).astype(jnp.float32)
    leaving = jnp.einsum("eb,bn->en", picker, pieces, precision=highest)
    whole = lax.all_to_all(
        leaving, ("dp", "shard"), split_axis=0, concat_axis=0, tiled=True
    ).reshape(width, width)

    left_mat = left_basis[0, 0, 0]
    right_mat = right_basis[0, 0, 0]
    first_old = first_moment[0, 0, 0]
    second_old = second_moment[0, 0, 0]
    first_new, second_new, change = adam(
        left_mat, right_mat, first_old, second_old, whole, highest
    )

    coming = lax.all_to_all(
        change.reshape(device_total, piece), ("dp", "shard"), split_axis=0, concat_axis=0, tiled=True
    )
    back = jnp.einsum("eb,en->bn", picker, coming, precision=highest)
    returned = lax.all_to_all(
        back.reshape(shard_count, home_count, piece), "shard", split_axis=0, concat_axis=0, tiled=True
    )
    returned = returned.swapaxes(0, 1).reshape(home_count, row_count, width)
    new_home = params - learn_rate * (returned + decay_rate * params)
    updated = jnp.concatenate(
        [
            spread(new_home[:middle], high_low, data_here),
            spread(new_home[middle:], list(range(1, bit_count)) + [0], data_here),
        ],
        axis=0,
    ).reshape(home_count, width, width)

    my_id = data_here * shard_count + shard_here
    live = jnp.any(owner_list == my_id)
    first_keep = jnp.where(live, first_new, first_old)
    second_keep = jnp.where(live, second_new, second_old)
    return (updated, first_keep[None, None, None], second_keep[None, None, None])


def local(partials, params, left_basis, right_basis, first_moment, second_moment, owner_list):
    shard_count, data_count = lax.axis_size("shard"), lax.axis_size("dp")
    plain = (data_count, shard_count) != (8, 4) or params.shape[1] % (8 * shard_count) != 0
    plain = plain or owner_list.shape[0] != shard_count * data_count or params.shape[0] % 2 != 0
    form = gathered if plain else routed
    return form(
        partials, params, left_basis, right_basis, first_moment, second_moment, owner_list
    )


def solution(mesh):
    return jax.shard_map(
        local,
        mesh=mesh,
        in_specs=(
            P("dp", "shard", None, None),
            P("shard", "dp", None),
            P("dp", "shard", None, None, None),
            P("dp", "shard", None, None, None),
            P("dp", "shard", None, None, None),
            P("dp", "shard", None, None, None),
            P(),
        ),
        out_specs=(
            P("shard", None, None),
            P("dp", "shard", None, None, None),
            P("dp", "shard", None, None, None),
        ),
        check_vma=False,
    )
```

```python
import jax
import jax.numpy as jnp
from jax import lax
from jax.sharding import PartitionSpec as P

beta_one = 0.9
beta_two = 0.95
epsilon = 1e-08
learn_rate = 0.2
decay_rate = 0.1
step_count = 10


def swap(values, name, mask, what="swap"):
    masks = mask if isinstance(mask, tuple) else (mask, mask)
    pairs = [(i, i ^ masks[i & 1]) for i in range(lax.axis_size(name))]
    with jax.named_scope(what):
        return lax.ppermute(values, name, pairs)


def take(values, axis, index):
    return lax.dynamic_index_in_dim(values, index, axis, keepdims=False)


def halve(values, axes, bits, me):
    for bit in bits:
        axis = 1 + axes.index(bit)
        mine = (me >> bit) & 1
        away = take(values, axis, 1 - mine).astype(jnp.float32)
        here = take(values, axis, mine).astype(jnp.float32)
        values = here + swap(away, "dp", 1 << bit)
        axes = [a for a in axes if a != bit]
    return values


def spread(values, bits, me):
    axes = []
    for bit in bits:
        mine = (me >> bit) & 1
        other = swap(values, "dp", 1 << bit)
        low = jnp.where(mine == 0, values, other)
        high = jnp.where(mine == 0, other, values)
        place = sum(1 for a in axes if a > bit)
        values = jnp.stack([low, high], axis=1 + place)
        axes = sorted(axes + [bit], reverse=True)
    return values


def unmix(values, index, axis=0):
    count = values.shape[axis]
    lead, tail = values.shape[:axis], values.shape[axis + 1 :]
    bits = count.bit_length() - 1
    values = values.reshape(lead + (2,) * bits + tail)
    for place in range(bits):
        bit = bits - 1 - place
        flipped = jnp.flip(values, axis + place)
        values = jnp.where((index >> bit) & 1 == 1, flipped, values)
    return values.reshape(lead + (count,) + tail)


def adam(left_mat, right_mat, first_old, second_old, whole, precision):
    partway = jnp.einsum("ia,ij->aj", left_mat, whole, precision=precision)
    rotated = jnp.einsum("aj,jb->ab", partway, right_mat, precision=precision)
    first_new = beta_one * first_old + (1.0 - beta_one) * rotated
    second_new = beta_two * second_old + (1.0 - beta_two) * rotated * rotated
    correct_one = 1.0 - beta_one**step_count
    correct_two = 1.0 - beta_two**step_count
    scaled = first_new / correct_one / (jnp.sqrt(second_new / correct_two) + epsilon)
    back_rot = jnp.einsum("ab,jb->aj", scaled, right_mat, precision=precision)
    change = jnp.einsum("ia,aj->ij", left_mat, back_rot, precision=precision)
    return first_new, second_new, change


def shard_exchange(parts):
    arrived = {k: swap(parts[k], "shard", k, f"shard_{k}") for k in (2, 3, 1)}
    return [parts[0]] + [arrived[k] for k in (1, 2, 3)]


def routed(partials, params, left_basis, right_basis, first_moment, second_moment, owner_list):
    high = lax.Precision.HIGH
    core, across = 1, 6
    first_link, second_link = (2, 4), (4, 2)
    near_order = (0, 1, 2, 3)
    shard_here = lax.axis_index("shard")
    data_here = lax.axis_index("dp")
    shard_count = lax.axis_size("shard")
    data_count = lax.axis_size("dp")
    device_total = shard_count * data_count
    home_count, row_count, width = params.shape
    half = home_count // 2
    piece = (row_count // shard_count, width)
    chips = data_count // 2
    my_core = data_here & core
    first_chip = jnp.where(my_core == 0, *first_link)
    second_chip = across - first_chip
    shard_half, shard_low = shard_here >> 1, shard_here & 1

    def set_of(values, index):
        split = values.reshape((home_count, 2, values.shape[1] // 2, width))
        return take(split, 1, index)

    grid = partials[0].reshape((home_count, chips, 2, row_count, width))
    away_rows = take(grid, 2, 1 - my_core)
    own_rows = take(grid, 2, my_core)
    away_rows, own_rows = lax.optimization_barrier((away_rows, own_rows))

    def rows_of(values, mask):
        return take(values, 1, (data_here ^ mask) // 2).astype(jnp.float32)

    near, far = {}, {}
    for name, mask, other_mask in (
        ("across", across, across),
        ("first", first_chip, second_chip),
        ("second", second_chip, first_chip),
        ("own", 0, 0),
    ):
        total = rows_of(own_rows, mask) + swap(
            rows_of(away_rows, other_mask), "dp", core, f"sum_core_{name}"
        )
        near[name], far[name] = lax.optimization_barrier(
            (set_of(total, shard_half), set_of(total, 1 - shard_half))
        )
        if name == "across":
            own_rows, near[name], far[name] = lax.optimization_barrier(
                (own_rows, near[name], far[name])
            )

    def sends(rows, what):
        relay = rows["second"] + swap(rows["across"], "dp", first_link, f"sum_across_{what}")
        direct = swap(rows["first"], "dp", first_link, f"sum_first_{what}")
        return direct, swap(relay, "dp", second_link, f"sum_relay_{what}")

    direct, relayed = sends(far, "far")
    far_sum = lax.optimization_barrier(far["own"] + direct) + relayed
    direct, relayed = sends(near, "near")
    near_sum = lax.optimization_barrier(near["own"] + relayed) + direct
    near_sum, owner_list = lax.optimization_barrier((near_sum, owner_list))

    mixed = shard_exchange(
        [
            set_of(near_sum, shard_low),
            set_of(near_sum, 1 - shard_low),
            set_of(far_sum, shard_low),
            set_of(far_sum, 1 - shard_low),
        ]
    )
    owners = unmix(owner_list.reshape(shard_count, home_count), shard_here)
    owners = jnp.concatenate([owners[k] for k in near_order])[None, :]
    device_ids = jnp.arange(device_total, dtype=jnp.int32)
    picker = (owners == device_ids[:, None]).astype(jnp.float32)
    pieces = jnp.concatenate([mixed[k] for k in near_order], axis=0).reshape(device_total, -1)
    leaving = jnp.einsum("eb,bn->en", picker, pieces, precision=high)
    whole = lax.all_to_all(
        leaving.reshape((device_total,) + piece),
        ("dp", "shard"),
        split_axis=0,
        concat_axis=0,
        tiled=True,
    ).reshape(width, width)

    first_new, second_new, change = adam(
        left_basis[0, 0, 0],
        right_basis[0, 0, 0],
        first_moment[0, 0, 0],
        second_moment[0, 0, 0],
        whole,
        high,
    )

    coming = lax.all_to_all(
        change.reshape((device_total,) + piece),
        ("dp", "shard"),
        split_axis=0,
        concat_axis=0,
        tiled=True,
    ).reshape(device_total, -1)
    coming, data_here, shard_here, params = lax.optimization_barrier(
        (coming, data_here, shard_here, params)
    )
    first_chip = jnp.where((data_here & core) == 0, *first_link)
    second_chip = across - first_chip
    back = jnp.einsum("eb,en->bn", picker, coming, precision=high)
    back = back.reshape((shard_count, home_count) + piece)
    returned = shard_exchange([back[near_order.index(k)] for k in range(shard_count)])

    new_home = params
    for k in (0, 3, 2, 1):
        start = (shard_here ^ k) * piece[0]
        home = lax.dynamic_slice_in_dim(params, start, piece[0], axis=1)
        home = home - learn_rate * (returned[k] + decay_rate * home)
        new_home = lax.dynamic_update_slice_in_dim(new_home, home, start, axis=1)

    low, top = new_home[:half], new_home[half:]
    first_top = swap(top, "dp", first_link, "rows_first_top")
    second_low = swap(low, "dp", second_link, "rows_second_low")
    other = swap(new_home, "dp", core, "rows_core_own")
    first_low = swap(low, "dp", first_link, "rows_first_low")
    second_top = swap(top, "dp", second_link, "rows_second_top")
    far_top = swap(first_top, "dp", second_link, "rows_relay_top")
    far_low = swap(second_low, "dp", first_link, "rows_relay_low")
    first_rows = jnp.concatenate([first_low, first_top], axis=0)
    second_rows = jnp.concatenate([second_top, second_low], axis=0)
    first_rows, second_rows, far_top, first_new, second_new = lax.optimization_barrier(
        (first_rows, second_rows, far_top, first_new, second_new)
    )
    far_rows = jnp.concatenate([far_low, far_top], axis=0)
    second_other = swap(second_rows, "dp", core, "rows_core_second")
    updated = jnp.zeros((home_count, width, width), jnp.float32)
    for mask, block, values in (
        (0, 0, new_home),
        (core, 0, other),
        (first_chip, 0, first_rows),
        (second_chip, half, second_rows[:half]),
        (second_chip, 0, second_rows[half:]),
        (second_chip ^ core, 0, swap(first_rows, "dp", core, "rows_core_first")),
        (first_chip ^ core, half, second_other[:half]),
        (first_chip ^ core, 0, second_other[half:]),
        (across, 0, far_rows),
        (across ^ core, 0, swap(far_rows, "dp", core, "rows_core_far")),
    ):
        start = (data_here ^ mask) * row_count
        updated = lax.dynamic_update_slice(updated, values, (block, start, 0))
    return updated, first_new[None, None, None], second_new[None, None, None]


def gathered(partials, params, left_basis, right_basis, first_moment, second_moment, owner_list):
    highest = lax.Precision.HIGHEST
    shard_here = lax.axis_index("shard")
    data_here = lax.axis_index("dp")
    shard_count = lax.axis_size("shard")
    data_count = lax.axis_size("dp")
    device_total = shard_count * data_count
    home_count, row_count, width = params.shape
    block_total = owner_list.shape[0]
    bit_count = data_count.bit_length() - 1
    high_low = list(range(bit_count))[::-1]
    middle = home_count // 2

    grid = partials[0].reshape((home_count,) + (2,) * bit_count + (row_count, width))
    low_first = halve(grid[:middle], high_low, list(range(bit_count)), data_here)
    high_first = halve(
        grid[middle:], high_low, [0] + list(range(1, bit_count))[::-1], data_here
    )
    summed = jnp.concatenate([low_first, high_first], axis=0)

    piece = row_count * width // shard_count
    cut = summed.reshape(home_count, shard_count, piece).swapaxes(0, 1)
    pieces = lax.all_to_all(cut, "shard", split_axis=0, concat_axis=0, tiled=True).reshape(
        block_total, piece
    )
    device_ids = jnp.arange(device_total, dtype=jnp.int32)
    picker = (owner_list[None, :] == device_ids[:, None]).astype(jnp.float32)
    leaving = jnp.einsum("eb,bn->en", picker, pieces, precision=highest)
    whole = lax.all_to_all(
        leaving, ("dp", "shard"), split_axis=0, concat_axis=0, tiled=True
    ).reshape(width, width)

    left_mat = left_basis[0, 0, 0]
    right_mat = right_basis[0, 0, 0]
    first_old = first_moment[0, 0, 0]
    second_old = second_moment[0, 0, 0]
    first_new, second_new, change = adam(
        left_mat, right_mat, first_old, second_old, whole, highest
    )

    coming = lax.all_to_all(
        change.reshape(device_total, piece), ("dp", "shard"), split_axis=0, concat_axis=0, tiled=True
    )
    back = jnp.einsum("eb,en->bn", picker, coming, precision=highest)
    returned = lax.all_to_all(
        back.reshape(shard_count, home_count, piece), "shard", split_axis=0, concat_axis=0, tiled=True
    )
    returned = returned.swapaxes(0, 1).reshape(home_count, row_count, width)
    new_home = params - learn_rate * (returned + decay_rate * params)
    updated = jnp.concatenate(
        [
            spread(new_home[:middle], high_low, data_here),
            spread(new_home[middle:], list(range(1, bit_count)) + [0], data_here),
        ],
        axis=0,
    ).reshape(home_count, width, width)

    my_id = data_here * shard_count + shard_here
    live = jnp.any(owner_list == my_id)
    first_keep = jnp.where(live, first_new, first_old)
    second_keep = jnp.where(live, second_new, second_old)
    return (updated, first_keep[None, None, None], second_keep[None, None, None])


def local(partials, params, left_basis, right_basis, first_moment, second_moment, owner_list):
    shard_count, data_count = lax.axis_size("shard"), lax.axis_size("dp")
    plain = (data_count, shard_count) != (8, 4) or params.shape[1] % (8 * shard_count) != 0
    plain = plain or owner_list.shape[0] != shard_count * data_count or params.shape[0] % 2 != 0
    form = gathered if plain else routed
    return form(
        partials, params, left_basis, right_basis, first_moment, second_moment, owner_list
    )


def solution(mesh):
    return jax.shard_map(
        local,
        mesh=mesh,
        in_specs=(
            P("dp", "shard", None, None),
            P("shard", "dp", None),
            P("dp", "shard", None, None, None),
            P("dp", "shard", None, None, None),
            P("dp", "shard", None, None, None),
            P("dp", "shard", None, None, None),
            P(),
        ),
        out_specs=(
            P("shard", None, None),
            P("dp", "shard", None, None, None),
            P("dp", "shard", None, None, None),
        ),
        check_vma=False,
    )
```

```python
import jax
import jax.numpy as jnp
from jax import lax
from jax.sharding import PartitionSpec as P

beta_one = 0.9
beta_two = 0.95
epsilon = 1e-08
learn_rate = 0.2
decay_rate = 0.1
step_count = 10


def swap(values, name, mask, what="swap"):
    masks = mask if isinstance(mask, tuple) else (mask, mask)
    pairs = [(i, i ^ masks[i & 1]) for i in range(lax.axis_size(name))]
    with jax.named_scope(what):
        return lax.ppermute(values, name, pairs)


def take(values, axis, index):
    return lax.dynamic_index_in_dim(values, index, axis, keepdims=False)


def halve(values, axes, bits, me):
    for bit in bits:
        axis = 1 + axes.index(bit)
        mine = (me >> bit) & 1
        away = take(values, axis, 1 - mine).astype(jnp.float32)
        here = take(values, axis, mine).astype(jnp.float32)
        values = here + swap(away, "dp", 1 << bit)
        axes = [a for a in axes if a != bit]
    return values


def spread(values, bits, me):
    axes = []
    for bit in bits:
        mine = (me >> bit) & 1
        other = swap(values, "dp", 1 << bit)
        low = jnp.where(mine == 0, values, other)
        high = jnp.where(mine == 0, other, values)
        place = sum(1 for a in axes if a > bit)
        values = jnp.stack([low, high], axis=1 + place)
        axes = sorted(axes + [bit], reverse=True)
    return values


def unmix(values, index, axis=0):
    count = values.shape[axis]
    lead, tail = values.shape[:axis], values.shape[axis + 1 :]
    bits = count.bit_length() - 1
    values = values.reshape(lead + (2,) * bits + tail)
    for place in range(bits):
        bit = bits - 1 - place
        flipped = jnp.flip(values, axis + place)
        values = jnp.where((index >> bit) & 1 == 1, flipped, values)
    return values.reshape(lead + (count,) + tail)


def adam(left_mat, right_mat, first_old, second_old, whole, precision):
    partway = jnp.einsum("ia,ij->aj", left_mat, whole, precision=precision)
    rotated = jnp.einsum("aj,jb->ab", partway, right_mat, precision=precision)
    first_new = beta_one * first_old + (1.0 - beta_one) * rotated
    second_new = beta_two * second_old + (1.0 - beta_two) * rotated * rotated
    correct_one = 1.0 - beta_one**step_count
    correct_two = 1.0 - beta_two**step_count
    scaled = first_new / correct_one / (jnp.sqrt(second_new / correct_two) + epsilon)
    back_rot = jnp.einsum("ab,jb->aj", scaled, right_mat, precision=precision)
    change = jnp.einsum("ia,aj->ij", left_mat, back_rot, precision=precision)
    return first_new, second_new, change


def shard_exchange(parts):
    arrived = {k: swap(parts[k], "shard", k, f"shard_{k}") for k in (2, 3, 1)}
    return [parts[0]] + [arrived[k] for k in (1, 2, 3)]


def routed(partials, params, left_basis, right_basis, first_moment, second_moment, owner_list):
    high = lax.Precision.HIGH
    core, across = 1, 6
    first_link, second_link = (2, 4), (4, 2)
    near_order = (0, 1, 3, 2)
    shard_here = lax.axis_index("shard")
    data_here = lax.axis_index("dp")
    shard_count = lax.axis_size("shard")
    data_count = lax.axis_size("dp")
    device_total = shard_count * data_count
    home_count, row_count, width = params.shape
    half = home_count // 2
    piece = (row_count // shard_count, width)
    chips = data_count // 2
    my_core = data_here & core
    first_chip = jnp.where(my_core == 0, *first_link)
    second_chip = across - first_chip
    shard_half, shard_low = shard_here >> 1, shard_here & 1

    def set_of(values, index):
        split = values.reshape((home_count, 2, values.shape[1] // 2, width))
        return take(split, 1, index)

    grid = partials[0].reshape((home_count, chips, 2, row_count, width))
    away_rows = take(grid, 2, 1 - my_core)
    own_rows = take(grid, 2, my_core)
    away_rows, own_rows = lax.optimization_barrier((away_rows, own_rows))

    def rows_of(values, mask):
        return take(values, 1, (data_here ^ mask) // 2).astype(jnp.float32)

    near, far = {}, {}
    for name, mask, other_mask in (
        ("across", across, across),
        ("first", first_chip, second_chip),
        ("second", second_chip, first_chip),
        ("own", 0, 0),
    ):
        total = rows_of(own_rows, mask) + swap(
            rows_of(away_rows, other_mask), "dp", core, f"sum_core_{name}"
        )
        near[name], far[name] = lax.optimization_barrier(
            (set_of(total, shard_half), set_of(total, 1 - shard_half))
        )
        if name == "across":
            own_rows, near[name], far[name] = lax.optimization_barrier(
                (own_rows, near[name], far[name])
            )

    def sends(rows, what):
        relay = rows["second"] + swap(rows["across"], "dp", first_link, f"sum_across_{what}")
        direct = swap(rows["first"], "dp", first_link, f"sum_first_{what}")
        return direct, swap(relay, "dp", second_link, f"sum_relay_{what}")

    direct, relayed = sends(far, "far")
    far_sum = lax.optimization_barrier(far["own"] + direct) + relayed
    direct, relayed = sends(near, "near")
    near_sum = lax.optimization_barrier(near["own"] + relayed) + direct
    near_sum, owner_list = lax.optimization_barrier((near_sum, owner_list))

    mixed = shard_exchange(
        [
            set_of(near_sum, shard_low),
            set_of(near_sum, 1 - shard_low),
            set_of(far_sum, shard_low),
            set_of(far_sum, 1 - shard_low),
        ]
    )
    owners = unmix(owner_list.reshape(shard_count, home_count), shard_here)
    owners = jnp.concatenate([owners[k] for k in near_order])[None, :]
    device_ids = jnp.arange(device_total, dtype=jnp.int32)
    picker = (owners == device_ids[:, None]).astype(jnp.float32)
    pieces = jnp.concatenate([mixed[k] for k in near_order], axis=0).reshape(device_total, -1)
    leaving = jnp.einsum("eb,bn->en", picker, pieces, precision=high)
    whole = lax.all_to_all(
        leaving.reshape((device_total,) + piece),
        ("dp", "shard"),
        split_axis=0,
        concat_axis=0,
        tiled=True,
    ).reshape(width, width)

    first_new, second_new, change = adam(
        left_basis[0, 0, 0],
        right_basis[0, 0, 0],
        first_moment[0, 0, 0],
        second_moment[0, 0, 0],
        whole,
        high,
    )

    coming = lax.all_to_all(
        change.reshape((device_total,) + piece),
        ("dp", "shard"),
        split_axis=0,
        concat_axis=0,
        tiled=True,
    ).reshape(device_total, -1)
    coming, data_here, shard_here, params = lax.optimization_barrier(
        (coming, data_here, shard_here, params)
    )
    first_chip = jnp.where((data_here & core) == 0, *first_link)
    second_chip = across - first_chip
    back = jnp.einsum("eb,en->bn", picker, coming, precision=high)
    back = back.reshape((shard_count, home_count) + piece)
    returned = shard_exchange([back[near_order.index(k)] for k in range(shard_count)])

    new_home = params
    for k in (0, 3, 2, 1):
        start = (shard_here ^ k) * piece[0]
        home = lax.dynamic_slice_in_dim(params, start, piece[0], axis=1)
        home = home - learn_rate * (returned[k] + decay_rate * home)
        new_home = lax.dynamic_update_slice_in_dim(new_home, home, start, axis=1)

    low, top = new_home[:half], new_home[half:]
    first_top = swap(top, "dp", first_link, "rows_first_top")
    second_low = swap(low, "dp", second_link, "rows_second_low")
    other = swap(new_home, "dp", core, "rows_core_own")
    first_low = swap(low, "dp", first_link, "rows_first_low")
    second_top = swap(top, "dp", second_link, "rows_second_top")
    far_top = swap(first_top, "dp", second_link, "rows_relay_top")
    far_low = swap(second_low, "dp", first_link, "rows_relay_low")

    updated = jnp.zeros((home_count, width, width), jnp.float32)

    def written(values, mask, block, rows):
        start = (data_here ^ mask) * row_count
        return lax.dynamic_update_slice(values, rows, (block, start, 0))

    updated = written(updated, 0, 0, new_home)
    updated = written(updated, core, 0, other)
    for what, mask, block, rows in (
        ("first_top", first_chip, half, first_top),
        ("second_low", second_chip, 0, second_low),
        ("first_low", first_chip, 0, first_low),
        ("second_top", second_chip, half, second_top),
    ):
        twin = swap(rows, "dp", core, f"rows_core_{what}")
        if what == "second_top":
            twin, first_new, second_new = lax.optimization_barrier((twin, first_new, second_new))
        updated = written(updated, mask, block, rows)
        updated = written(updated, (across - mask) ^ core, block, twin)
    far_rows = jnp.concatenate([far_low, far_top], axis=0)
    updated = written(updated, across, 0, far_rows)
    updated = written(updated, across ^ core, 0, swap(far_rows, "dp", core, "rows_core_far"))
    return updated, first_new[None, None, None], second_new[None, None, None]


def gathered(partials, params, left_basis, right_basis, first_moment, second_moment, owner_list):
    highest = lax.Precision.HIGHEST
    shard_here = lax.axis_index("shard")
    data_here = lax.axis_index("dp")
    shard_count = lax.axis_size("shard")
    data_count = lax.axis_size("dp")
    device_total = shard_count * data_count
    home_count, row_count, width = params.shape
    block_total = owner_list.shape[0]
    bit_count = data_count.bit_length() - 1
    high_low = list(range(bit_count))[::-1]
    middle = home_count // 2

    grid = partials[0].reshape((home_count,) + (2,) * bit_count + (row_count, width))
    low_first = halve(grid[:middle], high_low, list(range(bit_count)), data_here)
    high_first = halve(
        grid[middle:], high_low, [0] + list(range(1, bit_count))[::-1], data_here
    )
    summed = jnp.concatenate([low_first, high_first], axis=0)

    piece = row_count * width // shard_count
    cut = summed.reshape(home_count, shard_count, piece).swapaxes(0, 1)
    pieces = lax.all_to_all(cut, "shard", split_axis=0, concat_axis=0, tiled=True).reshape(
        block_total, piece
    )
    device_ids = jnp.arange(device_total, dtype=jnp.int32)
    picker = (owner_list[None, :] == device_ids[:, None]).astype(jnp.float32)
    leaving = jnp.einsum("eb,bn->en", picker, pieces, precision=highest)
    whole = lax.all_to_all(
        leaving, ("dp", "shard"), split_axis=0, concat_axis=0, tiled=True
    ).reshape(width, width)

    left_mat = left_basis[0, 0, 0]
    right_mat = right_basis[0, 0, 0]
    first_old = first_moment[0, 0, 0]
    second_old = second_moment[0, 0, 0]
    first_new, second_new, change = adam(
        left_mat, right_mat, first_old, second_old, whole, highest
    )

    coming = lax.all_to_all(
        change.reshape(device_total, piece), ("dp", "shard"), split_axis=0, concat_axis=0, tiled=True
    )
    back = jnp.einsum("eb,en->bn", picker, coming, precision=highest)
    returned = lax.all_to_all(
        back.reshape(shard_count, home_count, piece), "shard", split_axis=0, concat_axis=0, tiled=True
    )
    returned = returned.swapaxes(0, 1).reshape(home_count, row_count, width)
    new_home = params - learn_rate * (returned + decay_rate * params)
    updated = jnp.concatenate(
        [
            spread(new_home[:middle], high_low, data_here),
            spread(new_home[middle:], list(range(1, bit_count)) + [0], data_here),
        ],
        axis=0,
    ).reshape(home_count, width, width)

    my_id = data_here * shard_count + shard_here
    live = jnp.any(owner_list == my_id)
    first_keep = jnp.where(live, first_new, first_old)
    second_keep = jnp.where(live, second_new, second_old)
    return (updated, first_keep[None, None, None], second_keep[None, None, None])


def local(partials, params, left_basis, right_basis, first_moment, second_moment, owner_list):
    shard_count, data_count = lax.axis_size("shard"), lax.axis_size("dp")
    plain = (data_count, shard_count) != (8, 4) or params.shape[1] % (8 * shard_count) != 0
    plain = plain or owner_list.shape[0] != shard_count * data_count or params.shape[0] % 2 != 0
    form = gathered if plain else routed
    return form(
        partials, params, left_basis, right_basis, first_moment, second_moment, owner_list
    )


def solution(mesh):
    return jax.shard_map(
        local,
        mesh=mesh,
        in_specs=(
            P("dp", "shard", None, None),
            P("shard", "dp", None),
            P("dp", "shard", None, None, None),
            P("dp", "shard", None, None, None),
            P("dp", "shard", None, None, None),
            P("dp", "shard", None, None, None),
            P(),
        ),
        out_specs=(
            P("shard", None, None),
            P("dp", "shard", None, None, None),
            P("dp", "shard", None, None, None),
        ),
        check_vma=False,
    )
```

```python
import jax
import jax.numpy as jnp
from jax import lax
from jax.sharding import PartitionSpec as P

beta_one = 0.9
beta_two = 0.95
epsilon = 1e-08
learn_rate = 0.2
decay_rate = 0.1
step_count = 10


def swap(values, name, mask, what="swap"):
    masks = mask if isinstance(mask, tuple) else (mask, mask)
    pairs = [(i, i ^ masks[i & 1]) for i in range(lax.axis_size(name))]
    with jax.named_scope(what):
        return lax.ppermute(values, name, pairs)


def take(values, axis, index):
    return lax.dynamic_index_in_dim(values, index, axis, keepdims=False)


def halve(values, axes, bits, me):
    for bit in bits:
        axis = 1 + axes.index(bit)
        mine = (me >> bit) & 1
        away = take(values, axis, 1 - mine).astype(jnp.float32)
        here = take(values, axis, mine).astype(jnp.float32)
        values = here + swap(away, "dp", 1 << bit)
        axes = [a for a in axes if a != bit]
    return values


def spread(values, bits, me):
    axes = []
    for bit in bits:
        mine = (me >> bit) & 1
        other = swap(values, "dp", 1 << bit)
        low = jnp.where(mine == 0, values, other)
        high = jnp.where(mine == 0, other, values)
        place = sum(1 for a in axes if a > bit)
        values = jnp.stack([low, high], axis=1 + place)
        axes = sorted(axes + [bit], reverse=True)
    return values


def unmix(values, index, axis=0):
    count = values.shape[axis]
    lead, tail = values.shape[:axis], values.shape[axis + 1 :]
    bits = count.bit_length() - 1
    values = values.reshape(lead + (2,) * bits + tail)
    for place in range(bits):
        bit = bits - 1 - place
        flipped = jnp.flip(values, axis + place)
        values = jnp.where((index >> bit) & 1 == 1, flipped, values)
    return values.reshape(lead + (count,) + tail)


def adam(left_mat, right_mat, first_old, second_old, whole, precision):
    partway = jnp.einsum("ia,ij->aj", left_mat, whole, precision=precision)
    rotated = jnp.einsum("aj,jb->ab", partway, right_mat, precision=precision)
    first_new = beta_one * first_old + (1.0 - beta_one) * rotated
    second_new = beta_two * second_old + (1.0 - beta_two) * rotated * rotated
    correct_one = 1.0 - beta_one**step_count
    correct_two = 1.0 - beta_two**step_count
    scaled = first_new / correct_one / (jnp.sqrt(second_new / correct_two) + epsilon)
    back_rot = jnp.einsum("ab,jb->aj", scaled, right_mat, precision=precision)
    change = jnp.einsum("ia,aj->ij", left_mat, back_rot, precision=precision)
    return first_new, second_new, change


def shard_exchange(parts):
    arrived = {k: swap(parts[k], "shard", k, f"shard_{k}") for k in (2, 3, 1)}
    return [parts[0]] + [arrived[k] for k in (1, 2, 3)]


def routed(partials, params, left_basis, right_basis, first_moment, second_moment, owner_list):
    high = lax.Precision.HIGH
    core, across = 1, 6
    first_link, second_link = (2, 4), (4, 2)
    near_order = (0, 1, 3, 2)
    shard_here = lax.axis_index("shard")
    data_here = lax.axis_index("dp")
    shard_count = lax.axis_size("shard")
    data_count = lax.axis_size("dp")
    device_total = shard_count * data_count
    home_count, row_count, width = params.shape
    half = home_count // 2
    piece = (row_count // shard_count, width)
    chips = data_count // 2
    my_core = data_here & core
    first_chip = jnp.where(my_core == 0, *first_link)
    second_chip = across - first_chip
    shard_half, shard_low = shard_here >> 1, shard_here & 1

    def set_of(values, index):
        split = values.reshape((home_count, 2, values.shape[1] // 2, width))
        return take(split, 1, index)

    grid = partials[0].reshape((home_count, chips, 2, row_count, width))
    away_rows = take(grid, 2, 1 - my_core)
    own_rows = take(grid, 2, my_core)
    away_rows, own_rows = lax.optimization_barrier((away_rows, own_rows))

    def rows_of(values, mask):
        return take(values, 1, (data_here ^ mask) // 2).astype(jnp.float32)

    near, far = {}, {}
    for name, mask, other_mask in (
        ("across", across, across),
        ("first", first_chip, second_chip),
        ("second", second_chip, first_chip),
        ("own", 0, 0),
    ):
        total = rows_of(own_rows, mask) + swap(
            rows_of(away_rows, other_mask), "dp", core, f"sum_core_{name}"
        )
        near[name], far[name] = lax.optimization_barrier(
            (set_of(total, shard_half), set_of(total, 1 - shard_half))
        )
        if name == "across":
            own_rows, near[name], far[name] = lax.optimization_barrier(
                (own_rows, near[name], far[name])
            )

    def sends(rows, what):
        relay = rows["second"] + swap(rows["across"], "dp", first_link, f"sum_across_{what}")
        direct = swap(rows["first"], "dp", first_link, f"sum_first_{what}")
        return direct, swap(relay, "dp", second_link, f"sum_relay_{what}")

    direct, relayed = sends(far, "far")
    far_sum = lax.optimization_barrier(far["own"] + direct) + relayed
    direct, relayed = sends(near, "near")
    near_sum = lax.optimization_barrier(near["own"] + relayed) + direct
    near_sum, owner_list = lax.optimization_barrier((near_sum, owner_list))

    mixed = shard_exchange(
        [
            set_of(near_sum, shard_low),
            set_of(near_sum, 1 - shard_low),
            set_of(far_sum, shard_low),
            set_of(far_sum, 1 - shard_low),
        ]
    )
    owners = unmix(owner_list.reshape(shard_count, home_count), shard_here)
    owners = jnp.concatenate([owners[k] for k in near_order])[None, :]
    device_ids = jnp.arange(device_total, dtype=jnp.int32)
    picker = (owners == device_ids[:, None]).astype(jnp.float32)
    pieces = jnp.concatenate([mixed[k] for k in near_order], axis=0).reshape(device_total, -1)
    leaving = jnp.einsum("eb,bn->en", picker, pieces, precision=high)
    whole = lax.all_to_all(
        leaving.reshape((device_total,) + piece),
        ("dp", "shard"),
        split_axis=0,
        concat_axis=0,
        tiled=True,
    ).reshape(width, width)

    first_new, second_new, change = adam(
        left_basis[0, 0, 0],
        right_basis[0, 0, 0],
        first_moment[0, 0, 0],
        second_moment[0, 0, 0],
        whole,
        high,
    )

    coming = lax.all_to_all(
        change.reshape((device_total,) + piece),
        ("dp", "shard"),
        split_axis=0,
        concat_axis=0,
        tiled=True,
    ).reshape(device_total, -1)
    coming, data_here, shard_here, params = lax.optimization_barrier(
        (coming, data_here, shard_here, params)
    )
    first_chip = jnp.where((data_here & core) == 0, *first_link)
    second_chip = across - first_chip
    back = jnp.einsum("eb,en->bn", picker, coming, precision=high)
    back = back.reshape((shard_count, home_count) + piece)
    returned = shard_exchange([back[near_order.index(k)] for k in range(shard_count)])

    new_home = params
    for k in (0, 3, 2, 1):
        start = (shard_here ^ k) * piece[0]
        home = lax.dynamic_slice_in_dim(params, start, piece[0], axis=1)
        home = home - learn_rate * (returned[k] + decay_rate * home)
        new_home = lax.dynamic_update_slice_in_dim(new_home, home, start, axis=1)

    low, top = new_home[:half], new_home[half:]
    first_top = swap(top, "dp", first_link, "rows_first_top")
    second_low = swap(low, "dp", second_link, "rows_second_low")
    other = swap(new_home, "dp", core, "rows_core_own")
    first_low = swap(low, "dp", first_link, "rows_first_low")
    second_top = swap(top, "dp", second_link, "rows_second_top")
    far_top = swap(first_top, "dp", second_link, "rows_relay_top")
    far_low = swap(second_low, "dp", first_link, "rows_relay_low")
    first_rows = jnp.concatenate([first_low, first_top], axis=0)
    second_rows = jnp.concatenate([second_top, second_low], axis=0)
    first_rows, second_rows, far_top, first_new, second_new = lax.optimization_barrier(
        (first_rows, second_rows, far_top, first_new, second_new)
    )
    far_rows = jnp.concatenate([far_low, far_top], axis=0)
    first_other, second_other = swap(
        jnp.stack([first_rows, second_rows]), "dp", core, "rows_core_direct"
    )
    updated = jnp.zeros((home_count, width, width), jnp.float32)
    for mask, block, values in (
        (0, 0, new_home),
        (core, 0, other),
        (first_chip, 0, first_rows),
        (second_chip, half, second_rows[:half]),
        (second_chip, 0, second_rows[half:]),
        (second_chip ^ core, 0, first_other),
        (first_chip ^ core, half, second_other[:half]),
        (first_chip ^ core, 0, second_other[half:]),
        (across, 0, far_rows),
        (across ^ core, 0, swap(far_rows, "dp", core, "rows_core_far")),
    ):
        start = (data_here ^ mask) * row_count
        updated = lax.dynamic_update_slice(updated, values, (block, start, 0))
    return updated, first_new[None, None, None], second_new[None, None, None]


def gathered(partials, params, left_basis, right_basis, first_moment, second_moment, owner_list):
    highest = lax.Precision.HIGHEST
    shard_here = lax.axis_index("shard")
    data_here = lax.axis_index("dp")
    shard_count = lax.axis_size("shard")
    data_count = lax.axis_size("dp")
    device_total = shard_count * data_count
    home_count, row_count, width = params.shape
    block_total = owner_list.shape[0]
    bit_count = data_count.bit_length() - 1
    high_low = list(range(bit_count))[::-1]
    middle = home_count // 2

    grid = partials[0].reshape((home_count,) + (2,) * bit_count + (row_count, width))
    low_first = halve(grid[:middle], high_low, list(range(bit_count)), data_here)
    high_first = halve(
        grid[middle:], high_low, [0] + list(range(1, bit_count))[::-1], data_here
    )
    summed = jnp.concatenate([low_first, high_first], axis=0)

    piece = row_count * width // shard_count
    cut = summed.reshape(home_count, shard_count, piece).swapaxes(0, 1)
    pieces = lax.all_to_all(cut, "shard", split_axis=0, concat_axis=0, tiled=True).reshape(
        block_total, piece
    )
    device_ids = jnp.arange(device_total, dtype=jnp.int32)
    picker = (owner_list[None, :] == device_ids[:, None]).astype(jnp.float32)
    leaving = jnp.einsum("eb,bn->en", picker, pieces, precision=highest)
    whole = lax.all_to_all(
        leaving, ("dp", "shard"), split_axis=0, concat_axis=0, tiled=True
    ).reshape(width, width)

    left_mat = left_basis[0, 0, 0]
    right_mat = right_basis[0, 0, 0]
    first_old = first_moment[0, 0, 0]
    second_old = second_moment[0, 0, 0]
    first_new, second_new, change = adam(
        left_mat, right_mat, first_old, second_old, whole, highest
    )

    coming = lax.all_to_all(
        change.reshape(device_total, piece), ("dp", "shard"), split_axis=0, concat_axis=0, tiled=True
    )
    back = jnp.einsum("eb,en->bn", picker, coming, precision=highest)
    returned = lax.all_to_all(
        back.reshape(shard_count, home_count, piece), "shard", split_axis=0, concat_axis=0, tiled=True
    )
    returned = returned.swapaxes(0, 1).reshape(home_count, row_count, width)
    new_home = params - learn_rate * (returned + decay_rate * params)
    updated = jnp.concatenate(
        [
            spread(new_home[:middle], high_low, data_here),
            spread(new_home[middle:], list(range(1, bit_count)) + [0], data_here),
        ],
        axis=0,
    ).reshape(home_count, width, width)

    my_id = data_here * shard_count + shard_here
    live = jnp.any(owner_list == my_id)
    first_keep = jnp.where(live, first_new, first_old)
    second_keep = jnp.where(live, second_new, second_old)
    return (updated, first_keep[None, None, None], second_keep[None, None, None])


def local(partials, params, left_basis, right_basis, first_moment, second_moment, owner_list):
    shard_count, data_count = lax.axis_size("shard"), lax.axis_size("dp")
    plain = (data_count, shard_count) != (8, 4) or params.shape[1] % (8 * shard_count) != 0
    plain = plain or owner_list.shape[0] != shard_count * data_count or params.shape[0] % 2 != 0
    form = gathered if plain else routed
    return form(
        partials, params, left_basis, right_basis, first_moment, second_moment, owner_list
    )


def solution(mesh):
    return jax.shard_map(
        local,
        mesh=mesh,
        in_specs=(
            P("dp", "shard", None, None),
            P("shard", "dp", None),
            P("dp", "shard", None, None, None),
            P("dp", "shard", None, None, None),
            P("dp", "shard", None, None, None),
            P("dp", "shard", None, None, None),
            P(),
        ),
        out_specs=(
            P("shard", None, None),
            P("dp", "shard", None, None, None),
            P("dp", "shard", None, None, None),
        ),
        check_vma=False,
    )
```

```python
import jax
import jax.numpy as jnp
from jax import lax
from jax.sharding import PartitionSpec as P

beta_one = 0.9
beta_two = 0.95
epsilon = 1e-08
learn_rate = 0.2
decay_rate = 0.1
step_count = 10


def swap(values, name, mask, what="swap"):
    masks = mask if isinstance(mask, tuple) else (mask, mask)
    pairs = [(i, i ^ masks[i & 1]) for i in range(lax.axis_size(name))]
    with jax.named_scope(what):
        return lax.ppermute(values, name, pairs)


def take(values, axis, index):
    return lax.dynamic_index_in_dim(values, index, axis, keepdims=False)


def halve(values, axes, bits, me):
    for bit in bits:
        axis = 1 + axes.index(bit)
        mine = (me >> bit) & 1
        away = take(values, axis, 1 - mine).astype(jnp.float32)
        here = take(values, axis, mine).astype(jnp.float32)
        values = here + swap(away, "dp", 1 << bit)
        axes = [a for a in axes if a != bit]
    return values


def spread(values, bits, me):
    axes = []
    for bit in bits:
        mine = (me >> bit) & 1
        other = swap(values, "dp", 1 << bit)
        low = jnp.where(mine == 0, values, other)
        high = jnp.where(mine == 0, other, values)
        place = sum(1 for a in axes if a > bit)
        values = jnp.stack([low, high], axis=1 + place)
        axes = sorted(axes + [bit], reverse=True)
    return values


def unmix(values, index, axis=0):
    count = values.shape[axis]
    lead, tail = values.shape[:axis], values.shape[axis + 1 :]
    bits = count.bit_length() - 1
    values = values.reshape(lead + (2,) * bits + tail)
    for place in range(bits):
        bit = bits - 1 - place
        flipped = jnp.flip(values, axis + place)
        values = jnp.where((index >> bit) & 1 == 1, flipped, values)
    return values.reshape(lead + (count,) + tail)


def adam(left_mat, right_mat, first_old, second_old, whole, precision):
    partway = jnp.einsum("ia,ij->aj", left_mat, whole, precision=precision)
    rotated = jnp.einsum("aj,jb->ab", partway, right_mat, precision=precision)
    first_new = beta_one * first_old + (1.0 - beta_one) * rotated
    second_new = beta_two * second_old + (1.0 - beta_two) * rotated * rotated
    correct_one = 1.0 - beta_one**step_count
    correct_two = 1.0 - beta_two**step_count
    scaled = first_new / correct_one / (jnp.sqrt(second_new / correct_two) + epsilon)
    back_rot = jnp.einsum("ab,jb->aj", scaled, right_mat, precision=precision)
    change = jnp.einsum("ia,aj->ij", left_mat, back_rot, precision=precision)
    return first_new, second_new, change


def shard_exchange(parts):
    arrived = {k: swap(parts[k], "shard", k, f"shard_{k}") for k in (2, 3, 1)}
    return [parts[0]] + [arrived[k] for k in (1, 2, 3)]


def routed(partials, params, left_basis, right_basis, first_moment, second_moment, owner_list):
    high = lax.Precision.HIGH
    core, across = 1, 6
    first_link, second_link = (2, 4), (4, 2)
    near_order = (0, 1, 3, 2)
    shard_here = lax.axis_index("shard")
    data_here = lax.axis_index("dp")
    shard_count = lax.axis_size("shard")
    data_count = lax.axis_size("dp")
    device_total = shard_count * data_count
    home_count, row_count, width = params.shape
    half = home_count // 2
    piece = (row_count // shard_count, width)
    chips = data_count // 2
    my_core = data_here & core
    first_chip = jnp.where(my_core == 0, *first_link)
    second_chip = across - first_chip
    shard_half, shard_low = shard_here >> 1, shard_here & 1

    def set_of(values, index):
        split = values.reshape((home_count, 2, values.shape[1] // 2, width))
        return take(split, 1, index)

    grid = partials[0].reshape((home_count, chips, 2, row_count, width))
    away_rows = take(grid, 2, 1 - my_core)
    own_rows = take(grid, 2, my_core)
    away_rows, own_rows = lax.optimization_barrier((away_rows, own_rows))

    def rows_of(values, mask):
        return take(values, 1, (data_here ^ mask) // 2).astype(jnp.float32)

    near, far = {}, {}
    for name, mask, other_mask in (
        ("across", across, across),
        ("first", first_chip, second_chip),
        ("second", second_chip, first_chip),
        ("own", 0, 0),
    ):
        total = rows_of(own_rows, mask) + swap(
            rows_of(away_rows, other_mask), "dp", core, f"sum_core_{name}"
        )
        near[name], far[name] = lax.optimization_barrier(
            (set_of(total, shard_half), set_of(total, 1 - shard_half))
        )
        if name == "across":
            own_rows, near[name], far[name] = lax.optimization_barrier(
                (own_rows, near[name], far[name])
            )

    def sends(rows, what):
        relay = rows["second"] + swap(rows["across"], "dp", first_link, f"sum_across_{what}")
        direct = swap(rows["first"], "dp", first_link, f"sum_first_{what}")
        return direct, swap(relay, "dp", second_link, f"sum_relay_{what}")

    direct, relayed = sends(far, "far")
    far_sum = lax.optimization_barrier(far["own"] + direct) + relayed
    direct, relayed = sends(near, "near")
    near_sum = lax.optimization_barrier(near["own"] + relayed) + direct
    near_sum, owner_list = lax.optimization_barrier((near_sum, owner_list))

    mixed = shard_exchange(
        [
            set_of(near_sum, shard_low),
            set_of(near_sum, 1 - shard_low),
            set_of(far_sum, shard_low),
            set_of(far_sum, 1 - shard_low),
        ]
    )
    owners = unmix(owner_list.reshape(shard_count, home_count), shard_here)
    owners = jnp.concatenate([owners[k] for k in near_order])[None, :]
    device_ids = jnp.arange(device_total, dtype=jnp.int32)
    picker = (owners == device_ids[:, None]).astype(jnp.float32)
    pieces = jnp.concatenate([mixed[k] for k in near_order], axis=0).reshape(device_total, -1)
    leaving = jnp.einsum("eb,bn->en", picker, pieces, precision=high)
    whole = lax.all_to_all(
        leaving.reshape((device_total,) + piece),
        ("dp", "shard"),
        split_axis=0,
        concat_axis=0,
        tiled=True,
    ).reshape(width, width)

    first_new, second_new, change = adam(
        left_basis[0, 0, 0],
        right_basis[0, 0, 0],
        first_moment[0, 0, 0],
        second_moment[0, 0, 0],
        whole,
        high,
    )

    coming = lax.all_to_all(
        change.reshape((device_total,) + piece),
        ("dp", "shard"),
        split_axis=0,
        concat_axis=0,
        tiled=True,
    ).reshape(device_total, -1)
    coming, data_here, shard_here, params = lax.optimization_barrier(
        (coming, data_here, shard_here, params)
    )
    first_chip = jnp.where((data_here & core) == 0, *first_link)
    second_chip = across - first_chip
    cut = 2 * home_count
    far_back = jnp.einsum("eb,en->bn", picker[:, cut:], coming, precision=high)
    coming, far_back = lax.optimization_barrier((coming, far_back))
    near_back = jnp.einsum("eb,en->bn", picker[:, :cut], coming, precision=high)
    near_back = near_back.reshape((2, home_count) + piece)
    far_back = far_back.reshape((2, home_count) + piece)
    back = [near_back[0], near_back[1], far_back[0], far_back[1]]
    returned = shard_exchange([back[near_order.index(k)] for k in range(shard_count)])

    new_home = params
    for k in (0, 3, 2, 1):
        start = (shard_here ^ k) * piece[0]
        home = lax.dynamic_slice_in_dim(params, start, piece[0], axis=1)
        home = home - learn_rate * (returned[k] + decay_rate * home)
        new_home = lax.dynamic_update_slice_in_dim(new_home, home, start, axis=1)

    low, top = new_home[:half], new_home[half:]
    first_top = swap(top, "dp", first_link, "rows_first_top")
    second_low = swap(low, "dp", second_link, "rows_second_low")
    other = swap(new_home, "dp", core, "rows_core_own")
    first_low = swap(low, "dp", first_link, "rows_first_low")
    second_top = swap(top, "dp", second_link, "rows_second_top")
    far_top = swap(first_top, "dp", second_link, "rows_relay_top")
    far_low = swap(second_low, "dp", first_link, "rows_relay_low")
    first_rows = jnp.concatenate([first_low, first_top], axis=0)
    second_rows = jnp.concatenate([second_top, second_low], axis=0)
    first_rows, second_rows, far_top, first_new, second_new = lax.optimization_barrier(
        (first_rows, second_rows, far_top, first_new, second_new)
    )
    far_rows = jnp.concatenate([far_low, far_top], axis=0)
    second_other = swap(second_rows, "dp", core, "rows_core_second")
    updated = jnp.zeros((home_count, width, width), jnp.float32)
    for mask, block, values in (
        (0, 0, new_home),
        (core, 0, other),
        (first_chip, 0, first_rows),
        (second_chip, half, second_rows[:half]),
        (second_chip, 0, second_rows[half:]),
        (second_chip ^ core, 0, swap(first_rows, "dp", core, "rows_core_first")),
        (first_chip ^ core, half, second_other[:half]),
        (first_chip ^ core, 0, second_other[half:]),
        (across, 0, far_rows),
        (across ^ core, 0, swap(far_rows, "dp", core, "rows_core_far")),
    ):
        start = (data_here ^ mask) * row_count
        updated = lax.dynamic_update_slice(updated, values, (block, start, 0))
    return updated, first_new[None, None, None], second_new[None, None, None]


def gathered(partials, params, left_basis, right_basis, first_moment, second_moment, owner_list):
    highest = lax.Precision.HIGHEST
    shard_here = lax.axis_index("shard")
    data_here = lax.axis_index("dp")
    shard_count = lax.axis_size("shard")
    data_count = lax.axis_size("dp")
    device_total = shard_count * data_count
    home_count, row_count, width = params.shape
    block_total = owner_list.shape[0]
    bit_count = data_count.bit_length() - 1
    high_low = list(range(bit_count))[::-1]
    middle = home_count // 2

    grid = partials[0].reshape((home_count,) + (2,) * bit_count + (row_count, width))
    low_first = halve(grid[:middle], high_low, list(range(bit_count)), data_here)
    high_first = halve(
        grid[middle:], high_low, [0] + list(range(1, bit_count))[::-1], data_here
    )
    summed = jnp.concatenate([low_first, high_first], axis=0)

    piece = row_count * width // shard_count
    cut = summed.reshape(home_count, shard_count, piece).swapaxes(0, 1)
    pieces = lax.all_to_all(cut, "shard", split_axis=0, concat_axis=0, tiled=True).reshape(
        block_total, piece
    )
    device_ids = jnp.arange(device_total, dtype=jnp.int32)
    picker = (owner_list[None, :] == device_ids[:, None]).astype(jnp.float32)
    leaving = jnp.einsum("eb,bn->en", picker, pieces, precision=highest)
    whole = lax.all_to_all(
        leaving, ("dp", "shard"), split_axis=0, concat_axis=0, tiled=True
    ).reshape(width, width)

    left_mat = left_basis[0, 0, 0]
    right_mat = right_basis[0, 0, 0]
    first_old = first_moment[0, 0, 0]
    second_old = second_moment[0, 0, 0]
    first_new, second_new, change = adam(
        left_mat, right_mat, first_old, second_old, whole, highest
    )

    coming = lax.all_to_all(
        change.reshape(device_total, piece), ("dp", "shard"), split_axis=0, concat_axis=0, tiled=True
    )
    back = jnp.einsum("eb,en->bn", picker, coming, precision=highest)
    returned = lax.all_to_all(
        back.reshape(shard_count, home_count, piece), "shard", split_axis=0, concat_axis=0, tiled=True
    )
    returned = returned.swapaxes(0, 1).reshape(home_count, row_count, width)
    new_home = params - learn_rate * (returned + decay_rate * params)
    updated = jnp.concatenate(
        [
            spread(new_home[:middle], high_low, data_here),
            spread(new_home[middle:], list(range(1, bit_count)) + [0], data_here),
        ],
        axis=0,
    ).reshape(home_count, width, width)

    my_id = data_here * shard_count + shard_here
    live = jnp.any(owner_list == my_id)
    first_keep = jnp.where(live, first_new, first_old)
    second_keep = jnp.where(live, second_new, second_old)
    return (updated, first_keep[None, None, None], second_keep[None, None, None])


def local(partials, params, left_basis, right_basis, first_moment, second_moment, owner_list):
    shard_count, data_count = lax.axis_size("shard"), lax.axis_size("dp")
    plain = (data_count, shard_count) != (8, 4) or params.shape[1] % (8 * shard_count) != 0
    plain = plain or owner_list.shape[0] != shard_count * data_count or params.shape[0] % 2 != 0
    form = gathered if plain else routed
    return form(
        partials, params, left_basis, right_basis, first_moment, second_moment, owner_list
    )


def solution(mesh):
    return jax.shard_map(
        local,
        mesh=mesh,
        in_specs=(
            P("dp", "shard", None, None),
            P("shard", "dp", None),
            P("dp", "shard", None, None, None),
            P("dp", "shard", None, None, None),
            P("dp", "shard", None, None, None),
            P("dp", "shard", None, None, None),
            P(),
        ),
        out_specs=(
            P("shard", None, None),
            P("dp", "shard", None, None, None),
            P("dp", "shard", None, None, None),
        ),
        check_vma=False,
    )
```

```python
import jax
import jax.numpy as jnp
from jax import lax
from jax.sharding import PartitionSpec as P

beta_one = 0.9
beta_two = 0.95
epsilon = 1e-08
learn_rate = 0.2
decay_rate = 0.1
step_count = 10


def swap(values, name, mask, what="swap"):
    masks = mask if isinstance(mask, tuple) else (mask, mask)
    pairs = [(i, i ^ masks[i & 1]) for i in range(lax.axis_size(name))]
    with jax.named_scope(what):
        return lax.ppermute(values, name, pairs)


def take(values, axis, index):
    return lax.dynamic_index_in_dim(values, index, axis, keepdims=False)


def halve(values, axes, bits, me):
    for bit in bits:
        axis = 1 + axes.index(bit)
        mine = (me >> bit) & 1
        away = take(values, axis, 1 - mine).astype(jnp.float32)
        here = take(values, axis, mine).astype(jnp.float32)
        values = here + swap(away, "dp", 1 << bit)
        axes = [a for a in axes if a != bit]
    return values


def spread(values, bits, me):
    axes = []
    for bit in bits:
        mine = (me >> bit) & 1
        other = swap(values, "dp", 1 << bit)
        low = jnp.where(mine == 0, values, other)
        high = jnp.where(mine == 0, other, values)
        place = sum(1 for a in axes if a > bit)
        values = jnp.stack([low, high], axis=1 + place)
        axes = sorted(axes + [bit], reverse=True)
    return values


def unmix(values, index, axis=0):
    count = values.shape[axis]
    lead, tail = values.shape[:axis], values.shape[axis + 1 :]
    bits = count.bit_length() - 1
    values = values.reshape(lead + (2,) * bits + tail)
    for place in range(bits):
        bit = bits - 1 - place
        flipped = jnp.flip(values, axis + place)
        values = jnp.where((index >> bit) & 1 == 1, flipped, values)
    return values.reshape(lead + (count,) + tail)


def adam(left_mat, right_mat, first_old, second_old, whole, precision):
    partway = jnp.einsum("ia,ij->aj", left_mat, whole, precision=precision)
    rotated = jnp.einsum("aj,jb->ab", partway, right_mat, precision=precision)
    first_new = beta_one * first_old + (1.0 - beta_one) * rotated
    second_new = beta_two * second_old + (1.0 - beta_two) * rotated * rotated
    correct_one = 1.0 - beta_one**step_count
    correct_two = 1.0 - beta_two**step_count
    scaled = first_new / correct_one / (jnp.sqrt(second_new / correct_two) + epsilon)
    back_rot = jnp.einsum("ab,jb->aj", scaled, right_mat, precision=precision)
    change = jnp.einsum("ia,aj->ij", left_mat, back_rot, precision=precision)
    return first_new, second_new, change


def shard_exchange(parts):
    arrived = {k: swap(parts[k], "shard", k, f"shard_{k}") for k in (2, 3, 1)}
    return [parts[0]] + [arrived[k] for k in (1, 2, 3)]


def routed(partials, params, left_basis, right_basis, first_moment, second_moment, owner_list):
    high = lax.Precision.HIGH
    core, across = 1, 6
    first_link, second_link = (2, 4), (4, 2)
    near_order = (0, 1, 3, 2)
    shard_here = lax.axis_index("shard")
    data_here = lax.axis_index("dp")
    shard_count = lax.axis_size("shard")
    data_count = lax.axis_size("dp")
    device_total = shard_count * data_count
    home_count, row_count, width = params.shape
    half = home_count // 2
    piece = (row_count // shard_count, width)
    chips = data_count // 2
    my_core = data_here & core
    first_chip = jnp.where(my_core == 0, *first_link)
    second_chip = across - first_chip
    shard_half, shard_low = shard_here >> 1, shard_here & 1

    def set_of(values, index):
        split = values.reshape((home_count, 2, values.shape[1] // 2, width))
        return take(split, 1, index)

    grid = partials[0].reshape((home_count, chips, 2, row_count, width))
    away_rows = take(grid, 2, 1 - my_core)
    own_rows = take(grid, 2, my_core)
    away_rows, own_rows = lax.optimization_barrier((away_rows, own_rows))

    def rows_of(values, mask):
        return take(values, 1, (data_here ^ mask) // 2).astype(jnp.float32)

    near, far = {}, {}
    for name, mask, other_mask in (
        ("across", across, across),
        ("first", first_chip, second_chip),
        ("second", second_chip, first_chip),
        ("own", 0, 0),
    ):
        total = rows_of(own_rows, mask) + swap(
            rows_of(away_rows, other_mask), "dp", core, f"sum_core_{name}"
        )
        near[name], far[name] = lax.optimization_barrier(
            (set_of(total, shard_half), set_of(total, 1 - shard_half))
        )
        if name == "across":
            own_rows, near[name], far[name] = lax.optimization_barrier(
                (own_rows, near[name], far[name])
            )

    def sends(rows, what):
        relay = rows["second"] + swap(rows["across"], "dp", first_link, f"sum_across_{what}")
        direct = swap(rows["first"], "dp", first_link, f"sum_first_{what}")
        return direct, swap(relay, "dp", second_link, f"sum_relay_{what}")

    direct, relayed = sends(far, "far")
    far_sum = lax.optimization_barrier(far["own"] + direct) + relayed
    direct, relayed = sends(near, "near")
    near_sum = lax.optimization_barrier(near["own"] + relayed) + direct
    near_sum, owner_list = lax.optimization_barrier((near_sum, owner_list))

    mixed = shard_exchange(
        [
            set_of(near_sum, shard_low),
            set_of(near_sum, 1 - shard_low),
            set_of(far_sum, shard_low),
            set_of(far_sum, 1 - shard_low),
        ]
    )
    owners = unmix(owner_list.reshape(shard_count, home_count), shard_here)
    owners = jnp.concatenate([owners[k] for k in near_order])[None, :]
    device_ids = jnp.arange(device_total, dtype=jnp.int32)
    picker = (owners == device_ids[:, None]).astype(jnp.float32)
    pieces = jnp.concatenate([mixed[k] for k in near_order], axis=0).reshape(device_total, -1)
    leaving = jnp.einsum("eb,bn->en", picker, pieces, precision=high)
    whole = lax.all_to_all(
        leaving.reshape((device_total,) + piece),
        ("dp", "shard"),
        split_axis=0,
        concat_axis=0,
        tiled=True,
    ).reshape(width, width)

    first_new, second_new, change = adam(
        left_basis[0, 0, 0],
        right_basis[0, 0, 0],
        first_moment[0, 0, 0],
        second_moment[0, 0, 0],
        whole,
        high,
    )

    coming = lax.all_to_all(
        change.reshape((device_total,) + piece),
        ("dp", "shard"),
        split_axis=0,
        concat_axis=0,
        tiled=True,
    ).reshape(device_total, -1)
    coming, data_here, shard_here, params = lax.optimization_barrier(
        (coming, data_here, shard_here, params)
    )
    first_chip = jnp.where((data_here & core) == 0, *first_link)
    second_chip = across - first_chip
    back = jnp.einsum("eb,en->bn", picker, coming, precision=high)
    back = back.reshape((shard_count, home_count) + piece)
    returned = shard_exchange([back[near_order.index(k)] for k in range(shard_count)])

    new_home = params
    for k in (0, 2, 3, 1):
        start = (shard_here ^ k) * piece[0]
        home = lax.dynamic_slice_in_dim(params, start, piece[0], axis=1)
        home = home - learn_rate * (returned[k] + decay_rate * home)
        new_home = lax.dynamic_update_slice_in_dim(new_home, home, start, axis=1)

    low, top = new_home[:half], new_home[half:]
    first_top = swap(top, "dp", first_link, "rows_first_top")
    second_low = swap(low, "dp", second_link, "rows_second_low")
    other = swap(new_home, "dp", core, "rows_core_own")
    first_low = swap(low, "dp", first_link, "rows_first_low")
    second_top = swap(top, "dp", second_link, "rows_second_top")
    far_top = swap(first_top, "dp", second_link, "rows_relay_top")
    far_low = swap(second_low, "dp", first_link, "rows_relay_low")
    first_rows = jnp.concatenate([first_low, first_top], axis=0)
    second_rows = jnp.concatenate([second_top, second_low], axis=0)
    first_rows, second_rows, far_top, first_new, second_new = lax.optimization_barrier(
        (first_rows, second_rows, far_top, first_new, second_new)
    )
    far_rows = jnp.concatenate([far_low, far_top], axis=0)
    second_other = swap(second_rows, "dp", core, "rows_core_second")
    updated = jnp.zeros((home_count, width, width), jnp.float32)
    for mask, block, values in (
        (0, 0, new_home),
        (core, 0, other),
        (first_chip, 0, first_rows),
        (second_chip, half, second_rows[:half]),
        (second_chip, 0, second_rows[half:]),
        (second_chip ^ core, 0, swap(first_rows, "dp", core, "rows_core_first")),
        (first_chip ^ core, half, second_other[:half]),
        (first_chip ^ core, 0, second_other[half:]),
        (across, 0, far_rows),
        (across ^ core, 0, swap(far_rows, "dp", core, "rows_core_far")),
    ):
        start = (data_here ^ mask) * row_count
        updated = lax.dynamic_update_slice(updated, values, (block, start, 0))
    return updated, first_new[None, None, None], second_new[None, None, None]


def gathered(partials, params, left_basis, right_basis, first_moment, second_moment, owner_list):
    highest = lax.Precision.HIGHEST
    shard_here = lax.axis_index("shard")
    data_here = lax.axis_index("dp")
    shard_count = lax.axis_size("shard")
    data_count = lax.axis_size("dp")
    device_total = shard_count * data_count
    home_count, row_count, width = params.shape
    block_total = owner_list.shape[0]
    bit_count = data_count.bit_length() - 1
    high_low = list(range(bit_count))[::-1]
    middle = home_count // 2

    grid = partials[0].reshape((home_count,) + (2,) * bit_count + (row_count, width))
    low_first = halve(grid[:middle], high_low, list(range(bit_count)), data_here)
    high_first = halve(
        grid[middle:], high_low, [0] + list(range(1, bit_count))[::-1], data_here
    )
    summed = jnp.concatenate([low_first, high_first], axis=0)

    piece = row_count * width // shard_count
    cut = summed.reshape(home_count, shard_count, piece).swapaxes(0, 1)
    pieces = lax.all_to_all(cut, "shard", split_axis=0, concat_axis=0, tiled=True).reshape(
        block_total, piece
    )
    device_ids = jnp.arange(device_total, dtype=jnp.int32)
    picker = (owner_list[None, :] == device_ids[:, None]).astype(jnp.float32)
    leaving = jnp.einsum("eb,bn->en", picker, pieces, precision=highest)
    whole = lax.all_to_all(
        leaving, ("dp", "shard"), split_axis=0, concat_axis=0, tiled=True
    ).reshape(width, width)

    left_mat = left_basis[0, 0, 0]
    right_mat = right_basis[0, 0, 0]
    first_old = first_moment[0, 0, 0]
    second_old = second_moment[0, 0, 0]
    first_new, second_new, change = adam(
        left_mat, right_mat, first_old, second_old, whole, highest
    )

    coming = lax.all_to_all(
        change.reshape(device_total, piece), ("dp", "shard"), split_axis=0, concat_axis=0, tiled=True
    )
    back = jnp.einsum("eb,en->bn", picker, coming, precision=highest)
    returned = lax.all_to_all(
        back.reshape(shard_count, home_count, piece), "shard", split_axis=0, concat_axis=0, tiled=True
    )
    returned = returned.swapaxes(0, 1).reshape(home_count, row_count, width)
    new_home = params - learn_rate * (returned + decay_rate * params)
    updated = jnp.concatenate(
        [
            spread(new_home[:middle], high_low, data_here),
            spread(new_home[middle:], list(range(1, bit_count)) + [0], data_here),
        ],
        axis=0,
    ).reshape(home_count, width, width)

    my_id = data_here * shard_count + shard_here
    live = jnp.any(owner_list == my_id)
    first_keep = jnp.where(live, first_new, first_old)
    second_keep = jnp.where(live, second_new, second_old)
    return (updated, first_keep[None, None, None], second_keep[None, None, None])


def local(partials, params, left_basis, right_basis, first_moment, second_moment, owner_list):
    shard_count, data_count = lax.axis_size("shard"), lax.axis_size("dp")
    plain = (data_count, shard_count) != (8, 4) or params.shape[1] % (8 * shard_count) != 0
    plain = plain or owner_list.shape[0] != shard_count * data_count or params.shape[0] % 2 != 0
    form = gathered if plain else routed
    return form(
        partials, params, left_basis, right_basis, first_moment, second_moment, owner_list
    )


def solution(mesh):
    return jax.shard_map(
        local,
        mesh=mesh,
        in_specs=(
            P("dp", "shard", None, None),
            P("shard", "dp", None),
            P("dp", "shard", None, None, None),
            P("dp", "shard", None, None, None),
            P("dp", "shard", None, None, None),
            P("dp", "shard", None, None, None),
            P(),
        ),
        out_specs=(
            P("shard", None, None),
            P("dp", "shard", None, None, None),
            P("dp", "shard", None, None, None),
        ),
        check_vma=False,
    )
```

```python
import jax
import jax.numpy as jnp
from jax import lax
from jax.sharding import PartitionSpec as P

beta_one = 0.9
beta_two = 0.95
epsilon = 1e-08
learn_rate = 0.2
decay_rate = 0.1
step_count = 10


def swap(values, name, mask, what="swap"):
    masks = mask if isinstance(mask, tuple) else (mask, mask)
    pairs = [(i, i ^ masks[i & 1]) for i in range(lax.axis_size(name))]
    with jax.named_scope(what):
        return lax.ppermute(values, name, pairs)


def take(values, axis, index):
    return lax.dynamic_index_in_dim(values, index, axis, keepdims=False)


def halve(values, axes, bits, me):
    for bit in bits:
        axis = 1 + axes.index(bit)
        mine = (me >> bit) & 1
        away = take(values, axis, 1 - mine).astype(jnp.float32)
        here = take(values, axis, mine).astype(jnp.float32)
        values = here + swap(away, "dp", 1 << bit)
        axes = [a for a in axes if a != bit]
    return values


def spread(values, bits, me):
    axes = []
    for bit in bits:
        mine = (me >> bit) & 1
        other = swap(values, "dp", 1 << bit)
        low = jnp.where(mine == 0, values, other)
        high = jnp.where(mine == 0, other, values)
        place = sum(1 for a in axes if a > bit)
        values = jnp.stack([low, high], axis=1 + place)
        axes = sorted(axes + [bit], reverse=True)
    return values


def unmix(values, index, axis=0):
    count = values.shape[axis]
    lead, tail = values.shape[:axis], values.shape[axis + 1 :]
    bits = count.bit_length() - 1
    values = values.reshape(lead + (2,) * bits + tail)
    for place in range(bits):
        bit = bits - 1 - place
        flipped = jnp.flip(values, axis + place)
        values = jnp.where((index >> bit) & 1 == 1, flipped, values)
    return values.reshape(lead + (count,) + tail)


def adam(left_mat, right_mat, first_old, second_old, whole, precision):
    partway = jnp.einsum("ia,ij->aj", left_mat, whole, precision=precision)
    rotated = jnp.einsum("aj,jb->ab", partway, right_mat, precision=precision)
    first_new = beta_one * first_old + (1.0 - beta_one) * rotated
    second_new = beta_two * second_old + (1.0 - beta_two) * rotated * rotated
    correct_one = 1.0 - beta_one**step_count
    correct_two = 1.0 - beta_two**step_count
    scaled = first_new / correct_one / (jnp.sqrt(second_new / correct_two) + epsilon)
    back_rot = jnp.einsum("ab,jb->aj", scaled, right_mat, precision=precision)
    change = jnp.einsum("ia,aj->ij", left_mat, back_rot, precision=precision)
    return first_new, second_new, change


def shard_exchange(parts):
    arrived = {k: swap(parts[k], "shard", k, f"shard_{k}") for k in (2, 3, 1)}
    return [parts[0]] + [arrived[k] for k in (1, 2, 3)]


def routed(partials, params, left_basis, right_basis, first_moment, second_moment, owner_list):
    high = lax.Precision.HIGH
    core, across = 1, 6
    first_link, second_link = (2, 4), (4, 2)
    near_order = (0, 1, 3, 2)
    shard_here = lax.axis_index("shard")
    data_here = lax.axis_index("dp")
    shard_count = lax.axis_size("shard")
    data_count = lax.axis_size("dp")
    device_total = shard_count * data_count
    home_count, row_count, width = params.shape
    half = home_count // 2
    piece = (row_count // shard_count, width)
    chips = data_count // 2
    my_core = data_here & core
    first_chip = jnp.where(my_core == 0, *first_link)
    second_chip = across - first_chip
    shard_half, shard_low = shard_here >> 1, shard_here & 1

    def set_of(values, index):
        split = values.reshape((home_count, 2, values.shape[1] // 2, width))
        return take(split, 1, index)

    grid = partials[0].reshape((home_count, chips, 2, row_count, width))
    away_rows = take(grid, 2, 1 - my_core)
    own_rows = take(grid, 2, my_core)
    away_rows, own_rows = lax.optimization_barrier((away_rows, own_rows))

    def rows_of(values, mask):
        return take(values, 1, (data_here ^ mask) // 2).astype(jnp.float32)

    near, far = {}, {}
    for name, mask, other_mask in (
        ("across", across, across),
        ("first", first_chip, second_chip),
        ("second", second_chip, first_chip),
        ("own", 0, 0),
    ):
        total = rows_of(own_rows, mask) + swap(
            rows_of(away_rows, other_mask), "dp", core, f"sum_core_{name}"
        )
        near[name], far[name] = lax.optimization_barrier(
            (set_of(total, shard_half), set_of(total, 1 - shard_half))
        )
        if name == "across":
            own_rows, near[name], far[name] = lax.optimization_barrier(
                (own_rows, near[name], far[name])
            )

    def sends(rows, what):
        relay = rows["second"] + swap(rows["across"], "dp", first_link, f"sum_across_{what}")
        direct = swap(rows["first"], "dp", first_link, f"sum_first_{what}")
        return direct, swap(relay, "dp", second_link, f"sum_relay_{what}")

    direct, relayed = sends(far, "far")
    far_sum = lax.optimization_barrier(far["own"] + direct) + relayed
    direct, relayed = sends(near, "near")
    near_sum = lax.optimization_barrier(near["own"] + relayed) + direct
    near_sum, owner_list = lax.optimization_barrier((near_sum, owner_list))

    mixed = shard_exchange(
        [
            set_of(near_sum, shard_low),
            set_of(near_sum, 1 - shard_low),
            set_of(far_sum, shard_low),
            set_of(far_sum, 1 - shard_low),
        ]
    )
    owners = unmix(owner_list.reshape(shard_count, home_count), shard_here)
    owners = jnp.concatenate([owners[k] for k in near_order])[None, :]
    device_ids = jnp.arange(device_total, dtype=jnp.int32)
    picker = (owners == device_ids[:, None]).astype(jnp.float32)
    pieces = jnp.concatenate([mixed[k] for k in near_order], axis=0).reshape(device_total, -1)
    leaving = jnp.einsum("eb,bn->en", picker, pieces, precision=high)
    whole = lax.all_to_all(
        leaving.reshape((device_total,) + piece),
        ("dp", "shard"),
        split_axis=0,
        concat_axis=0,
        tiled=True,
    ).reshape(width, width)

    first_new, second_new, change = adam(
        left_basis[0, 0, 0],
        right_basis[0, 0, 0],
        first_moment[0, 0, 0],
        second_moment[0, 0, 0],
        whole,
        high,
    )

    coming = lax.all_to_all(
        change.reshape((device_total,) + piece),
        ("dp", "shard"),
        split_axis=0,
        concat_axis=0,
        tiled=True,
    ).reshape(device_total, -1)
    coming, data_here, shard_here, params = lax.optimization_barrier(
        (coming, data_here, shard_here, params)
    )
    first_chip = jnp.where((data_here & core) == 0, *first_link)
    second_chip = across - first_chip
    back = jnp.einsum("eb,en->bn", picker, coming, precision=high)
    back = back.reshape((shard_count, home_count) + piece)
    returned = shard_exchange([back[near_order.index(k)] for k in range(shard_count)])

    new_home = params
    for k in (0, 2, 3, 1):
        start = (shard_here ^ k) * piece[0]
        home = lax.dynamic_slice_in_dim(params, start, piece[0], axis=1)
        home = home - learn_rate * (returned[k] + decay_rate * home)
        new_home = lax.dynamic_update_slice_in_dim(new_home, home, start, axis=1)

    low, top = new_home[:half], new_home[half:]
    first_top = swap(top, "dp", first_link, "rows_first_top")
    second_low = swap(low, "dp", second_link, "rows_second_low")
    other = swap(new_home, "dp", core, "rows_core_own")
    first_low = swap(low, "dp", first_link, "rows_first_low")
    second_top = swap(top, "dp", second_link, "rows_second_top")
    far_top = swap(first_top, "dp", second_link, "rows_relay_top")
    far_low = swap(second_low, "dp", first_link, "rows_relay_low")
    first_rows = jnp.concatenate([first_low, first_top], axis=0)
    second_rows = jnp.concatenate([second_top, second_low], axis=0)
    first_rows, second_rows, far_top, first_new, second_new = lax.optimization_barrier(
        (first_rows, second_rows, far_top, first_new, second_new)
    )
    far_rows = jnp.concatenate([far_low, far_top], axis=0)
    first_other, second_other = swap(
        jnp.stack([first_rows, second_rows]), "dp", core, "rows_core_direct"
    )
    updated = jnp.zeros((home_count, width, width), jnp.float32)
    for mask, block, values in (
        (0, 0, new_home),
        (core, 0, other),
        (first_chip, 0, first_rows),
        (second_chip, half, second_rows[:half]),
        (second_chip, 0, second_rows[half:]),
        (second_chip ^ core, 0, first_other),
        (first_chip ^ core, half, second_other[:half]),
        (first_chip ^ core, 0, second_other[half:]),
        (across, 0, far_rows),
        (across ^ core, 0, swap(far_rows, "dp", core, "rows_core_far")),
    ):
        start = (data_here ^ mask) * row_count
        updated = lax.dynamic_update_slice(updated, values, (block, start, 0))
    return updated, first_new[None, None, None], second_new[None, None, None]


def gathered(partials, params, left_basis, right_basis, first_moment, second_moment, owner_list):
    highest = lax.Precision.HIGHEST
    shard_here = lax.axis_index("shard")
    data_here = lax.axis_index("dp")
    shard_count = lax.axis_size("shard")
    data_count = lax.axis_size("dp")
    device_total = shard_count * data_count
    home_count, row_count, width = params.shape
    block_total = owner_list.shape[0]
    bit_count = data_count.bit_length() - 1
    high_low = list(range(bit_count))[::-1]
    middle = home_count // 2

    grid = partials[0].reshape((home_count,) + (2,) * bit_count + (row_count, width))
    low_first = halve(grid[:middle], high_low, list(range(bit_count)), data_here)
    high_first = halve(
        grid[middle:], high_low, [0] + list(range(1, bit_count))[::-1], data_here
    )
    summed = jnp.concatenate([low_first, high_first], axis=0)

    piece = row_count * width // shard_count
    cut = summed.reshape(home_count, shard_count, piece).swapaxes(0, 1)
    pieces = lax.all_to_all(cut, "shard", split_axis=0, concat_axis=0, tiled=True).reshape(
        block_total, piece
    )
    device_ids = jnp.arange(device_total, dtype=jnp.int32)
    picker = (owner_list[None, :] == device_ids[:, None]).astype(jnp.float32)
    leaving = jnp.einsum("eb,bn->en", picker, pieces, precision=highest)
    whole = lax.all_to_all(
        leaving, ("dp", "shard"), split_axis=0, concat_axis=0, tiled=True
    ).reshape(width, width)

    left_mat = left_basis[0, 0, 0]
    right_mat = right_basis[0, 0, 0]
    first_old = first_moment[0, 0, 0]
    second_old = second_moment[0, 0, 0]
    first_new, second_new, change = adam(
        left_mat, right_mat, first_old, second_old, whole, highest
    )

    coming = lax.all_to_all(
        change.reshape(device_total, piece), ("dp", "shard"), split_axis=0, concat_axis=0, tiled=True
    )
    back = jnp.einsum("eb,en->bn", picker, coming, precision=highest)
    returned = lax.all_to_all(
        back.reshape(shard_count, home_count, piece), "shard", split_axis=0, concat_axis=0, tiled=True
    )
    returned = returned.swapaxes(0, 1).reshape(home_count, row_count, width)
    new_home = params - learn_rate * (returned + decay_rate * params)
    updated = jnp.concatenate(
        [
            spread(new_home[:middle], high_low, data_here),
            spread(new_home[middle:], list(range(1, bit_count)) + [0], data_here),
        ],
        axis=0,
    ).reshape(home_count, width, width)

    my_id = data_here * shard_count + shard_here
    live = jnp.any(owner_list == my_id)
    first_keep = jnp.where(live, first_new, first_old)
    second_keep = jnp.where(live, second_new, second_old)
    return (updated, first_keep[None, None, None], second_keep[None, None, None])


def local(partials, params, left_basis, right_basis, first_moment, second_moment, owner_list):
    shard_count, data_count = lax.axis_size("shard"), lax.axis_size("dp")
    plain = (data_count, shard_count) != (8, 4) or params.shape[1] % (8 * shard_count) != 0
    plain = plain or owner_list.shape[0] != shard_count * data_count or params.shape[0] % 2 != 0
    form = gathered if plain else routed
    return form(
        partials, params, left_basis, right_basis, first_moment, second_moment, owner_list
    )


def solution(mesh):
    return jax.shard_map(
        local,
        mesh=mesh,
        in_specs=(
            P("dp", "shard", None, None),
            P("shard", "dp", None),
            P("dp", "shard", None, None, None),
            P("dp", "shard", None, None, None),
            P("dp", "shard", None, None, None),
            P("dp", "shard", None, None, None),
            P(),
        ),
        out_specs=(
            P("shard", None, None),
            P("dp", "shard", None, None, None),
            P("dp", "shard", None, None, None),
        ),
        check_vma=False,
    )
```
